128 devices in a mesh: dp: 16 (over y, x_hi, core), row: 4 (over z), col: 2 (over x_lo).
Axes of the slice: x: 4 (x_hi: 2, x_lo: 2; x = x_hi * 2 + x_lo), y: 4, z: 4, core: 2. Of those that a mesh axis runs over, the one named last changes fastest.
Arguments:
- inputs: bfloat16 [12288, 2048], P('dp', 'col')
- segments: int32 [12288], P('dp'), may hold values from 0 to 2, as said below
- w_query: bfloat16 [2048, 2048], P('col', 'row')
- w_key: bfloat16 [2048, 2048], P('col', 'row')
- w_value: bfloat16 [2048, 2048], P('col', 'row'), may hold values from -0.125 to 0.125
- w_mix: bfloat16 [2048, 2048], P('row', 'col')
- w_gate: bfloat16 [2048, 8192], P('col', 'row'), may hold values from -0.125 to 0.125
- w_up: bfloat16 [2048, 8192], P('col', 'row'), may hold values from -0.125 to 0.125
- w_down: bfloat16 [8192, 2048], P('row', 'col')
- attn_gain: float32 [2048], P('col'), may hold values from 0.25 to 1.75
- ffn_gain: float32 [2048], P('col'), may hold values from 0.25 to 1.75
- query_gain: float32 [2048], P(('row', 'col')), may hold values from 0.25 to 1.75
- key_gain: float32 [2048], P(('row', 'col')), may hold values from 0.25 to 1.75
- out_grad: bfloat16 [12288, 2048], P('dp', 'col'), may hold values from -6 to 6
Outputs:
- block_out: bfloat16 [12288, 2048], P('dp', 'col')
- input_grad: float32 [12288, 2048], P('dp', 'col')
- query_grad: float32 [2048, 2048], P(('col', 'dp'), 'row')
- key_grad: float32 [2048, 2048], P(('col', 'dp'), 'row')
- value_grad: float32 [2048, 2048], P(('col', 'dp'), 'row')
- mix_grad: float32 [2048, 2048], P('row', ('col', 'dp'))
- gate_grad: float32 [2048, 8192], P(('col', 'dp'), 'row')
- up_grad: float32 [2048, 8192], P(('col', 'dp'), 'row')
- down_grad: float32 [8192, 2048], P('row', ('col', 'dp'))
- attn_gain_grad: float32 [2048], P(('col', 'dp'))
- ffn_gain_grad: float32 [2048], P(('col', 'dp'))
- query_gain_grad: float32 [2048], P(('row', 'col', 'dp'))
- key_gain_grad: float32 [2048], P(('row', 'col', 'dp'))
The draws below stay inside these ranges and needn't reach their ends.
Inputs may be any that keep to these rules, and one draw needn't show every extreme that they name: `segments`: within each sequence of 768 tokens the segment numbers start at 0 and never fall; every document holds at least 200 tokens; in every draw one sequence is a single document and another holds 3 documents.
All inputs are finite; a program needn't handle non-finite values.
Results may differ from the reference program's by a relative error of at most 0.028.
Values may be sent and summed in bfloat16 or wider, within the bound.
No kernel may reach another device: no remote copies, remote signals or barrier semaphores. Data moves between devices by JAX's collectives and lax.ppermute only.
A program may use at most 192 MiB of HBM per device.

```python
import jax
import jax.numpy as jnp
from jax import lax

D = 2048
HEADS = 16
KV_HEADS = 16
HEAD = 128
FF = 8192
SEQ = 768
MAX_DOCS = 3
SEQS = 1
MIN_DOC = 200
TOKENS = 12288
N_DP = 16


def column_scale(key, columns, top_scale, jitter):
    fraction = jnp.arange(columns, dtype=jnp.float32) / (columns - 1)
    wobble = jax.random.uniform(key, (columns,), jnp.float32, -jitter, jitter)
    return jnp.exp(jnp.log(top_scale) * fraction + wobble)


def rising_matrix(scale_key, rows_in, columns, top_scale, entries):
    return entries * rows_in ** (-0.5) * column_scale(scale_key, columns, top_scale, 0.2)[None, :]


def draw_w_query(key, part):
    key = jax.random.fold_in(key, 11)
    entry_key, scale_key = jax.random.split(key)
    entries = jax.random.normal(entry_key, (D, HEADS * HEAD), jnp.float32)
    top_scale = 1.8
    return rising_matrix(scale_key, D, HEADS * HEAD, top_scale, entries).astype(jnp.bfloat16)


def draw_w_key(key, part):
    key = jax.random.fold_in(key, 12)
    entry_key, scale_key = jax.random.split(key)
    entries = jax.random.normal(entry_key, (D, KV_HEADS * HEAD), jnp.float32)
    top_scale = 1.8
    return rising_matrix(scale_key, D, KV_HEADS * HEAD, top_scale, entries).astype(jnp.bfloat16)


def draw_w_mix(key, part):
    key = jax.random.fold_in(key, 13)
    entry_key, scale_key = jax.random.split(key)
    entries = jax.random.normal(entry_key, (HEADS * HEAD, D), jnp.float32)
    top_scale = 4.0
    return rising_matrix(scale_key, HEADS * HEAD, D, top_scale, entries).astype(jnp.bfloat16)


def draw_w_down(key, part):
    key = jax.random.fold_in(key, 14)
    entry_key, scale_key = jax.random.split(key)
    entries = jax.random.normal(entry_key, (FF, D), jnp.float32)
    top_scale = 4.0
    return rising_matrix(scale_key, FF, D, top_scale, entries).astype(jnp.bfloat16)


def draw_inputs(key, part):
    key = jax.random.fold_in(key, 15)
    entry_key, row_key = jax.random.split(key, 2)
    entries = jnp.clip(jax.random.normal(entry_key, (TOKENS, D), jnp.float32), -5.0, 5.0)
    row_scale = jnp.exp(jax.random.uniform(row_key, (TOKENS, 1), jnp.float32, jnp.log(0.5), jnp.log(4.0)))
    return (entries * row_scale).astype(jnp.bfloat16)


def draw_segments(key, part):
    key = jax.random.fold_in(key, 5)
    count_key, cut_key, pick_key, other_key = jax.random.split(key, 4)
    seq_total = SEQS * N_DP
    seq_index = jnp.arange(seq_total, dtype=jnp.int32)
    counts = jax.random.randint(count_key, (seq_total,), 1, MAX_DOCS + 1)
    whole_seq = jax.random.randint(pick_key, (), 0, seq_total)
    full_seq = (whole_seq + 1 + jax.random.randint(other_key, (), 0, seq_total - 1)) % seq_total
    counts = jnp.where(seq_index == whole_seq, 1, counts)
    counts = jnp.where(seq_index == full_seq, MAX_DOCS, counts)
    spare_room = SEQ - counts * MIN_DOC
    cut_points = jax.random.randint(cut_key, (seq_total, MAX_DOCS - 1), 0, spare_room[:, None] + 1)
    cut_points = jnp.sort(cut_points, axis=1)
    doc_number = jnp.arange(1, MAX_DOCS, dtype=jnp.int32)
    doc_starts = doc_number[None, :] * MIN_DOC + cut_points
    live_docs = doc_number[None, :] < counts[:, None]
    doc_starts = jnp.where(live_docs, doc_starts, SEQ + 1)
    position = jnp.arange(SEQ, dtype=jnp.int32)
    segment_ids = jnp.sum((position[None, :, None] >= doc_starts[:, None, :]).astype(jnp.int32), axis=2)
    return segment_ids.reshape(-1).astype(jnp.int32)


def level_of(stream_key, dims, pieces, low, largest):
    def one(dim, parts):
        steps = jax.random.uniform(jax.random.fold_in(jax.random.fold_in(stream_key, 6), dim), (parts,), jnp.float32, low / len(pieces), largest / len(pieces))
        return jnp.repeat(jnp.exp(steps), dims[dim] // parts).reshape((-1,) + (1,) * (len(dims) - dim - 1))

    level = one(*pieces[0])
    for cut in pieces[1:]:
        level = level * one(*cut)
    return level


def normal_values(rng, extent, scale, most, shards=(), held_as=jnp.bfloat16):
    factor_of = level_of(rng, extent, shards, -0.22, 0.18) if shards else 1.0
    values = jax.random.normal(rng, extent, jnp.float32) * scale * factor_of
    return jnp.minimum(jnp.maximum(values, -most), most).astype(held_as)


def setup_inputs(seed: int = 0) -> dict:
    splits = jax.random.split(jax.random.key(seed), 15)
    inputs = draw_inputs(jax.random.fold_in(splits[14], 71), 0)
    segments = draw_segments(jax.random.fold_in(splits[14], 71), 0)
    w_query = draw_w_query(jax.random.fold_in(splits[14], 71), 0)
    w_key = draw_w_key(jax.random.fold_in(splits[14], 71), 0)
    w_value = normal_values(splits[4], (D, KV_HEADS * HEAD), D ** -0.5, 0.125, ((0, 2), (1, 4)))
    w_mix = draw_w_mix(jax.random.fold_in(splits[14], 71), 0)
    w_gate = normal_values(splits[6], (D, FF), D ** -0.5, 0.125, ((0, 2), (1, 4)))
    w_up = normal_values(splits[7], (D, FF), D ** -0.5, 0.125, ((0, 2), (1, 4)))
    w_down = draw_w_down(jax.random.fold_in(splits[14], 71), 0)
    attn_gain = jnp.clip(1.0 + 0.15 * jax.random.normal(splits[9], (D,), jnp.float32), 0.25, 1.75)
    ffn_gain = jnp.clip(1.0 + 0.15 * jax.random.normal(splits[10], (D,), jnp.float32), 0.25, 1.75)
    query_gain = jnp.clip(1.0 + 0.15 * jax.random.normal(splits[11], (HEADS * HEAD,), jnp.float32), 0.25, 1.75)
    key_gain = jnp.clip(1.0 + 0.15 * jax.random.normal(splits[12], (KV_HEADS * HEAD,), jnp.float32), 0.25, 1.75)
    out_grad = normal_values(splits[13], (TOKENS, D), 1.0, 6.0, ((0, 16), (1, 2)))
    return {"inputs": inputs, "segments": segments, "w_query": w_query, "w_key": w_key, "w_value": w_value, "w_mix": w_mix, "w_gate": w_gate, "w_up": w_up, "w_down": w_down, "attn_gain": attn_gain, "ffn_gain": ffn_gain, "query_gain": query_gain, "key_gain": key_gain, "out_grad": out_grad}


@jax.custom_vjp
def low(v):
    return lax.optimization_barrier(v.astype(jnp.bfloat16)).astype(jnp.float32)

@jax.custom_vjp
def low_back(v):
    return v

def low_keep(v):
    return (low(v), None)

def low_pass(kept, grad):
    return (grad,)

def back_keep(v):
    return (v, None)

def back_low(kept, grad):
    return (low(grad),)
low.defvjp(low_keep, low_pass)
low_back.defvjp(back_keep, back_low)
EPSILON = 1e-06
ROPE_BASE = 500000.0
MASKED = -1e+30

def product(left_side, right_side):
    return jnp.dot(left_side, right_side, precision=lax.Precision.HIGHEST)

def angle_tables(segment_ids):
    seq_length = segment_ids.shape[-1]
    step_index = jnp.arange(seq_length, dtype=jnp.int32)
    earlier = jnp.concatenate([segment_ids[..., :1] - 1, segment_ids[..., :-1]], axis=-1)
    begins = jnp.where(segment_ids != earlier, step_index, 0)
    places = (step_index - lax.cummax(begins, axis=segment_ids.ndim - 1)).astype(jnp.float32)
    half_width = HEAD // 2
    frequency = ROPE_BASE ** (-2.0 * jnp.arange(half_width, dtype=jnp.float32) / HEAD)
    angles = places[..., None] * frequency
    angles = jnp.concatenate([angles, angles], axis=-1)
    return (jnp.cos(angles), jnp.sin(angles))

def rotate(vector, cosine_table, sine_table):
    front_half, second = jnp.split(vector, 2, axis=-1)
    return vector * cosine_table + jnp.concatenate([-second, front_half], axis=-1) * sine_table

def attend(block_items):
    queries, key_rows, value_rows, segment_ids = block_items
    group_size = HEADS // KV_HEADS
    key_rows = jnp.repeat(key_rows, group_size, axis=1)
    value_rows = jnp.repeat(value_rows, group_size, axis=1)
    scores = jnp.einsum('qhd,khd->hqk', queries, key_rows, precision=lax.Precision.HIGHEST) * HEAD ** (-0.5)
    scores = low_back(scores)
    step_index = jnp.arange(segment_ids.shape[0], dtype=jnp.int32)
    allowed = (segment_ids[:, None] == segment_ids[None, :]) & (step_index[:, None] >= step_index[None, :])
    scores = jnp.where(allowed[None], scores, MASKED)
    totals = jax.nn.logsumexp(scores, axis=-1, keepdims=True)
    weights = low(jnp.exp(scores - totals))
    return jnp.einsum('hqk,khd->qhd', weights, value_rows, precision=lax.Precision.HIGHEST)

def post_norm(branch, gain_vector):
    return gain_vector * branch * lax.rsqrt(lax.optimization_barrier(jnp.mean(branch * branch, axis=-1, keepdims=True)) + EPSILON)

def forward(inputs, w_query, w_key, w_value, w_mix, w_gate, w_up, w_down, attn_gain, ffn_gain, query_gain, key_gain, cosines, sines, segments):
    token_count = inputs.shape[0]
    sequences = token_count // SEQ
    queries = low_back(product(inputs, w_query))
    key_states = low_back(product(inputs, w_key))
    value_states = low(low_back(product(inputs, w_value)))
    queries = queries * lax.rsqrt(lax.optimization_barrier(jnp.mean(queries * queries, axis=-1, keepdims=True)) + EPSILON) * query_gain
    key_states = key_states * lax.rsqrt(lax.optimization_barrier(jnp.mean(key_states * key_states, axis=-1, keepdims=True)) + EPSILON) * key_gain
    queries = low(rotate(queries.reshape(token_count, HEADS, HEAD), cosines, sines))
    key_states = low(rotate(key_states.reshape(token_count, KV_HEADS, HEAD), cosines, sines))
    mixed_heads = lax.map(jax.checkpoint(attend), (queries.reshape(sequences, SEQ, HEADS, HEAD), key_states.reshape(sequences, SEQ, KV_HEADS, HEAD), value_states.reshape(sequences, SEQ, KV_HEADS, HEAD), segments.reshape(sequences, SEQ)))
    mixed_heads = low_back(low(mixed_heads.reshape(token_count, HEADS * HEAD)))
    attn_branch = low_back(product(mixed_heads, w_mix))
    hidden_state = inputs + post_norm(attn_branch, attn_gain)
    hidden_low = low(hidden_state)
    gate_states = low_back(product(hidden_low, w_gate))
    up_states = low_back(product(hidden_low, w_up))
    unit_values = low(jax.nn.silu(gate_states) * up_states)
    ffn_branch = low_back(product(unit_values, w_down))
    return hidden_state + post_norm(ffn_branch, ffn_gain)

def reference(inputs, segments, w_query, w_key, w_value, w_mix, w_gate, w_up, w_down, attn_gain, ffn_gain, query_gain, key_gain, out_grad):
    cosines, sines = angle_tables(segments.reshape(-1, SEQ))
    cosines = cosines.reshape(-1, 1, HEAD)
    sines = sines.reshape(-1, 1, HEAD)
    floats = [member.astype(jnp.float32) for member in (inputs, w_query, w_key, w_value, w_mix, w_gate, w_up, w_down, attn_gain, ffn_gain, query_gain, key_gain)]

    def closed(*members):
        return forward(*members, cosines, sines, segments)
    result, pullback = jax.vjp(closed, *floats)
    gradients = pullback(out_grad.astype(jnp.float32))
    return (result.astype(jnp.bfloat16), gradients[0], gradients[1], gradients[2], gradients[3], gradients[4], gradients[5], gradients[6], gradients[7], gradients[8], gradients[9], gradients[10], gradients[11])
```

```python
import jax
import jax.numpy as jnp
from jax import lax
from jax.sharding import Mesh, PartitionSpec as P

D = 2048
HEADS = 16
HEAD = 128
SEQ = 768
NEAR = D // 2
EPSILON = 1e-06
ROPE_BASE = 500000.0
MASKED = -1e30
LOW = jnp.bfloat16
F32 = jnp.float32
RING = 4
BLOCK = SEQ // 8


def dot(a, b, dims=((1,), (0,))):
    return lax.dot_general(a, b, (dims, ((), ())), preferred_element_type=F32)


def ring_shift(a, axes, step):
    return lax.ppermute(a, axes, [(i, (i + step) % RING) for i in range(RING)])


def z_shift(a, step):
    return ring_shift(a, "z", step)


def x_shift(a, step):
    return ring_shift(a, ("xh", "xl"), step)


def y_shift(a, step):
    return ring_shift(a, "y", step)


def core_swap(a):
    return lax.ppermute(a, "core", [(0, 1), (1, 0)])


def pair_swap(a):
    return lax.ppermute(a, "xl", [(0, 1), (1, 0)])


def pick(blocks, index, axis=0):
    return lax.dynamic_index_in_dim(blocks, index, axis, keepdims=False)


def angle_tables(segment_ids):
    step_index = jnp.arange(SEQ, dtype=jnp.int32)
    earlier = jnp.concatenate([segment_ids[:1] - 1, segment_ids[:-1]])
    begins = jnp.where(segment_ids != earlier, step_index, 0)
    places = (step_index - lax.cummax(begins)).astype(F32)
    frequency = ROPE_BASE ** (-2.0 * jnp.arange(HEAD // 2, dtype=F32) / HEAD)
    angles = places[:, None] * frequency
    angles = jnp.concatenate([angles, angles], axis=-1)
    return jnp.cos(angles)[:, None], jnp.sin(angles)[:, None]


def rotate(vector, cosines, sines):
    first, second = jnp.split(vector, 2, axis=-1)
    return vector * cosines + jnp.concatenate([-second, first], axis=-1) * sines


def rotate_back(vector, cosines, sines):
    first, second = jnp.split(vector * sines, 2, axis=-1)
    return vector * cosines + jnp.concatenate([second, -first], axis=-1)


class Place:
    def __init__(self):
        self.s = lax.axis_index("xl")
        self.xh = lax.axis_index("xh")
        self.x = self.xh * 2 + self.s
        self.y = lax.axis_index("y")
        self.c = lax.axis_index("core")
        self.z = lax.axis_index("z")
        self.home = self.c == self.s


def to_sequence(at, a):
    first = lax.ppermute(a, ("core", "xl"), [(0, 2), (3, 1), (2, 3), (1, 0)])
    second = lax.ppermute(first, ("core", "xl"), [(0, 2), (3, 1)])
    return jnp.where(at.home, a, first), jnp.where(at.home, first, second)


def from_sequence(at, a):
    halves = a[:, :NEAR], a[:, NEAR:]
    received = []
    for k in range(2):
        sent = jnp.where(at.c == k, halves[0], halves[1])
        perm = [(c * 2 + s, s * 2 + (s ^ c ^ k)) for s in range(2) for c in range(2)]
        received.append(lax.ppermute(sent, ("core", "xl"), perm))
    return received


def in_order(at, received, width):
    flat = jnp.stack([r.reshape(RING, -1, width) for r in received])
    out = []
    for c in range(2):
        part = pick(flat, at.s ^ at.c ^ c)
        for z in range(RING):
            out.append(pick(part, (at.z - z) % RING))
    return jnp.concatenate(out, axis=0)


def own_rows(at, a, other=False):
    blocks = a.reshape(2, RING, BLOCK, -1)
    half = pick(blocks, 1 - at.c if other else at.c)
    return jnp.concatenate([pick(half, (at.z - i) % RING) for i in range(RING)], axis=0)


def token_order(at, own, other):
    flat = jnp.stack([own, other]).reshape(2, RING, BLOCK, -1)
    out = []
    for c in range(2):
        part = pick(flat, at.c ^ c)
        for z in range(RING):
            out.append(pick(part, (at.z - z) % RING))
    return jnp.concatenate(out, axis=0)


def reduce_rows(left_own, left_other, right, dims=((1,), (0,))):
    sent = dot(left_other, right, dims).astype(LOW)
    came = core_swap(sent)
    own = dot(left_own, right, dims) + came.astype(F32)
    total = own[:BLOCK]
    for i in range(1, RING):
        total = total + z_shift(own[i * BLOCK : (i + 1) * BLOCK].astype(LOW), -i).astype(F32)
    return total


def gather_z(rows):
    return jnp.concatenate([rows] + [z_shift(rows, i) for i in range(1, RING)], axis=0)


def fetch(mine):
    half = mine.shape[0] // 2
    return jnp.concatenate([x_shift(mine[:half], -1), x_shift(mine[half:], 1)], axis=0)


def reduce_weight(at, grad, x_first):
    n = grad.shape[1]
    blocks = grad.reshape(2, RING, 2, 128, n)

    def over_y(b):
        total = pick(b, at.y).astype(F32)
        for i in range(1, RING):
            total = total + y_shift(pick(b, (at.y + i) % RING), i).astype(F32)
        return total

    def over_x(b):
        total = pick(b[0], at.xh).astype(F32)
        for i in range(1, RING):
            there = ((at.x + i) % RING) // 2
            total = total + x_shift(pick(b[i % 2], there), i).astype(F32)
        return total

    if x_first:
        rows = over_x(blocks.transpose(0, 2, 1, 3, 4)).astype(LOW)
        rows = over_y(rows)
    else:
        rows = over_y(blocks.transpose(1, 0, 2, 3, 4)).astype(LOW)
        rows = over_x(rows)
    rows = rows.reshape(2, 64, n)
    own = pick(rows, at.c)
    came = core_swap(pick(rows, 1 - at.c).astype(LOW)).astype(F32)
    first = at.c == 0
    return jnp.where(first, own, came), jnp.where(first, came, own)


def reduce_vector(vector):
    for shift in (y_shift, x_shift):
        total = vector
        for i in range(1, RING):
            total = total + shift(vector, i)
        vector = total
    return vector


def all_stats(pair):
    pair = pair + core_swap(pair)
    return pair + (z_shift(pair, 1) + z_shift(pair, 2) + z_shift(pair, 3))


def scores_of(queries, keys, visible):
    scores = jnp.einsum("qhd,khd->hqk", queries, keys, preferred_element_type=F32) * HEAD**-0.5
    return jnp.where(visible[None], scores, MASKED)


def attend(queries, keys, values, visible):
    scores = scores_of(queries, keys, visible)
    peak = jnp.max(scores, axis=-1, keepdims=True)
    totals = peak + jnp.log(jnp.sum(jnp.exp(scores - peak), axis=-1, keepdims=True))
    weights = jnp.exp(scores - totals).astype(LOW)
    mixed = jnp.einsum("hqk,khd->qhd", weights, values, preferred_element_type=F32)
    return mixed.astype(LOW), totals


def attend_back(queries, keys, values, visible, totals, mixed_grad):
    weights = jnp.exp(scores_of(queries, keys, visible) - totals)
    weight_grad = jnp.einsum("qhd,khd->hqk", mixed_grad, values, preferred_element_type=F32)
    values_grad = jnp.einsum(
        "hqk,qhd->khd", weights.astype(LOW), mixed_grad, preferred_element_type=F32
    )
    centre = jnp.sum(weights * weight_grad, axis=-1, keepdims=True)
    score_grad = (weights * (weight_grad - centre)).astype(LOW)
    queries_grad = jnp.einsum("hqk,khd->qhd", score_grad, keys, preferred_element_type=F32)
    keys_grad = jnp.einsum("hqk,qhd->khd", score_grad, queries, preferred_element_type=F32)
    return queries_grad * HEAD**-0.5, keys_grad * HEAD**-0.5, values_grad


def scale_of(branch):
    return lax.rsqrt(jnp.mean(branch * branch, axis=1, keepdims=True) + EPSILON)


def norm_back(upstream, branch, scale, gain):
    gain_part = jnp.sum(upstream * branch * scale, axis=0)
    scaled = upstream * gain
    inner = jnp.sum(scaled * branch, axis=1, keepdims=True)
    return (scale * scaled - branch * (scale**3 * inner / D)).astype(LOW), gain_part


def local(
    inputs, segments, w_query, w_key, w_value, w_mix, w_gate, w_up, w_down,
    attn_gain, ffn_gain, query_gain, key_gain, out_grad,
):
    at = Place()

    near, far = to_sequence(at, inputs)
    states = jnp.concatenate([near, far], axis=1)
    segment_ids = jnp.where(at.home, segments, core_swap(segments))

    def columns(w):
        return lax.dynamic_slice_in_dim(w, at.c * (w.shape[1] // 2), w.shape[1] // 2, 1)

    def rows(w):
        return lax.dynamic_slice_in_dim(w, at.c * (w.shape[0] // 2), w.shape[0] // 2, 0)

    mine = jnp.concatenate([columns(w_query), columns(w_key), columns(w_value)], axis=1)
    w_qkv = jnp.concatenate([mine, fetch(mine)], axis=0)
    mine = rows(w_mix)
    w_mixed = jnp.concatenate([mine, fetch(mine)], axis=1)
    mine = jnp.concatenate([columns(w_gate), columns(w_up)], axis=1)
    w_pair = jnp.concatenate([mine, fetch(mine)], axis=0)
    mine = rows(w_down)
    w_out = jnp.concatenate([mine, fetch(mine)], axis=1)

    gains = jnp.concatenate([attn_gain, ffn_gain, query_gain, key_gain])
    their_gains = pair_swap(gains)
    attn_gains = jnp.concatenate([attn_gain, their_gains[:NEAR]])
    ffn_gains = jnp.concatenate([ffn_gain, their_gains[NEAR:D]])
    head_gains = jnp.where(at.home, gains[D:], their_gains[D:])
    query_gains = head_gains[:256].reshape(2, HEAD)
    key_gains = head_gains[256:].reshape(2, HEAD)

    cosines, sines = angle_tables(segment_ids)
    step_index = jnp.arange(SEQ, dtype=jnp.int32)
    visible = (segment_ids[:, None] == segment_ids[None]) & (step_index[:, None] >= step_index)
    qkv = dot(states, w_qkv)
    queries = qkv[:, :256].reshape(SEQ, 2, HEAD)
    keys = qkv[:, 256:512].reshape(SEQ, 2, HEAD)
    stats = all_stats(
        jnp.stack([jnp.sum(queries * queries, axis=(1, 2)), jnp.sum(keys * keys, axis=(1, 2))])
    )
    query_rms, key_rms = lax.rsqrt(stats / D + EPSILON)[:, :, None, None]
    query_low = rotate(queries * query_rms * query_gains, cosines, sines).astype(LOW)
    key_low = rotate(keys * key_rms * key_gains, cosines, sines).astype(LOW)
    value_low = qkv[:, 512:].astype(LOW).reshape(SEQ, 2, HEAD)
    mixed, totals = attend(query_low, key_low, value_low, visible)
    mixed = mixed.reshape(SEQ, 256)
    mixed_own, mixed_other = own_rows(at, mixed), own_rows(at, mixed, True)
    attn_branch = gather_z(reduce_rows(mixed_own, mixed_other, w_mixed).astype(LOW)).astype(F32)
    attn_rms = scale_of(attn_branch)
    hidden = own_rows(at, states).astype(F32) + attn_gains * attn_branch * attn_rms
    hidden_own = hidden.astype(LOW)
    hidden_other = core_swap(hidden_own)

    def units_of(rows):
        pair = dot(rows, w_pair)
        gate, up = pair[:, :1024], pair[:, 1024:]
        return gate, up, (jax.nn.silu(gate) * up).astype(LOW)

    gate_own, up_own, units_own = units_of(hidden_own)
    gate_other, up_other, units_other = units_of(hidden_other)
    ffn_branch = gather_z(reduce_rows(units_own, units_other, w_out).astype(LOW)).astype(F32)
    ffn_rms = scale_of(ffn_branch)
    block_rows = (hidden + ffn_gains * ffn_branch * ffn_rms).astype(LOW)
    block_out = in_order(at, from_sequence(at, block_rows), NEAR)

    upstream_near, upstream_far = to_sequence(at, out_grad)
    upstream = jnp.concatenate([upstream_near, upstream_far], axis=1)
    upstream = own_rows(at, upstream).astype(F32)
    branch_own, ffn_gain_part = norm_back(upstream, ffn_branch, ffn_rms, ffn_gains)
    branch_other = core_swap(branch_own)

    def units_back(branch, gate, up):
        units_grad = dot(branch, w_out, ((1,), (1,)))
        sigmoid = jax.nn.sigmoid(gate)
        gate_back = units_grad * up * sigmoid * (1.0 + gate * (1.0 - sigmoid))
        up_back = units_grad * gate * sigmoid
        return jnp.concatenate([gate_back.astype(LOW), up_back.astype(LOW)], axis=1)

    pair_own = units_back(branch_own, gate_own, up_own)
    pair_other = units_back(branch_other, gate_other, up_other)
    hidden_sum = reduce_rows(pair_own, pair_other, w_pair, ((1,), (1,)))
    hidden_rows = hidden_sum + upstream[:BLOCK]
    hidden_grad = gather_z(hidden_sum.astype(LOW)).astype(F32) + upstream
    mix_own, attn_gain_part = norm_back(hidden_grad, attn_branch, attn_rms, attn_gains)
    mix_other = core_swap(mix_own)

    down_grad = dot(
        jnp.concatenate([branch_own, branch_other]),
        jnp.concatenate([units_own, units_other]),
        ((0,), (0,)),
    ).astype(LOW)
    hidden_low = jnp.concatenate([hidden_own, hidden_other])
    pair_back = jnp.concatenate([pair_own, pair_other])
    gate_grad = dot(hidden_low, pair_back[:, :1024], ((0,), (0,))).astype(LOW)
    up_grad = dot(hidden_low, pair_back[:, 1024:], ((0,), (0,))).astype(LOW)

    mixed_grad = token_order(
        at,
        dot(mix_own, w_mixed, ((1,), (1,))).astype(LOW),
        dot(mix_other, w_mixed, ((1,), (1,))).astype(LOW),
    ).reshape(SEQ, 2, HEAD)
    query_rot_grad, key_rot_grad, value_back = attend_back(
        query_low, key_low, value_low, visible, totals, mixed_grad
    )
    query_normed_grad = rotate_back(query_rot_grad, cosines, sines)
    key_normed_grad = rotate_back(key_rot_grad, cosines, sines)
    query_gain_part = jnp.sum(query_normed_grad * queries * query_rms, axis=0).reshape(-1)
    key_gain_part = jnp.sum(key_normed_grad * keys * key_rms, axis=0).reshape(-1)
    query_hat = query_normed_grad * query_gains
    key_hat = key_normed_grad * key_gains
    query_dot, key_dot = all_stats(
        jnp.stack([jnp.sum(query_hat * queries, axis=(1, 2)), jnp.sum(key_hat * keys, axis=(1, 2))])
    )[:, :, None, None]
    query_back = (query_rms * query_hat - queries * (query_rms**3 * query_dot / D)).astype(LOW)
    key_back = (key_rms * key_hat - keys * (key_rms**3 * key_dot / D)).astype(LOW)
    qkv_back = jnp.concatenate(
        [
            query_back.reshape(SEQ, 256),
            key_back.reshape(SEQ, 256),
            value_back.astype(LOW).reshape(SEQ, 256),
        ],
        axis=1,
    )
    input_sum = reduce_rows(
        own_rows(at, qkv_back), own_rows(at, qkv_back, True), w_qkv, ((1,), (1,))
    )
    input_rows = from_sequence(at, (input_sum + hidden_rows).astype(LOW))
    input_rows = gather_z(jnp.stack(input_rows)[None])
    input_grad = in_order(at, [input_rows[:, 0], input_rows[:, 1]], NEAR).astype(F32)

    attn_grad = jnp.concatenate(
        [
            dot(states, qkv_back, ((0,), (0,))).astype(LOW),
            dot(
                jnp.concatenate([mix_own, mix_other]),
                jnp.concatenate([mixed_own, mixed_other]),
                ((0,), (0,)),
            ).astype(LOW),
        ],
        axis=1,
    )

    down = jnp.concatenate(reduce_weight(at, down_grad, False), axis=1).T
    gate = jnp.concatenate(reduce_weight(at, gate_grad, True), axis=1)
    up = jnp.concatenate(reduce_weight(at, up_grad, False), axis=1)
    attn0, attn1 = reduce_weight(at, attn_grad, True)
    query, key, value, mix = (
        jnp.concatenate([attn0[:, i : i + 256], attn1[:, i : i + 256]], axis=1)
        for i in range(0, 1024, 256)
    )

    heads_part = jnp.stack([query_gain_part, key_gain_part])
    width_part = jnp.stack([attn_gain_part, ffn_gain_part])
    width_part = jnp.where(
        at.s == 0, width_part, jnp.concatenate([width_part[:, NEAR:], width_part[:, :NEAR]], axis=1)
    )
    gain_part = jnp.concatenate([heads_part, width_part], axis=1)
    theirs = core_swap(gain_part)
    first = at.c == 0
    totals = reduce_vector(
        jnp.concatenate(
            [
                jnp.where(first, heads_part, theirs[:, :256]),
                jnp.where(first, theirs[:, :256], heads_part),
                width_part + theirs[:, 256:],
            ],
            axis=1,
        )
    )
    part = at.y * 4 + at.xh * 2 + at.c
    heads_total = lax.dynamic_slice_in_dim(totals, at.s * 256 + part * 16, 16, 1)
    width_total = lax.dynamic_slice_in_dim(totals, 512 + at.s * NEAR + part * 64, 64, 1)

    return (
        block_out, input_grad, query, key, value, mix.T, gate, up, down,
        width_total[0], width_total[1], heads_total[0], heads_total[1],
    )


def solution(mesh):
    fine = Mesh(mesh.devices.reshape(4, 2, 2, 4, 2), ("y", "xh", "core", "z", "xl"))
    dp = ("y", "xh", "core")
    row, col = "z", "xl"
    return jax.shard_map(
        local,
        mesh=fine,
        in_specs=(
            P(dp, col), P(dp), P(col, row), P(col, row), P(col, row), P(row, col),
            P(col, row), P(col, row), P(row, col), P(col), P(col), P((row, col)),
            P((row, col)), P(dp, col),
        ),
        out_specs=(
            P(dp, col), P(dp, col),
            P((col,) + dp, row), P((col,) + dp, row), P((col,) + dp, row), P(row, (col,) + dp),
            P((col,) + dp, row), P((col,) + dp, row), P(row, (col,) + dp),
            P((col,) + dp), P((col,) + dp), P((row, col) + dp), P((row, col) + dp),
        ),
        check_vma=False,
    )
```

```python
import functools

import jax
import jax.numpy as jnp
from jax import lax
from jax.experimental import pallas as pl
from jax.experimental.pallas import tpu as pltpu
from jax.sharding import Mesh, PartitionSpec as P

D = 2048
HEAD = 128
SEQ = 768
NEAR = D // 2
OWN = SEQ // 2
RING = 4
BLOCK = SEQ // 8
EPSILON = 1e-06
ROPE_BASE = 500000.0
MASKED = -1e30
LOW = jnp.bfloat16
F32 = jnp.float32
FREE = pl.CostEstimate(flops=0, bytes_accessed=0, transcendentals=0)
PARAMS = pltpu.CompilerParams(vmem_limit_bytes=48 * 1024 * 1024)


def dot(a, b, dims=((1,), (0,))):
    return lax.dot_general(a, b, (dims, ((), ())), preferred_element_type=F32)


NT = ((1,), (1,))
TN = ((0,), (0,))


def after(value, *earlier):
    return lax.optimization_barrier((value, earlier))[0]


def ring_shift(a, axes, step):
    return lax.ppermute(a, axes, [(i, (i + step) % RING) for i in range(RING)])


def z_shift(a, step):
    return ring_shift(a, "z", step)


def plane_shift(a, step, swapped):
    pairs = []
    for y in range(4):
        for x in range(4):
            for c in range(2):
                there = ((y + step) % 4, x) if (c == 0) != swapped else (y, (x + step) % 4)
                xh, xl = x // 2, x % 2
                source = ((y * 2 + xh) * 2 + c) * 2 + xl
                pairs.append((source, ((there[0] * 2 + there[1] // 2) * 2 + c) * 2 + there[1] % 2))
    return lax.ppermute(a, ("y", "xh", "core", "xl"), pairs)


def core_swap(a):
    return lax.ppermute(a, "core", [(0, 1), (1, 0)])


def pair_swap(a):
    return lax.ppermute(a, "xl", [(0, 1), (1, 0)])


def wrap_swap(a):
    return lax.ppermute(a, ("xh", "xl"), [(0, 3), (3, 0), (1, 2), (2, 1)])


def pick(blocks, index, axis=0):
    return lax.dynamic_index_in_dim(blocks, index, axis, keepdims=False)


class Place:
    def __init__(self):
        self.s = lax.axis_index("xl")
        self.xh = lax.axis_index("xh")
        self.x = self.xh * 2 + self.s
        self.y = lax.axis_index("y")
        self.c = lax.axis_index("core")
        self.z = lax.axis_index("z")
        self.home = self.c == self.s
        steps = jnp.arange(RING, dtype=jnp.int32)
        back = (self.z - steps) % RING
        self.rows = jnp.concatenate([self.c * 4 + back, (1 - self.c) * 4 + back])
        first, second = steps[:, None], steps[None, :]
        dx = jnp.where(self.c == 0, second, first)
        dy = jnp.where(self.c == 0, first, second)
        self.columns = (
            (dx % 2) * 8 + ((self.y + dy) % 4) * 2 + ((self.x + dx) % 4) // 2
        ).reshape(-1)


def place_kernel(plan, sources, table, *refs):
    ins, outs, sems = refs[:sources], refs[sources:-1], refs[-1]
    copies = []
    for i, (source, there) in enumerate(plan(table, ins, outs)):
        copies.append(pltpu.make_async_copy(source, there, sems.at[i]))
        copies[-1].start()
    for copy in copies:
        copy.wait()


def place(plan, count, shapes, table, *sources):
    return pl.pallas_call(
        functools.partial(place_kernel, plan, len(sources)),
        in_specs=[pl.BlockSpec(memory_space=pltpu.SMEM)]
        + [pl.BlockSpec(memory_space=pltpu.HBM)] * len(sources),
        out_specs=tuple(pl.BlockSpec(memory_space=pltpu.HBM) for _ in shapes),
        out_shape=tuple(jax.ShapeDtypeStruct(shape, LOW) for shape in shapes),
        scratch_shapes=[pltpu.SemaphoreType.DMA((count,))],
        compiler_params=PARAMS,
        cost_estimate=FREE,
    )(jnp.stack(table).astype(jnp.int32), *sources)


def at_block(index, size):
    return pl.ds(pl.multiple_of(index * size, size), size)


def to_sequence(at, first, second, index):
    count = index.shape[0]

    def plan(table, ins, outs):
        own, other = ins
        return [
            (ref.at[at_block(table[i], BLOCK)], outs[0].at[pl.ds(i * BLOCK, BLOCK), pl.ds(lo, NEAR)])
            for i in range(count)
            for ref, lo in ((own, 0), (other, NEAR))
        ]

    return place(plan, 2 * count, [(count * BLOCK, D)], list(index), first, second)[0]


def first_hop(a):
    return lax.ppermute(a, ("core", "xl"), [(0, 2), (3, 1), (2, 3), (1, 0)])


def second_hop(at, a, first):
    second = lax.ppermute(first, ("core", "xl"), [(0, 2), (3, 1)])
    return jnp.where(at.home, a, first), jnp.where(at.home, first, second)


def order_rows(at, sources, index, which):
    joined = jnp.concatenate(sources) if len(sources) > 1 else sources[0]
    rows = sources[0].shape[0] // BLOCK

    def plan(table, ins, outs):
        return [
            (ins[0].at[at_block(table[i], BLOCK)], outs[0].at[pl.ds(i * BLOCK, BLOCK)])
            for i in range(8)
        ]

    table = index + rows * which if len(sources) > 1 else index * 2 + which
    return place(plan, 8, [(SEQ, joined.shape[1])], list(table), joined)[0]


def cut_columns(at, heights, *weights):
    width = weights[0].shape[1] // 2
    starts = [sum(heights[:i]) for i in range(len(heights))]

    def plan(table, ins, outs):
        return [
            (
                ref.at[pl.ds(start, height), at_block(table[0], width)],
                out.at[:, pl.ds(width * i, width)],
            )
            for i, ref in enumerate(ins)
            for start, height, out in zip(starts, heights, outs)
        ]

    shapes = [(height, width * len(weights)) for height in heights]
    return place(plan, len(heights) * len(weights), shapes, [at.c], *weights)


def cut_rows(at, weight):
    def plan(table, ins, outs):
        return [(ins[0].at[at_block(2 * table[0] + half, 512)], outs[half]) for half in range(2)]

    return place(plan, 2, [(512, NEAR)] * 2, [at.c], weight)


def join_columns(parts):
    starts = [sum(part.shape[1] for part in parts[:i]) for i in range(len(parts) + 1)]

    def plan(table, ins, outs):
        return [
            (ref, outs[0].at[:, pl.ds(starts[i], parts[i].shape[1])]) for i, ref in enumerate(ins)
        ]

    return place(plan, len(parts), [(D, starts[-1])], [0], *parts)[0]


def fetch(first, second):
    return pair_swap(first), wrap_swap(second)


def scatter_z(parts):
    total = parts[0]
    for i in range(1, RING):
        total = total + z_shift(parts[i], -i).astype(F32)
    return total


def gather_z(rows):
    return [rows] + [z_shift(rows, i) for i in range(1, RING)]


def all_stats(pair):
    theirs = core_swap(pair)
    pair = pair + jnp.concatenate([theirs[:, OWN:], theirs[:, :OWN]], axis=1)
    total = pair
    for i in range(1, RING):
        came, cut = z_shift(pair, i), OWN - i * BLOCK
        total = total + jnp.concatenate(
            [came[:, cut:OWN], came[:, :cut], came[:, OWN + cut :], came[:, OWN : OWN + cut]],
            axis=1,
        )
    return total


def plane_sum(parts, steps, total=None, *earlier):
    total = (parts[0] if total is None else total).astype(F32)
    for i in steps:
        total = total + plane_shift(after(parts[i], earlier), i, False).astype(F32)
    return total.astype(LOW)


def plane_second(rows):
    total = rows[:128].astype(F32)
    for i in range(1, RING):
        total = total + plane_shift(rows[i * 128 : (i + 1) * 128], i, True).astype(F32)
    return total


def share_cores(at, rows):
    rows = rows.reshape(2, 64, -1)
    own = pick(rows, at.c)
    came = core_swap(pick(rows, 1 - at.c).astype(LOW)).astype(F32)
    first = at.c == 0
    return jnp.where(first, own, came), jnp.where(first, came, own)


def tiled(kernel, steps, args, specs, outs, out_specs, scratch=()):
    return pl.pallas_call(
        kernel,
        grid=(steps,),
        in_specs=specs,
        out_specs=tuple(out_specs),
        out_shape=tuple(jax.ShapeDtypeStruct(shape, dtype) for shape, dtype in outs),
        scratch_shapes=list(scratch),
        compiler_params=PARAMS,
        cost_estimate=FREE,
    )(*args)


def whole(shape):
    return pl.BlockSpec(shape, lambda j: (0,) * len(shape))


def columns_of(block, width):
    return pl.BlockSpec((block.shape[0], width), lambda j: (0, j))


def rows_of(block, height):
    return pl.BlockSpec((height, block.shape[1]), lambda j: (j, 0))


def ones_dot(values):
    return lax.dot_general(
        jnp.ones((8, values.shape[1]), F32), values, (NT, ((), ())),
        precision=lax.Precision.HIGHEST, preferred_element_type=F32,
    )


def row_dot(rows, refs, start=0):
    value = 0.0
    for ref in refs:
        height = ref.shape[0]
        value += dot(rows[:, start : start + height], ref[...])
        start += height
    return value


def qkv_kernel(states_ref, *refs):
    *blocks, qkv_ref, sums_ref = refs
    j = pl.program_id(0)
    value = row_dot(states_ref, blocks)
    qkv_ref[...] = value

    @pl.when(j == 0)
    def _():
        sums_ref[...] = ones_dot(value * value)

    @pl.when(j == 1)
    def _():
        sums_ref[1:2, :] = ones_dot(value * value)[0:1, :]


def project(states, blocks):
    return tiled(
        qkv_kernel, 3, [states, *blocks],
        [whole(states.shape)] + [columns_of(block, 256) for block in blocks],
        [((SEQ, SEQ), F32), ((8, SEQ), F32)],
        [pl.BlockSpec((SEQ, 256), lambda j: (0, j)), whole((8, SEQ))],
    )


def put(outs, at, value):
    if len(outs) == 1:
        outs[0][:, at] = value.astype(LOW)
        return
    for i, ref in enumerate(outs):
        ref[:, at] = value[i * BLOCK : (i + 1) * BLOCK].astype(ref.dtype)


def result_of(came):
    if came is None:
        return [((OWN, D), LOW)]
    return [((BLOCK, D), F32)] + [((BLOCK, D), LOW)] * 3


def out_kernel_of(body, count, came):
    def kernel(*refs):
        outs = refs[count + (came is not None) :]
        for at, value in body(pl.program_id(0), refs[:count]):
            if came is not None:
                value += refs[count][:, at].astype(F32)
            put(outs, at, value)

    return kernel


def product(body, steps, args, specs, came=None):
    outs = result_of(came)
    extra = [] if came is None else [came]
    return tiled(
        out_kernel_of(body, len(args), came), steps, [*args, *extra],
        [*specs] + [whole(a.shape) for a in extra], outs, [whole(shape) for shape, _ in outs],
    )


def strip(start, j, size=256):
    return pl.ds(pl.multiple_of(start + j * size, 128), size)


def mix(left, near, far, came=None):
    def body(j, refs):
        left, near, far = refs
        yield strip(0, j, 512), dot(left[...], near[...])
        yield strip(NEAR, j, 512), dot(left[...], far[...])

    specs = [whole(left.shape), columns_of(near, 512), columns_of(far, 512)]
    return product(body, 2, [left, near, far], specs, came)


def down(units, blocks, came=None):
    def body(j, refs):
        units, *w = refs
        for i in range(2):
            value = dot(units[:, :512], w[2 * i][...]) + dot(units[:, 512:], w[2 * i + 1][...])
            yield strip(NEAR * i, j), value

    specs = [whole(units.shape)] + [columns_of(block, 256) for block in blocks]
    return product(body, 4, [units, *blocks], specs, came)


def starts_of(blocks):
    heights = [block.shape[0] for block in blocks]
    return [sum(heights[:i]) for i in range(len(heights))]


def pair_down(gate_back, up_back, gates, ups, came=None):
    def body(j, refs):
        gate_back, up_back, *w = refs
        for i, start in enumerate(starts_of(ups)):
            value = dot(gate_back[...], w[i][...], NT)
            value += dot(up_back[...], w[len(gates) + i][...], NT)
            yield strip(start, j, ups[i].shape[0] // 2), value

    specs = [whole(gate_back.shape)] * 2 + [rows_of(b, b.shape[0] // 2) for b in [*gates, *ups]]
    return product(body, 2, [gate_back, up_back, *gates, *ups], specs, came)


def qkv_down(back, blocks, came=None):
    def body(j, refs):
        back, *w = refs
        for i, start in enumerate(starts_of(blocks)):
            yield strip(start, j, blocks[i].shape[0] // 2), dot(back[...], w[i][...], NT)

    specs = [whole(back.shape)] + [rows_of(block, block.shape[0] // 2) for block in blocks]
    return product(body, 2, [back, *blocks], specs, came)


def units_kernel(count, rows_ref, *refs):
    gate_ref, up_ref, units_ref = refs[-3:]
    gate = row_dot(rows_ref, refs[:count])
    up = row_dot(rows_ref, refs[count:-3])
    gate_ref[...] = gate.astype(LOW)
    up_ref[...] = up.astype(LOW)
    units_ref[...] = (gate * jax.nn.sigmoid(gate) * up).astype(LOW)


def units_of(rows, gates, ups):
    return tiled(
        functools.partial(units_kernel, len(gates)), 4, [rows, *gates, *ups],
        [whole(rows.shape)] + [columns_of(block, 256) for block in [*gates, *ups]],
        [((OWN, 1024), LOW)] * 3, [pl.BlockSpec((OWN, 256), lambda j: (0, j))] * 3,
    )


def units_back_kernel(branch_ref, w0, w1, w2, w3, gate_ref, up_ref, gate_back_ref, up_back_ref):
    j = pl.program_id(0)
    for i, (near, far) in enumerate(((w0, w2), (w1, w3))):
        at = strip(512 * i, j)
        grad = dot(branch_ref[:, :NEAR], near[...], NT) + dot(branch_ref[:, NEAR:], far[...], NT)
        gate, up = gate_ref[:, at].astype(F32), up_ref[:, at].astype(F32)
        sigmoid = jax.nn.sigmoid(gate)
        gate_back_ref[:, at] = (grad * up * sigmoid * (1.0 + gate * (1.0 - sigmoid))).astype(LOW)
        up_back_ref[:, at] = (grad * gate * sigmoid).astype(LOW)


def units_back(branch, blocks, gate, up):
    return tiled(
        units_back_kernel, 2, [branch, *blocks, gate, up],
        [whole(branch.shape)] + [rows_of(block, 256) for block in blocks]
        + [whole(gate.shape)] * 2,
        [((OWN, 1024), LOW)] * 2, [whole((OWN, 1024))] * 2,
    )


def grad_kernel(pairs, *refs):
    table = refs[0]
    ins = refs[1 : 1 + 4 * pairs]
    rest = refs[1 + 4 * pairs :]
    extra = rest[0] if len(rest) == 7 else None
    outs, (buffer, sems) = rest[-6:-2], rest[-2:]
    copies = []
    for d in range(RING):
        at = d % 2
        if d >= 2:
            copies[d - 2].wait()
        places = [at_block(table[4 * d + e], 128) for e in range(RING)]
        start = 0
        for k in range(pairs):
            left0, left1, right0, right1 = ins[4 * k : 4 * k + 4]
            value = 0.0
            for left, right in ((left0, right0), (left1, right1)):
                chosen = jnp.concatenate([left[:, place] for place in places], axis=1)
                value += dot(chosen, right[...], TN)
            width = right0.shape[1]
            buffer[at, :, start : start + width] = value.astype(LOW)
            start += width
        if extra is not None:
            for e in range(RING):
                buffer[at, 128 * e : 128 * (e + 1), start:] = extra[places[e], :]
        copies.append(pltpu.make_async_copy(buffer.at[at], outs[d], sems.at[at]))
        copies[d].start()
    copies[2].wait()
    copies[3].wait()


def weight_grad(at, pairs, extra=None):
    width = sum(pair[2].shape[1] for pair in pairs) + (0 if extra is None else extra.shape[1])
    args = [a for pair in pairs for a in pair] + ([] if extra is None else [extra])
    return pl.pallas_call(
        functools.partial(grad_kernel, len(pairs)),
        in_specs=[pl.BlockSpec(memory_space=pltpu.SMEM)]
        + [pl.BlockSpec(memory_space=pltpu.VMEM)] * len(args),
        out_specs=tuple(pl.BlockSpec(memory_space=pltpu.HBM) for _ in range(RING)),
        out_shape=tuple(jax.ShapeDtypeStruct((512, width), LOW) for _ in range(RING)),
        scratch_shapes=[pltpu.VMEM((2, 512, width), LOW), pltpu.SemaphoreType.DMA((2,))],
        compiler_params=PARAMS,
        cost_estimate=FREE,
    )(at.columns.astype(jnp.int32), *args)


def turn(v, cosines, sines):
    return v * cosines + pltpu.roll(v, HEAD // 2, 1) * sines


def turn_back(v, cosines, sines):
    return v * cosines - pltpu.roll(v, HEAD // 2, 1) * sines


TILE = 256


def seen(place_ref, row_ref, lo):
    here = place_ref[lo : lo + TILE]
    there = row_ref[0:1, :]
    return (there <= here[:, 0:1]) & (there >= here[:, 1:2])


def attend_kernel(
    qkv_ref, sums_ref, gain_ref, cos_ref, sin_ref, place_ref, row_ref,
    mixed_ref, low_ref, lse_ref, rms_ref,
):
    cosines, sines = cos_ref[...], sin_ref[...]
    rms_ref[...] = lax.rsqrt(sums_ref[...] * (1.0 / D) + EPSILON).T
    for h in range(2):
        at = slice(h * HEAD, (h + 1) * HEAD)
        q = qkv_ref[:, h * HEAD : (h + 1) * HEAD] * rms_ref[:, 0:1] * gain_ref[0:1, at]
        k = qkv_ref[:, 256 + h * HEAD : 256 + (h + 1) * HEAD] * rms_ref[:, 1:2] * gain_ref[1:2, at]
        low_ref[:, h * HEAD : (h + 1) * HEAD] = turn(q, cosines, sines).astype(LOW)
        k = turn(k, cosines, sines).astype(LOW)
        v = qkv_ref[:, 512 + h * HEAD : 512 + (h + 1) * HEAD].astype(LOW)
        low_ref[:, 256 + h * HEAD : 256 + (h + 1) * HEAD] = k
        low_ref[:, 512 + h * HEAD : 512 + (h + 1) * HEAD] = v
        for lo in range(0, SEQ, TILE):
            q = low_ref[lo : lo + TILE, h * HEAD : (h + 1) * HEAD]
            scores = dot(q, k, NT) * HEAD**-0.5
            scores = jnp.where(seen(place_ref, row_ref, lo), scores, MASKED)
            peak = jnp.max(scores, axis=1, keepdims=True)
            weights = jnp.exp(scores - peak)
            total = jnp.sum(weights, axis=1, keepdims=True)
            weights = (weights * (1.0 / total)).astype(LOW)
            mixed_ref[lo : lo + TILE, at] = dot(weights, v).astype(LOW)
            lse_ref[lo : lo + TILE, h : h + 1] = peak + jnp.log(total)


def attend_back_kernel(
    qkv_ref, rms_ref, gain_ref, cos_ref, sin_ref, place_ref, row_ref, low_ref, lse_ref,
    own_ref, other_ref, near_ref, far_ref,
    hat_ref, value_ref, dots_ref, part_ref, dk_ref, dv_ref, grad_ref,
):
    cosines, sines = cos_ref[...], sin_ref[...]
    for i, ref in enumerate((own_ref, other_ref)):
        grad = dot(ref[:, :NEAR], near_ref[...], NT) + dot(ref[:, NEAR:], far_ref[...], NT)
        grad_ref[OWN * i : OWN * (i + 1), :] = grad.astype(LOW)
    for h in range(2):
        at = slice(h * HEAD, (h + 1) * HEAD)
        k_at = slice(256 + h * HEAD, 256 + (h + 1) * HEAD)
        k = low_ref[:, k_at]
        v = low_ref[:, 512 + h * HEAD : 512 + (h + 1) * HEAD]
        for lo in range(0, SEQ, TILE):
            q = low_ref[lo : lo + TILE, at]
            grad = grad_ref[lo : lo + TILE, at]
            scores = dot(q, k, NT) * HEAD**-0.5
            weights = jnp.exp(scores - lse_ref[lo : lo + TILE, h : h + 1])
            weights = jnp.where(seen(place_ref, row_ref, lo), weights, 0.0)
            weight_grad = dot(grad, v, NT)
            centre = jnp.sum(weights * weight_grad, axis=1, keepdims=True)
            score_grad = (weights * (weight_grad - centre)).astype(LOW)
            hat_ref[lo : lo + TILE, at] = dot(score_grad, k) * HEAD**-0.5
            value_part = dot(weights.astype(LOW), grad, TN)
            key_part = dot(score_grad, q, TN)
            if lo == 0:
                dv_ref[...] = value_part
                dk_ref[...] = key_part
            else:
                dv_ref[...] += value_part
                dk_ref[...] += key_part
        value_ref[:, at] = dv_ref[...].astype(LOW)
        q_grad = turn_back(hat_ref[:, at], cosines, sines)
        k_grad = turn_back(dk_ref[...] * HEAD**-0.5, cosines, sines)
        q, k = qkv_ref[:, at], qkv_ref[:, k_at]
        part_ref[0:1, at] = jnp.sum(q_grad * q * rms_ref[:, 0:1], axis=0, keepdims=True)
        part_ref[1:2, at] = jnp.sum(k_grad * k * rms_ref[:, 1:2], axis=0, keepdims=True)
        hat_ref[:, at] = q_grad * gain_ref[0:1, at]
        hat_ref[:, k_at] = k_grad * gain_ref[1:2, at]
    dots_ref[...] = ones_dot(hat_ref[:, :256] * qkv_ref[:, :256])
    dots_ref[1:2, :] = ones_dot(hat_ref[:, 256:] * qkv_ref[:, 256:512])[0:1, :]


def qkv_back_kernel(hat_ref, qkv_ref, rms_ref, dots_ref, value_ref, out_ref):
    dots = dots_ref[...].T
    for i in range(2):
        at = slice(i * 256, (i + 1) * 256)
        rms = rms_ref[:, i : i + 1]
        coefficient = rms * rms * rms * dots[:, i : i + 1] * (1.0 / D)
        out_ref[:, at] = (rms * hat_ref[:, at] - qkv_ref[:, at] * coefficient).astype(LOW)
    out_ref[:, 512:] = value_ref[...]


def widen_kernel(table, rows_ref, out_ref):
    for i in range(8):
        block = pl.ds(pl.multiple_of(table[i] * BLOCK, BLOCK), BLOCK)
        out_ref[i * BLOCK : (i + 1) * BLOCK, :] = rows_ref[block, :].astype(F32)


def call(kernel, shapes, *args, scratch=(), scalars=0):
    return pl.pallas_call(
        kernel,
        in_specs=[
            pl.BlockSpec(memory_space=pltpu.SMEM if i < scalars else pltpu.VMEM)
            for i in range(len(args))
        ],
        out_shape=tuple(jax.ShapeDtypeStruct(shape, dtype) for shape, dtype in shapes),
        scratch_shapes=list(scratch),
        compiler_params=PARAMS,
        cost_estimate=FREE,
    )(*args)


def blocks_of(ref):
    return [slice(i * BLOCK, (i + 1) * BLOCK) for i in range(ref.shape[0] // BLOCK)]


def hidden_kernel(b0, b1, b2, b3, states_ref, gain_ref, low_ref, rms_ref):
    for at, ref in zip(blocks_of(low_ref), (b0, b1, b2, b3)):
        branch = ref[...].astype(F32)
        rms = lax.rsqrt(jnp.mean(branch * branch, axis=1, keepdims=True) + EPSILON)
        hidden = states_ref[at, :].astype(F32) + gain_ref[...] * branch * rms
        low_ref[at, :] = hidden.astype(LOW)
        rms_ref[at, :] = rms


def back_of(upstream, branch, rms, gain):
    part = jnp.sum(upstream * branch * rms, axis=0, keepdims=True)
    scaled = upstream * gain
    inner = jnp.sum(scaled * branch, axis=1, keepdims=True)
    return rms * scaled - branch * (rms * rms * rms * inner * (1.0 / D)), part


def ffn_back_kernel(b0, b1, b2, b3, upstream_ref, gain_ref, back_ref, rms_ref, part_ref):
    for i, (at, ref) in enumerate(zip(blocks_of(back_ref), (b0, b1, b2, b3))):
        branch = ref[...].astype(F32)
        rms = lax.rsqrt(jnp.mean(branch * branch, axis=1, keepdims=True) + EPSILON)
        back, part = back_of(upstream_ref[at, :].astype(F32), branch, rms, gain_ref[...])
        back_ref[at, :] = back.astype(LOW)
        rms_ref[at, :] = rms
        part_ref[...] = part if i == 0 else part_ref[...] + part


def attn_back_kernel(
    g0, g1, g2, g3, b0, b1, b2, b3, upstream_ref, rms_ref, gain_ref, back_ref, part_ref
):
    pairs = zip(blocks_of(back_ref), (g0, g1, g2, g3), (b0, b1, b2, b3))
    for i, (at, grad_ref, ref) in enumerate(pairs):
        grad = grad_ref[...].astype(F32) + upstream_ref[at, :].astype(F32)
        back, part = back_of(grad, ref[...].astype(F32), rms_ref[at, :], gain_ref[...])
        back_ref[at, :] = back.astype(LOW)
        part_ref[...] = part if i == 0 else part_ref[...] + part


def out_kernel(
    core_ref, a0, a1, a2, a3, b0, b1, b2, b3, states_ref, attn_rms_ref, ffn_rms_ref,
    attn_gain_ref, ffn_gain_ref, sent0_ref, sent1_ref,
):
    pairs = zip(blocks_of(states_ref), (a0, a1, a2, a3), (b0, b1, b2, b3))
    flip = core_ref[0] == 1
    for at, a_ref, b_ref in pairs:
        value = (
            states_ref[at, :].astype(F32)
            + attn_gain_ref[...] * a_ref[...].astype(F32) * attn_rms_ref[at, :]
            + ffn_gain_ref[...] * b_ref[...].astype(F32) * ffn_rms_ref[at, :]
        ).astype(LOW)
        near, far = value[:, :NEAR], value[:, NEAR:]
        sent0_ref[at, :] = jnp.where(flip, far, near)
        sent1_ref[at, :] = jnp.where(flip, near, far)


def shuffle(sent):
    return [
        lax.ppermute(
            sent[k],
            ("core", "xl"),
            [(c * 2 + s, s * 2 + (s ^ c ^ k)) for s in range(2) for c in range(2)],
        )
        for k in range(2)
    ]


def local(
    inputs, segments, w_query, w_key, w_value, w_mix, w_gate, w_up, w_down,
    attn_gain, ffn_gain, query_gain, key_gain, out_grad,
):
    at = Place()
    first = first_hop(inputs)
    near_qkv = cut_columns(at, (768, 256), w_query, w_key, w_value)
    far_qkv = [wrap_swap(near_qkv[0]), pair_swap(near_qkv[1])]
    near_mix = lax.dynamic_slice_in_dim(w_mix, at.c * 256, 256, 0)
    far_mix = pick(lax.all_gather(near_mix, "xl"), 1 - at.s)
    near_gate, near_up = cut_columns(at, (512, 512), w_gate), cut_columns(at, (512, 512), w_up)
    near_down = cut_rows(at, w_down)

    gains = jnp.concatenate([attn_gain, ffn_gain, query_gain, key_gain])
    their_gains = pair_swap(gains)
    attn_gains = jnp.concatenate([attn_gain, their_gains[:NEAR]])[None]
    ffn_gains = jnp.concatenate([ffn_gain, their_gains[NEAR:D]])[None]
    head_gains = jnp.where(at.home, gains[D:], their_gains[D:]).reshape(2, 256)

    segment_ids = jnp.where(at.home, segments, core_swap(segments))
    step_index = jnp.arange(SEQ, dtype=jnp.int32)
    earlier = jnp.concatenate([segment_ids[:1] - 1, segment_ids[:-1]])
    begins = lax.cummax(jnp.where(segment_ids != earlier, step_index, 0))
    begins = jnp.concatenate([pick(begins.reshape(8, BLOCK), at.rows[i]) for i in range(8)])
    index = (at.rows[:, None] * BLOCK + jnp.arange(BLOCK, dtype=jnp.int32)[None]).reshape(-1)
    frequency = ROPE_BASE ** (-2.0 * jnp.arange(HEAD // 2, dtype=F32) / HEAD)
    angles = (index - begins).astype(F32)[:, None] * frequency
    cosines, sines = jnp.cos(angles), jnp.sin(angles)
    cosines = jnp.concatenate([cosines, cosines], axis=1)
    sines = jnp.concatenate([-sines, sines], axis=1)
    tables = (cosines, sines, jnp.stack([index, begins], axis=1), index[None])

    states = to_sequence(at, *second_hop(at, inputs, first), at.rows)
    states, far_qkv = lax.optimization_barrier((states, far_qkv))
    qkv_blocks = [*near_qkv, *far_qkv]
    far_gate = fetch(*after(near_gate, far_qkv))
    qkv, squares = project(states, qkv_blocks)
    squares = all_stats(squares)
    mixed, low, totals, head_rms = call(
        attend_kernel,
        [((SEQ, 256), LOW), ((SEQ, SEQ), LOW), ((SEQ, 2), F32), ((SEQ, 8), F32)],
        qkv, squares, head_gains, *tables,
    )
    came = core_swap(mix(mixed[OWN:], near_mix, far_mix)[0])
    mix_parts = mix(mixed[:OWN], near_mix, far_mix, came)
    mix_parts, far_gate = lax.optimization_barrier((mix_parts, far_gate))
    far_up = fetch(*after(near_up, mix_parts))
    attn_sum = scatter_z(mix_parts).astype(LOW)
    attn_sum, far_up = lax.optimization_barrier((attn_sum, far_up))
    far_down = fetch(*after(near_down, attn_sum))
    attn_blocks = gather_z(attn_sum)
    own_states = states[:OWN]
    attn_blocks, far_down, own_states = lax.optimization_barrier(
        (attn_blocks, far_down, own_states)
    )
    hidden_own, attn_rms = call(
        hidden_kernel,
        [((OWN, D), LOW), ((OWN, 1), F32)],
        *attn_blocks, own_states, attn_gains,
    )
    hidden_other = core_swap(hidden_own)

    gates, ups, downs = [*near_gate, *far_gate], [*near_up, *far_up], [*near_down, *far_down]
    gate_own, up_own, units_own = units_of(hidden_own, gates, ups)
    gate_other, up_other, units_other = units_of(hidden_other, gates, ups)
    came = core_swap(down(units_other, downs)[0])
    ffn_parts = down(units_own, downs, came)
    grad_first = first_hop(after(out_grad, ffn_parts))
    ffn_sum = scatter_z(ffn_parts).astype(LOW)
    ffn_sum, grad_first = lax.optimization_barrier((ffn_sum, grad_first))
    ffn_blocks = gather_z(ffn_sum)
    upstream = to_sequence(at, *second_hop(at, out_grad, grad_first), at.rows[:RING])
    ffn_blocks, upstream = lax.optimization_barrier((ffn_blocks, upstream))
    branch_own, ffn_rms, ffn_gain_part = call(
        ffn_back_kernel,
        [((OWN, D), LOW), ((OWN, 1), F32), ((1, D), F32)],
        *ffn_blocks, upstream, ffn_gains,
    )
    branch_other = core_swap(branch_own)
    gate_back_own, up_back_own = units_back(branch_own, downs, gate_own, up_own)
    gate_back_other, up_back_other = units_back(branch_other, downs, gate_other, up_other)
    came = core_swap(pair_down(gate_back_other, up_back_other, gates, ups)[0])
    pair_parts = pair_down(gate_back_own, up_back_own, gates, ups, came)

    hidden_sum = scatter_z(pair_parts)
    hidden_rows = hidden_sum + upstream[:BLOCK].astype(F32)
    branch_own, hidden_own, pair_parts = lax.optimization_barrier(
        (branch_own, hidden_own, pair_parts)
    )
    down_parts = weight_grad(at, [(branch_own, branch_other, units_own, units_other)])
    down_sum = plane_sum(down_parts, (1, 3))
    gate_parts = weight_grad(at, [(hidden_own, hidden_other, gate_back_own, gate_back_other)])
    up_parts = weight_grad(at, [(hidden_own, hidden_other, up_back_own, up_back_other)])
    hidden_sum, down_sum, gate_parts, up_parts = lax.optimization_barrier(
        (hidden_sum.astype(LOW), down_sum, gate_parts, up_parts)
    )

    hidden_blocks = gather_z(hidden_sum)
    down_sum = plane_sum(down_parts, (2,), down_sum, hidden_sum)
    gate_sum = plane_sum(gate_parts, (1,), None, hidden_sum)
    sent = call(
        out_kernel,
        [((OWN, NEAR), LOW)] * 2,
        after(at.c.reshape(1).astype(jnp.int32), hidden_sum), *attn_blocks, *ffn_blocks,
        own_states, attn_rms, ffn_rms, attn_gains, ffn_gains,
        scalars=1,
    )
    hidden_blocks, down_sum, gate_sum, sent = lax.optimization_barrier(
        (hidden_blocks, down_sum, gate_sum, sent)
    )
    mix_own, attn_gain_part = call(
        attn_back_kernel,
        [((OWN, D), LOW), ((1, D), F32)],
        *hidden_blocks, *attn_blocks, upstream, attn_rms, attn_gains,
    )
    mix_other = core_swap(mix_own)

    gate_sum = plane_sum(gate_parts, (2, 3), gate_sum, hidden_blocks)
    shuffled = shuffle(sent)
    hat, value_back, dots, head_parts = call(
        attend_back_kernel,
        [((SEQ, 512), F32), ((SEQ, 256), LOW), ((8, SEQ), F32), ((2, 256), F32)],
        qkv, head_rms, head_gains, *tables, low, totals, mix_own, mix_other, near_mix, far_mix,
        scratch=[pltpu.VMEM((SEQ, HEAD), F32)] * 2 + [pltpu.VMEM((SEQ, 256), LOW)],
    )
    hat, gate_sum, shuffled = lax.optimization_barrier((hat, gate_sum, shuffled))
    up_sum = plane_sum(up_parts, (1, 3), None, hat)
    down_rows = plane_second(after(down_sum, hat))
    (qkv_back,) = call(
        qkv_back_kernel, [((SEQ, SEQ), LOW)], hat, qkv, head_rms, all_stats(dots), value_back
    )
    came = core_swap(qkv_down(qkv_back[OWN:], qkv_blocks)[0])
    input_parts = qkv_down(qkv_back[:OWN], qkv_blocks, came)
    input_parts, up_sum, down_rows, mix_own, qkv_back = lax.optimization_barrier(
        (input_parts, up_sum, down_rows, mix_own, qkv_back)
    )

    up_sum = plane_sum(up_parts, (2,), up_sum, input_parts)
    gate_rows = plane_second(after(gate_sum, input_parts))
    heads = head_parts.reshape(2, 8, 32).transpose(1, 0, 2).reshape(8, 64)
    heads = jnp.pad(heads, ((0, 0), (0, 64)))
    gain_columns = jnp.stack(
        [attn_gain_part[0], ffn_gain_part[0], jnp.concatenate([heads, heads]).reshape(D)], axis=1
    )
    gain_columns = jnp.pad(gain_columns.astype(LOW), ((0, 0), (0, 125)))
    attn_parts = weight_grad(
        at,
        [
            (own_states, states[OWN:], qkv_back[:OWN], qkv_back[OWN:]),
            (mix_own, mix_other, mixed[:OWN], mixed[OWN:]),
        ],
        gain_columns,
    )
    attn_grad = plane_sum(attn_parts, (1,))
    input_low = (scatter_z(input_parts) + hidden_rows).astype(LOW)
    input_low, attn_grad, up_sum, gate_rows = lax.optimization_barrier(
        (input_low, attn_grad, up_sum, gate_rows)
    )

    attn_grad = plane_sum(attn_parts, (2, 3), attn_grad, input_low)
    near, far = input_low[:, :NEAR], input_low[:, NEAR:]
    flip = at.c == 1
    input_rows = shuffle([jnp.where(flip, far, near), jnp.where(flip, near, far)])
    input_rows = gather_z(jnp.concatenate(input_rows))

    steps = jnp.arange(8, dtype=jnp.int32)
    from_part = at.s ^ at.c ^ (steps // RING)
    from_z = (at.z - steps) % RING
    block_out = order_rows(at, shuffled, from_z, from_part)
    (input_grad,) = call(
        widen_kernel, [((SEQ, NEAR), F32)],
        (from_z * 2 + from_part).astype(jnp.int32), jnp.concatenate(input_rows),
        scalars=1,
    )

    down_out = jnp.concatenate(share_cores(at, down_rows), axis=1).T
    gate_out = jnp.concatenate(share_cores(at, gate_rows), axis=1)
    up_rows = plane_second(after(up_sum, input_low))
    up_out = jnp.concatenate(share_cores(at, up_rows), axis=1)
    attn_rows = plane_second(attn_grad)
    attn0, attn1 = share_cores(at, attn_rows)
    query, key, value, mix_out = (
        jnp.concatenate([attn0[:, i : i + 256], attn1[:, i : i + 256]], axis=1)
        for i in range(0, 1024, 256)
    )
    width = attn0[:, 1024:1026] + attn1[:, 1024:1026]
    head_column = attn_rows[:, 1026].astype(LOW)
    their_column = core_swap(head_column)
    head_column = jnp.where(at.home, head_column, their_column).astype(F32)
    head_column = lax.dynamic_slice_in_dim(head_column[:64].reshape(2, 32), at.c * 16, 16, 1)

    return (
        block_out, input_grad, query, key, value, mix_out.T, gate_out, up_out, down_out,
        width[:, 0], width[:, 1], head_column[0], head_column[1],
    )


def solution(mesh):
    fine = Mesh(mesh.devices.reshape(4, 2, 2, 4, 2), ("y", "xh", "core", "z", "xl"))
    dp = ("y", "xh", "core")
    row, col = "z", "xl"
    return jax.shard_map(
        local,
        mesh=fine,
        in_specs=(
            P(dp, col), P(dp), P(col, row), P(col, row), P(col, row), P(row, col),
            P(col, row), P(col, row), P(row, col), P(col), P(col), P((row, col)),
            P((row, col)), P(dp, col),
        ),
        out_specs=(
            P(dp, col), P(dp, col),
            P((col,) + dp, row), P((col,) + dp, row), P((col,) + dp, row), P(row, (col,) + dp),
            P((col,) + dp, row), P((col,) + dp, row), P(row, (col,) + dp),
            P((col,) + dp), P((col,) + dp), P((row, col) + dp), P((row, col) + dp),
        ),
        check_vma=False,
    )
```

```python
import functools

import jax
import jax.numpy as jnp
from jax import lax
from jax.experimental import pallas as pl
from jax.experimental.pallas import tpu as pltpu
from jax.sharding import Mesh, PartitionSpec as P

D = 2048
HEAD = 128
SEQ = 768
NEAR = D // 2
OWN = SEQ // 2
RING = 4
BLOCK = SEQ // 8
EPSILON = 1e-06
ROPE_BASE = 500000.0
MASKED = -1e30
LOW = jnp.bfloat16
F32 = jnp.float32
FREE = pl.CostEstimate(flops=0, bytes_accessed=0, transcendentals=0)
PARAMS = pltpu.CompilerParams(vmem_limit_bytes=24 * 1024 * 1024)
EARLY = pltpu.CompilerParams(vmem_limit_bytes=60 * 1024 * 1024)


def dot(a, b, dims=((1,), (0,))):
    return lax.dot_general(a, b, (dims, ((), ())), preferred_element_type=F32)


NT = ((1,), (1,))
TN = ((0,), (0,))


def after(value, *earlier):
    return lax.optimization_barrier((value, earlier))[0]


def ring_shift(a, axes, step):
    return lax.ppermute(a, axes, [(i, (i + step) % RING) for i in range(RING)])


def z_shift(a, step):
    return ring_shift(a, "z", step)


def plane_shift(a, step, swapped):
    pairs = []
    for y in range(4):
        for x in range(4):
            for c in range(2):
                there = ((y + step) % 4, x) if (c == 0) != swapped else (y, (x + step) % 4)
                xh, xl = x // 2, x % 2
                source = ((y * 2 + xh) * 2 + c) * 2 + xl
                pairs.append((source, ((there[0] * 2 + there[1] // 2) * 2 + c) * 2 + there[1] % 2))
    return lax.ppermute(a, ("y", "xh", "core", "xl"), pairs)


def core_swap(a):
    return lax.ppermute(a, "core", [(0, 1), (1, 0)])


def pair_swap(a):
    return lax.ppermute(a, "xl", [(0, 1), (1, 0)])


def wrap_swap(a):
    return lax.ppermute(a, ("xh", "xl"), [(0, 3), (3, 0), (1, 2), (2, 1)])


def pick(blocks, index, axis=0):
    return lax.dynamic_index_in_dim(blocks, index, axis, keepdims=False)


class Place:
    def __init__(self):
        self.s = lax.axis_index("xl")
        self.xh = lax.axis_index("xh")
        self.x = self.xh * 2 + self.s
        self.y = lax.axis_index("y")
        self.c = lax.axis_index("core")
        self.z = lax.axis_index("z")
        self.home = self.c == self.s
        steps = jnp.arange(RING, dtype=jnp.int32)
        self.back = (self.z - steps) % RING
        self.rows = jnp.concatenate([self.c * 4 + self.back, (1 - self.c) * 4 + self.back])
        first, second = steps[:, None], steps[None, :]
        dx = jnp.where(self.c == 0, second, first)
        dy = jnp.where(self.c == 0, first, second)
        self.columns = (
            (dx % 2) * 8 + ((self.y + dy) % 4) * 2 + ((self.x + dx) % 4) // 2
        ).reshape(-1)
        y, x = first, second
        self.plain = (((x % 2) ^ self.s) * 8 + y * 2 + x // 2).reshape(-1)


def place_kernel(plan, sources, table, *refs):
    ins, outs, sems = refs[:sources], refs[sources:-1], refs[-1]
    copies = []
    for i, (source, there) in enumerate(plan(table, ins, outs)):
        copies.append(pltpu.make_async_copy(source, there, sems.at[i]))
        copies[-1].start()
    for copy in copies:
        copy.wait()


def place(plan, count, shapes, table, *sources, params=PARAMS):
    return pl.pallas_call(
        functools.partial(place_kernel, plan, len(sources)),
        in_specs=[pl.BlockSpec(memory_space=pltpu.SMEM)]
        + [pl.BlockSpec(memory_space=pltpu.HBM)] * len(sources),
        out_specs=tuple(pl.BlockSpec(memory_space=pltpu.VMEM) for _ in shapes),
        out_shape=tuple(jax.ShapeDtypeStruct(shape, LOW) for shape in shapes),
        scratch_shapes=[pltpu.SemaphoreType.DMA((count,))],
        compiler_params=params,
        cost_estimate=FREE,
    )(jnp.stack(table).astype(jnp.int32), *sources)


def at_block(index, size):
    return pl.ds(pl.multiple_of(index * size, size), size)


def first_hop(a):
    return lax.ppermute(a, ("core", "xl"), [(0, 2), (3, 1), (2, 3), (1, 0)])


def second_hop(first):
    return lax.ppermute(first, ("core", "xl"), [(0, 2), (3, 1)])


def sequence_kernel(count, table, a_ref, first_ref, second_ref, out_ref, sems):
    def move(near, far):
        copies = []
        for i in range(count):
            block = at_block(table[i], BLOCK)
            there = pl.ds(i * BLOCK, BLOCK)
            for source, lo in ((near.at[block], 0), (far.at[block], NEAR)):
                copies.append(
                    pltpu.make_async_copy(
                        source, out_ref.at[there, pl.ds(lo, NEAR)], sems.at[len(copies)]
                    )
                )
        for copy in copies:
            copy.start()
        for copy in copies:
            copy.wait()

    pl.when(table[count] == 1)(functools.partial(move, a_ref, first_ref))
    pl.when(table[count] == 0)(functools.partial(move, first_ref, second_ref))


def to_sequence(at, a, first, second, count=8):
    table = jnp.concatenate([at.rows[:count], at.home[None].astype(jnp.int32)])
    return pl.pallas_call(
        functools.partial(sequence_kernel, count),
        in_specs=[pl.BlockSpec(memory_space=pltpu.SMEM)]
        + [pl.BlockSpec(memory_space=pltpu.HBM)] * 3,
        out_specs=pl.BlockSpec(memory_space=pltpu.VMEM),
        out_shape=jax.ShapeDtypeStruct((count * BLOCK, D), LOW),
        scratch_shapes=[pltpu.SemaphoreType.DMA((2 * count,))],
        compiler_params=PARAMS,
        cost_estimate=FREE,
    )(table.astype(jnp.int32), a, first, second)


def order_rows(at, sources, index, which):
    joined = jnp.concatenate(sources) if len(sources) > 1 else sources[0]
    rows = sources[0].shape[0] // BLOCK

    def plan(table, ins, outs):
        return [
            (ins[0].at[at_block(table[i], BLOCK)], outs[0].at[pl.ds(i * BLOCK, BLOCK)])
            for i in range(8)
        ]

    table = index + rows * which if len(sources) > 1 else index * 2 + which
    return place(plan, 8, [(SEQ, joined.shape[1])], list(table), joined)[0]


def cut_columns(at, heights, *weights):
    width = weights[0].shape[1] // 2
    starts = [sum(heights[:i]) for i in range(len(heights))]

    def plan(table, ins, outs):
        return [
            (
                ref.at[pl.ds(start, height), at_block(table[0], width)],
                out.at[:, pl.ds(width * i, width)],
            )
            for i, ref in enumerate(ins)
            for start, height, out in zip(starts, heights, outs)
        ]

    shapes = [(height, width * len(weights)) for height in heights]
    return place(plan, len(heights) * len(weights), shapes, [at.c], *weights, params=EARLY)


PIECES = (
    (("gate", 0),), (("gate", 1),),
    (("gate", 2), ("up", 0)), (("gate", 3), ("up", 1)),
    (("up", 2), ("down", 0)), (("up", 3), ("down", 1)),
    (("down", 2),), (("down", 3),),
)
PART = 256


def cut_pieces(at, w_gate, w_up, w_down):
    def plan(table, ins, outs):
        named = dict(zip(("gate", "up", "down"), ins))
        copies = []
        for out, piece in zip(outs, PIECES):
            for i, (name, part) in enumerate(piece):
                if name == "down":
                    rows = pl.ds(pl.multiple_of(table[0] * NEAR + PART * part, PART), PART)
                    source = named[name].at[rows]
                else:
                    source = named[name].at[pl.ds(PART * part, PART), at_block(table[0], NEAR)]
                copies.append((source, out.at[pl.ds(PART * i, PART)]))
        return copies

    shapes = [(PART * len(piece), NEAR) for piece in PIECES]
    return place(plan, 12, shapes, [at.c], w_gate, w_up, w_down, params=EARLY)


def pieces_with(name):
    return [k for k, piece in enumerate(PIECES) if name in dict(piece)]


def views(name, refs):
    out = []
    for ref, k in zip(refs, pieces_with(name)):
        for i, (found, _) in enumerate(PIECES[k]):
            if found == name:
                out.append(ref.at[pl.ds(PART * i, PART)])
    return out


def join_columns(parts):
    starts = [sum(part.shape[1] for part in parts[:i]) for i in range(len(parts) + 1)]

    def plan(table, ins, outs):
        return [
            (ref, outs[0].at[:, pl.ds(starts[i], parts[i].shape[1])]) for i, ref in enumerate(ins)
        ]

    return place(plan, len(parts), [(D, starts[-1])], [0], *parts)[0]


def fetch(first, second):
    return pair_swap(first), wrap_swap(second)


def scatter_z(parts):
    total = parts[0]
    for i in range(1, RING):
        total = total + z_shift(parts[i], -i).astype(F32)
    return total


def gather_z(rows):
    return [rows] + [z_shift(rows, i) for i in range(1, RING)]


def all_stats(pair):
    theirs = core_swap(pair)
    pair = pair + jnp.concatenate([theirs[:, OWN:], theirs[:, :OWN]], axis=1)
    total = pair
    for i in range(1, RING):
        came, cut = z_shift(pair, i), OWN - i * BLOCK
        total = total + jnp.concatenate(
            [came[:, cut:OWN], came[:, :cut], came[:, OWN + cut :], came[:, OWN : OWN + cut]],
            axis=1,
        )
    return total


def plane_sum(own, came):
    total = own.astype(F32) + came[0].astype(F32) + came[1].astype(F32) + came[2].astype(F32)
    total = lax.optimization_barrier(total.astype(LOW))
    height = own.shape[0] // RING
    return [total[height * i : height * (i + 1)] for i in range(RING)]


def share_kernel(core, p0, p1, p2, p3, own_ref, sent_ref):
    total = p0[...].astype(F32) + p1[...].astype(F32) + p2[...].astype(F32) + p3[...].astype(F32)
    flip = core[0] == 1
    own_ref[:64, :] = jnp.where(flip, total[64:128, :], total[:64, :])
    sent_ref[:64, :] = jnp.where(flip, total[:64, :], total[64:128, :]).astype(LOW)
    if total.shape[0] > 128:
        own_ref[64:, :] = total[128:, :]
        sent_ref[64:, :] = total[128:, :].astype(LOW)


def share_cores(at, own, came):
    shape = (own.shape[0] - 64, own.shape[1])
    core = at.c.reshape(1).astype(jnp.int32)
    own, sent = call(share_kernel, [(shape, F32), (shape, LOW)], core, own, *came, scalars=1)
    came = core_swap(sent).astype(F32)
    first = at.c == 0
    return jnp.where(first, own, came), jnp.where(first, came, own)


def call(kernel, shapes, *args, scratch=(), scalars=0):
    return pl.pallas_call(
        kernel,
        in_specs=[
            pl.BlockSpec(memory_space=pltpu.SMEM if i < scalars else pltpu.VMEM)
            for i in range(len(args))
        ],
        out_shape=tuple(jax.ShapeDtypeStruct(shape, dtype) for shape, dtype in shapes),
        scratch_shapes=list(scratch),
        compiler_params=PARAMS,
        cost_estimate=FREE,
    )(*args)


def row_dot(rows, refs, at):
    value = 0.0
    start = 0
    for ref in refs:
        height = ref.shape[0]
        value += dot(rows[:, start : start + height], ref[:, at])
        start += height
    return value


def strips(width, size):
    return [slice(i, i + size) for i in range(0, width, size)]


def as_rows(first, second):
    return jnp.concatenate([first, second, jnp.zeros((SEQ, 6), F32)], axis=1).T


def qkv_kernel(states_ref, *refs):
    *blocks, qkv_ref, sums_ref = refs
    sums = []
    for at in strips(SEQ, 256):
        value = row_dot(states_ref, blocks, at)
        qkv_ref[:, at] = value
        sums.append(jnp.sum(value * value, axis=1, keepdims=True))
    sums_ref[...] = as_rows(*sums[:2])


def product_kernel(body, *refs):
    *refs, out_ref = refs
    for at, value in body(refs):
        out_ref[:, at] = value.astype(out_ref.dtype)


def product(body, dtype, *args):
    return call(functools.partial(product_kernel, body), [((OWN, D), dtype)], *args)[0]


def half_rows(ref, half):
    return ref[OWN * half : OWN * (half + 1), :]


def mix(left, half, near, far, dtype):
    def body(refs):
        left, near, far = refs
        left = half_rows(left, half)
        for at in strips(NEAR, 512):
            yield at, dot(left, near[:, at])
            yield slice(NEAR + at.start, NEAR + at.stop), dot(left, far[:, at])

    return product(body, dtype, left, near, far)


def down(units, pieces, dtype):
    count = len(pieces) // 2

    def body(refs):
        units, *w = refs
        for i in range(2):
            blocks = views("down", w[count * i : count * (i + 1)])
            for at in strips(NEAR, 512):
                yield slice(NEAR * i + at.start, NEAR * i + at.stop), row_dot(units, blocks, at)

    return product(body, dtype, units, *pieces)


def pair_down(gate_back, up_back, gates, ups, dtype):
    def body(refs):
        gate_back, up_back, *w = refs
        for i in range(2):
            n, m = len(gates) // 2, len(ups) // 2
            gate = views("gate", w[n * i : n * (i + 1)])
            up = views("up", w[2 * n + m * i : 2 * n + m * (i + 1)])
            for k in range(4):
                value = dot(gate_back[...], gate[k][...], NT) + dot(up_back[...], up[k][...], NT)
                yield slice(NEAR * i + PART * k, NEAR * i + PART * (k + 1)), value

    return product(body, dtype, gate_back, up_back, *gates, *ups)


def qkv_down(back, half, blocks, dtype):
    def body(refs):
        back, *w = refs
        back = half_rows(back, half)
        start = 0
        for ref in w:
            for at in strips(ref.shape[0], 256):
                yield slice(start + at.start, start + at.stop), dot(back, ref[at, :], NT)
            start += ref.shape[0]

    return product(body, dtype, back, *blocks)


def settle_kernel(own_ref, came_ref, *outs):
    for i, ref in enumerate(outs):
        at = slice(i * BLOCK, (i + 1) * BLOCK)
        ref[...] = (own_ref[at, :] + came_ref[at, :].astype(F32)).astype(ref.dtype)


def settle(own, came):
    return call(
        settle_kernel, [((BLOCK, D), F32)] + [((BLOCK, D), LOW)] * 3, own, came
    )


def units_kernel(n, m, rows_ref, *refs):
    gate_ref, up_ref, units_ref = refs[-3:]
    gates = views("gate", refs[:n]) + views("gate", refs[n : 2 * n])
    ups = views("up", refs[2 * n : 2 * n + m]) + views("up", refs[2 * n + m : 2 * n + 2 * m])
    for at in strips(1024, 512):
        gate, up = row_dot(rows_ref, gates, at), row_dot(rows_ref, ups, at)
        gate_ref[:, at] = gate.astype(LOW)
        up_ref[:, at] = up.astype(LOW)
        units_ref[:, at] = (gate * jax.nn.sigmoid(gate) * up).astype(LOW)


def units_of(rows, gates, ups):
    kernel = functools.partial(units_kernel, len(gates) // 2, len(ups) // 2)
    return call(kernel, [((OWN, 1024), LOW)] * 3, rows, *gates, *ups)


def units_back_kernel(branch_ref, *refs):
    *w, gate_ref, up_ref, gate_back_ref, up_back_ref = refs
    count = len(w) // 2
    near, far = views("down", w[:count]), views("down", w[count:])
    for k in range(4):
        at = slice(PART * k, PART * (k + 1))
        grad = dot(branch_ref[:, :NEAR], near[k][...], NT)
        grad += dot(branch_ref[:, NEAR:], far[k][...], NT)
        gate, up = gate_ref[:, at].astype(F32), up_ref[:, at].astype(F32)
        sigmoid = jax.nn.sigmoid(gate)
        gate_back_ref[:, at] = (grad * up * sigmoid * (1.0 + gate * (1.0 - sigmoid))).astype(LOW)
        up_back_ref[:, at] = (grad * gate * sigmoid).astype(LOW)


def units_back(branch, pieces, gate, up):
    return call(units_back_kernel, [((OWN, 1024), LOW)] * 2, branch, *pieces, gate, up)


def grad_kernel(plan, count, extras, *refs):
    table, ins = refs[0], refs[1 : 1 + count]
    extra, outs = refs[1 + count : 1 + count + extras], refs[1 + count + extras :]
    for d in range(RING):
        blocks = [table[4 * d + e] for e in range(RING)]
        places = [at_block(block, 128) for block in blocks]
        start = 0
        for lo, width, terms in plan:
            value = 0.0
            for left, right, row in terms:
                left, right = ins[left], ins[right]
                chosen = jnp.concatenate([left[:, place] for place in places], axis=1)
                value += dot(chosen, right[row : row + left.shape[0], lo : lo + width], TN)
            value = value.astype(LOW)
            at = slice(start, start + width)
            if len(outs) == 1:
                outs[0][512 * d : 512 * (d + 1), at] = value
            elif not extras:
                outs[d][:, at] = value
            else:
                for e in range(RING):
                    outs[d][144 * e : 144 * e + 128, at] = value[128 * e : 128 * (e + 1)]
            start += width
        if extras:
            attn_ref, ffn_ref, heads_ref = extra
            for e in range(RING):
                block = lax.rem(blocks[e], 8)
                rows = [attn_ref[0:1, places[e]], ffn_ref[0:1, places[e]]]
                rows += [heads_ref[pl.ds(block + 8 * i, 1), :] for i in range(2)]
                rows = jnp.concatenate([*rows, jnp.zeros((12, 128), F32)])
                at = slice(144 * e + 128, 144 * (e + 1))
                outs[d][at, :128] = rows.astype(LOW)
                outs[d][at, 128:] = jnp.zeros((16, start - 128), LOW)


def weight_grad(table, arrays, plan, extra=(), joined=False):
    width = sum(span[1] for span in plan)
    height = 576 if extra else 512
    shapes = [(D, width)] if joined else [(height, width)] * RING
    kernel = functools.partial(grad_kernel, plan, len(arrays), len(extra))
    outs = [(shape, LOW) for shape in shapes]
    return call(kernel, outs, table.astype(jnp.int32), *arrays, *extra, scalars=1)


def turn(v, cosines, sines):
    return v * cosines + pltpu.roll(v, HEAD // 2, 1) * sines


def turn_back(v, cosines, sines):
    return v * cosines - pltpu.roll(v, HEAD // 2, 1) * sines


TILE = 256


def seen(table_ref, row_ref, lo):
    here = table_ref[lo : lo + TILE, 2 * HEAD : 3 * HEAD]
    there = row_ref[0:1, :]
    return (there <= here[:, 0:1]) & (there >= here[:, 1:2])


def attend_kernel(
    qkv_ref, sums_ref, gain_ref, table_ref, row_ref, mixed_ref, low_ref, scale_ref
):
    cosines, sines = table_ref[:, :HEAD], table_ref[:, HEAD : 2 * HEAD]
    scale_ref[...] = lax.rsqrt(sums_ref[...] * (1.0 / D) + EPSILON).T
    for h in range(2):
        at = slice(h * HEAD, (h + 1) * HEAD)
        k_at = slice(256 + h * HEAD, 256 + (h + 1) * HEAD)
        q = qkv_ref[:, at] * scale_ref[:, 0:1] * gain_ref[0:1, at]
        k = qkv_ref[:, k_at] * scale_ref[:, 1:2] * gain_ref[1:2, at]
        low_ref[:, at] = turn(q, cosines, sines).astype(LOW)
        k = turn(k, cosines, sines).astype(LOW)
        v = qkv_ref[:, 512 + h * HEAD : 512 + (h + 1) * HEAD].astype(LOW)
        low_ref[:, k_at] = k
        low_ref[:, 512 + h * HEAD : 512 + (h + 1) * HEAD] = v
        for lo in range(0, SEQ, TILE):
            q = low_ref[lo : lo + TILE, at]
            scores = dot(q, k, NT) * HEAD**-0.5
            scores = jnp.where(seen(table_ref, row_ref, lo), scores, MASKED)
            peak = jnp.max(scores, axis=1, keepdims=True)
            weights = jnp.exp(scores - peak)
            total = jnp.sum(weights, axis=1, keepdims=True)
            weights = (weights * (1.0 / total)).astype(LOW)
            mixed_ref[lo : lo + TILE, at] = dot(weights, v).astype(LOW)
            scale_ref[lo : lo + TILE, 2 + h : 3 + h] = peak + jnp.log(total)


def attend_back_kernel(
    qkv_ref, scale_ref, gain_ref, table_ref, row_ref, low_ref,
    own_ref, other_ref, near_ref, far_ref,
    hat_ref, value_ref, dots_ref, part_ref, dk_ref, dv_ref, grad_ref,
):
    cosines, sines = table_ref[:, :HEAD], table_ref[:, HEAD : 2 * HEAD]
    for i, ref in enumerate((own_ref, other_ref)):
        grad = dot(ref[:, :NEAR], near_ref[...], NT) + dot(ref[:, NEAR:], far_ref[...], NT)
        grad_ref[OWN * i : OWN * (i + 1), :] = grad.astype(LOW)
    for h in range(2):
        at = slice(h * HEAD, (h + 1) * HEAD)
        k_at = slice(256 + h * HEAD, 256 + (h + 1) * HEAD)
        k = low_ref[:, k_at]
        v = low_ref[:, 512 + h * HEAD : 512 + (h + 1) * HEAD]
        for lo in range(0, SEQ, TILE):
            q = low_ref[lo : lo + TILE, at]
            grad = grad_ref[lo : lo + TILE, at]
            scores = dot(q, k, NT) * HEAD**-0.5
            weights = jnp.exp(scores - scale_ref[lo : lo + TILE, 2 + h : 3 + h])
            weights = jnp.where(seen(table_ref, row_ref, lo), weights, 0.0)
            weight_grad = dot(grad, v, NT)
            centre = jnp.sum(weights * weight_grad, axis=1, keepdims=True)
            score_grad = (weights * (weight_grad - centre)).astype(LOW)
            hat_ref[lo : lo + TILE, at] = dot(score_grad, k) * HEAD**-0.5
            value_part = dot(weights.astype(LOW), grad, TN)
            key_part = dot(score_grad, q, TN)
            if lo == 0:
                dv_ref[...] = value_part
                dk_ref[...] = key_part
            else:
                dv_ref[...] += value_part
                dk_ref[...] += key_part
        value_ref[:, at] = dv_ref[...].astype(LOW)
        q_grad = turn_back(hat_ref[:, at], cosines, sines)
        k_grad = turn_back(dk_ref[...] * HEAD**-0.5, cosines, sines)
        q, k = qkv_ref[:, at], qkv_ref[:, k_at]
        part_ref[0:1, at] = jnp.sum(q_grad * q * scale_ref[:, 0:1], axis=0, keepdims=True)
        part_ref[1:2, at] = jnp.sum(k_grad * k * scale_ref[:, 1:2], axis=0, keepdims=True)
        hat_ref[:, at] = q_grad * gain_ref[0:1, at]
        hat_ref[:, k_at] = k_grad * gain_ref[1:2, at]
    dots_ref[...] = as_rows(
        jnp.sum(hat_ref[:, :256] * qkv_ref[:, :256], axis=1, keepdims=True),
        jnp.sum(hat_ref[:, 256:] * qkv_ref[:, 256:512], axis=1, keepdims=True),
    )


def qkv_back_kernel(hat_ref, qkv_ref, rms_ref, dots_ref, value_ref, out_ref):
    dots = dots_ref[...].T
    for i in range(2):
        at = slice(i * 256, (i + 1) * 256)
        rms = rms_ref[:, i : i + 1]
        coefficient = rms * rms * rms * dots[:, i : i + 1] * (1.0 / D)
        out_ref[:, at] = (rms * hat_ref[:, at] - qkv_ref[:, at] * coefficient).astype(LOW)
    out_ref[:, 512:] = value_ref[...]


def widen_kernel(table, rows_ref, out_ref):
    for i in range(8):
        block = pl.ds(pl.multiple_of(table[i] * BLOCK, BLOCK), BLOCK)
        out_ref[i * BLOCK : (i + 1) * BLOCK, :] = rows_ref[block, :].astype(F32)


def blocks_of(ref):
    return [slice(i * BLOCK, (i + 1) * BLOCK) for i in range(ref.shape[0] // BLOCK)]


def hidden_kernel(b0, b1, b2, b3, states_ref, gain_ref, low_ref, rms_ref):
    for at, ref in zip(blocks_of(low_ref), (b0, b1, b2, b3)):
        branch = ref[...].astype(F32)
        rms = lax.rsqrt(jnp.mean(branch * branch, axis=1, keepdims=True) + EPSILON)
        hidden = states_ref[at, :].astype(F32) + gain_ref[...] * branch * rms
        low_ref[at, :] = hidden.astype(LOW)
        rms_ref[at, :] = rms


def back_of(upstream, branch, rms, gain):
    part = jnp.sum(upstream * branch * rms, axis=0, keepdims=True)
    scaled = upstream * gain
    inner = jnp.sum(scaled * branch, axis=1, keepdims=True)
    return rms * scaled - branch * (rms * rms * rms * inner * (1.0 / D)), part


def ffn_back_kernel(b0, b1, b2, b3, upstream_ref, gain_ref, back_ref, rms_ref, part_ref):
    for i, (at, ref) in enumerate(zip(blocks_of(back_ref), (b0, b1, b2, b3))):
        branch = ref[...].astype(F32)
        rms = lax.rsqrt(jnp.mean(branch * branch, axis=1, keepdims=True) + EPSILON)
        back, part = back_of(upstream_ref[at, :].astype(F32), branch, rms, gain_ref[...])
        back_ref[at, :] = back.astype(LOW)
        rms_ref[at, :] = rms
        part_ref[...] = part if i == 0 else part_ref[...] + part


def attn_back_kernel(
    g0, g1, g2, g3, b0, b1, b2, b3, upstream_ref, rms_ref, gain_ref, back_ref, part_ref
):
    pairs = zip(blocks_of(back_ref), (g0, g1, g2, g3), (b0, b1, b2, b3))
    for i, (at, grad_ref, ref) in enumerate(pairs):
        grad = grad_ref[...].astype(F32) + upstream_ref[at, :].astype(F32)
        back, part = back_of(grad, ref[...].astype(F32), rms_ref[at, :], gain_ref[...])
        back_ref[at, :] = back.astype(LOW)
        part_ref[...] = part if i == 0 else part_ref[...] + part


def out_kernel(
    core_ref, a0, a1, a2, a3, b0, b1, b2, b3, states_ref, attn_rms_ref, ffn_rms_ref,
    attn_gain_ref, ffn_gain_ref, sent0_ref, sent1_ref,
):
    pairs = zip(blocks_of(states_ref), (a0, a1, a2, a3), (b0, b1, b2, b3))
    flip = core_ref[0] == 1
    for at, a_ref, b_ref in pairs:
        value = (
            states_ref[at, :].astype(F32)
            + attn_gain_ref[...] * a_ref[...].astype(F32) * attn_rms_ref[at, :]
            + ffn_gain_ref[...] * b_ref[...].astype(F32) * ffn_rms_ref[at, :]
        ).astype(LOW)
        near, far = value[:, :NEAR], value[:, NEAR:]
        sent0_ref[at, :] = jnp.where(flip, far, near)
        sent1_ref[at, :] = jnp.where(flip, near, far)


def shuffle(sent):
    out = []
    for k in range(2):
        perm = [(c * 2 + s, s * 2 + (s ^ c ^ k)) for s in range(2) for c in range(2)]
        out.append(lax.ppermute(sent[k], ("core", "xl"), [p for p in perm if p[0] != p[1]]))
    return out


def shuffled_of(at, sent, came):
    return [jnp.where((at.s == k) & (at.c == k), sent[k], came[k]) for k in range(2)]


def local(
    inputs, segments, w_query, w_key, w_value, w_mix, w_gate, w_up, w_down,
    attn_gain, ffn_gain, query_gain, key_gain, out_grad,
):
    at = Place()
    first = first_hop(inputs)
    near_qkv = cut_columns(at, (768, 256), w_query, w_key, w_value)
    far_qkv = [wrap_swap(near_qkv[0]), pair_swap(near_qkv[1])]
    near_mix = lax.dynamic_slice_in_dim(w_mix, at.c * 256, 256, 0)
    near = cut_pieces(at, after(w_gate, near_qkv), w_up, w_down)

    gains = jnp.concatenate([attn_gain, ffn_gain, query_gain, key_gain])
    their_gains = pair_swap(gains)
    attn_gains = jnp.concatenate([attn_gain, their_gains[:NEAR]])[None]
    ffn_gains = jnp.concatenate([ffn_gain, their_gains[NEAR:D]])[None]
    head_gains = jnp.where(at.home, gains[D:], their_gains[D:]).reshape(2, 256)

    segment_ids = jnp.where(at.home, segments, core_swap(segments))
    step_index = jnp.arange(SEQ, dtype=jnp.int32)
    earlier = jnp.concatenate([segment_ids[:1] - 1, segment_ids[:-1]])
    begins = lax.cummax(jnp.where(segment_ids != earlier, step_index, 0))
    chosen = at.rows[:, None, None] == jnp.arange(8, dtype=jnp.int32)[None, :, None]
    begins = jnp.sum(jnp.where(chosen, begins.reshape(1, 8, BLOCK), 0), axis=1).reshape(-1)
    index = (at.rows[:, None] * BLOCK + jnp.arange(BLOCK, dtype=jnp.int32)[None]).reshape(-1)
    frequency = ROPE_BASE ** (-2.0 * jnp.arange(HEAD // 2, dtype=F32) / HEAD)
    angles = (index - begins).astype(F32)[:, None] * frequency
    cosines, sines = jnp.cos(angles), jnp.sin(angles)
    place_columns = jnp.stack([index, begins], axis=1).astype(F32)
    table = jnp.concatenate(
        [cosines, cosines, -sines, sines, jnp.pad(place_columns, ((0, 0), (0, 126)))], axis=1
    )
    tables = (table, index[None].astype(F32))

    tables, head_gains, attn_gains, ffn_gains, at.columns, at.plain, at.rows, near, first = (
        lax.optimization_barrier(
            (tables, head_gains, attn_gains, ffn_gains, at.columns, at.plain, at.rows, near, first)
        )
    )
    states = to_sequence(at, inputs, first, second_hop(after(first, far_qkv)))
    states, far_qkv = lax.optimization_barrier((states, far_qkv))
    qkv_blocks = [*near_qkv, *far_qkv]
    qkv, squares = call(qkv_kernel, [((SEQ, SEQ), F32), ((8, SEQ), F32)], states, *qkv_blocks)
    far = fetch(*after(near[:2], far_qkv))
    both_mix = lax.all_gather(after(near_mix, far_qkv), "xl")
    squares = all_stats(squares)
    squares, far = lax.optimization_barrier((squares, far))
    far_mix = jnp.where(at.s == 0, both_mix[1], both_mix[0])
    mixed, low, scales = call(
        attend_kernel,
        [((SEQ, 256), LOW), ((SEQ, SEQ), LOW), ((SEQ, 8), F32)],
        qkv, squares, head_gains, *tables,
    )
    came = core_swap(mix(mixed, 1, near_mix, far_mix, LOW))
    mix_parts = settle(mix(mixed, 0, near_mix, far_mix, F32), came)
    mix_parts = lax.optimization_barrier(mix_parts)
    far = [*far, *fetch(*after(near[2:4], mix_parts))]
    attn_sum = scatter_z(mix_parts).astype(LOW)
    attn_sum, far = lax.optimization_barrier((attn_sum, far))
    far = [*far, *fetch(*after(near[4:6], attn_sum))]
    attn_blocks = gather_z(attn_sum)
    own_states = after(states, attn_sum)[:OWN]
    attn_blocks, far, own_states = lax.optimization_barrier((attn_blocks, far, own_states))
    far = [*far, *fetch(*after(near[6:], attn_blocks))]
    hidden_own, attn_rms = call(
        hidden_kernel,
        [((OWN, D), LOW), ((OWN, 1), F32)],
        *attn_blocks, own_states, attn_gains,
    )
    hidden_other = core_swap(hidden_own)

    gates, ups, downs = (
        [side[k] for side in (near, far) for k in pieces_with(name)]
        for name in ("gate", "up", "down")
    )
    gate_own, up_own, units_own = units_of(hidden_own, gates, ups)
    hidden_other = after(hidden_other, units_own)
    gate_other, up_other, units_other = units_of(hidden_other, gates, ups)
    came = core_swap(down(units_other, downs, LOW))
    ffn_parts = settle(down(after(units_own, units_other), downs, F32), came)
    ffn_parts = lax.optimization_barrier(ffn_parts)
    grad_first = first_hop(after(out_grad, ffn_parts))
    ffn_sum = scatter_z(ffn_parts).astype(LOW)
    ffn_sum, grad_first = lax.optimization_barrier((ffn_sum, grad_first))
    ffn_blocks = gather_z(ffn_sum)
    upstream = to_sequence(at, out_grad, grad_first, second_hop(grad_first), RING)
    ffn_blocks, upstream = lax.optimization_barrier((ffn_blocks, upstream))
    branch_own, ffn_rms, ffn_gain_part = call(
        ffn_back_kernel,
        [((OWN, D), LOW), ((OWN, 1), F32), ((1, D), F32)],
        *ffn_blocks, upstream, ffn_gains,
    )
    branch_other = core_swap(branch_own)
    gate_back_own, up_back_own = units_back(branch_own, downs, gate_own, up_own)
    sent = call(
        out_kernel,
        [((OWN, NEAR), LOW)] * 2,
        at.c.reshape(1).astype(jnp.int32), *attn_blocks, *ffn_blocks,
        own_states, attn_rms, after(ffn_rms, gate_back_own), attn_gains, ffn_gains,
        scalars=1,
    )
    branch_other = after(branch_other, gate_back_own, sent)
    gate_back_other, up_back_other = units_back(branch_other, downs, gate_other, up_other)
    came = core_swap(pair_down(gate_back_other, up_back_other, gates, ups, LOW))
    pair_parts = pair_down(after(gate_back_own, gate_back_other), up_back_own, gates, ups, F32)
    pair_parts = settle(pair_parts, came)

    hidden_sum = scatter_z(pair_parts)
    hidden_rows = hidden_sum + upstream[:BLOCK].astype(F32)
    branch_own, hidden_own, pair_parts = lax.optimization_barrier(
        (branch_own, hidden_own, pair_parts)
    )
    shuffled = shuffle(after(sent, pair_parts))
    gate_args = [hidden_own, hidden_other, gate_back_own, gate_back_other]
    up_args = [hidden_own, hidden_other, up_back_own, up_back_other]
    down_args = [branch_own, branch_other, units_own, units_other]
    plan = [(0, 1024, [(0, 2, 0), (1, 3, 0)])]
    (down_grads,) = weight_grad(at.plain, down_args, plan, joined=True)
    gate_grads = weight_grad(at.columns, gate_args, plan)
    hidden_sum, down_grads, gate_grads, shuffled, up_args = lax.optimization_barrier(
        (hidden_sum.astype(LOW), down_grads, gate_grads, shuffled, up_args)
    )
    down_rows = lax.psum_scatter(down_grads, ("y", "xh", "xl"), scatter_dimension=0, tiled=True)

    hidden_blocks = gather_z(hidden_sum)
    gate_came = {i: plane_shift(after(gate_grads[i], hidden_sum), i, False) for i in (1, 3)}
    up_grads = weight_grad(at.columns, up_args, plan)
    hidden_blocks, gate_came, up_grads = lax.optimization_barrier(
        (hidden_blocks, gate_came, up_grads)
    )
    mix_own, attn_gain_part = call(
        attn_back_kernel,
        [((OWN, D), LOW), ((1, D), F32)],
        *hidden_blocks, *attn_blocks, upstream, attn_rms, attn_gains,
    )
    mix_other = core_swap(mix_own)

    up_came = {i: plane_shift(after(up_grads[i], hidden_blocks), i, False) for i in (1, 3)}
    hat, value_back, dots, head_parts = call(
        attend_back_kernel,
        [((SEQ, 512), F32), ((SEQ, 256), LOW), ((8, SEQ), F32), ((2, 256), F32)],
        qkv, scales, head_gains, *tables, low, mix_own, mix_other, near_mix, far_mix,
        scratch=[pltpu.VMEM((SEQ, HEAD), F32)] * 2 + [pltpu.VMEM((SEQ, 256), LOW)],
    )
    hat, up_came, dots = lax.optimization_barrier((hat, up_came, dots))
    gate_came[2] = plane_shift(after(gate_grads[2], hat), 2, False)
    up_came[2] = plane_shift(after(up_grads[2], hat), 2, False)
    dots = all_stats(dots)
    (qkv_back,) = call(
        qkv_back_kernel, [((SEQ, SEQ), LOW)], hat, qkv, scales, dots, value_back
    )
    came = core_swap(qkv_down(qkv_back, 1, qkv_blocks, LOW))
    input_parts = settle(qkv_down(qkv_back, 0, qkv_blocks, F32), came)
    input_parts, qkv_back, gate_came, up_came = lax.optimization_barrier(
        (input_parts, qkv_back, gate_came, up_came)
    )

    gate_rows = plane_sum(gate_grads[0], [gate_came[i] for i in (1, 2, 3)])
    up_rows = plane_sum(up_grads[0], [up_came[i] for i in (1, 2, 3)])
    ffn_rows = [jnp.concatenate([g, u], axis=1) for g, u in zip(gate_rows, up_rows)]
    ffn_came = {i: plane_shift(after(ffn_rows[i], input_parts), i, True) for i in (1, 3)}
    ffn_came[2] = plane_shift(after(ffn_rows[2], ffn_came), 2, True)
    attn_grads = weight_grad(
        at.columns,
        [states, qkv_back, mix_own, mix_other, mixed],
        [(0, SEQ, [(0, 1, 0)]), (0, 256, [(2, 4, 0), (3, 4, OWN)])],
        [attn_gain_part, ffn_gain_part, jnp.pad(head_parts.reshape(16, 32), ((0, 0), (0, 96)))],
    )
    input_low = (scatter_z(input_parts) + hidden_rows).astype(LOW)
    input_low, attn_grads, ffn_came, down_rows = lax.optimization_barrier(
        (input_low, attn_grads, ffn_came, down_rows)
    )

    near, far = input_low[:, :NEAR], input_low[:, NEAR:]
    flip = at.c == 1
    input_sent = [jnp.where(flip, far, near), jnp.where(flip, near, far)]
    input_rows = shuffled_of(at, input_sent, shuffle(input_sent))
    input_rows, attn_grads = lax.optimization_barrier((jnp.concatenate(input_rows), attn_grads))
    input_rows = lax.all_gather(input_rows, "z", axis=0, tiled=True)
    attn_came = [plane_shift(attn_grads[i], i, False) for i in range(1, RING)]

    steps = jnp.arange(8, dtype=jnp.int32)
    from_part = at.s ^ at.c ^ (steps // RING)
    from_z = (at.z - steps) % RING
    block_out = order_rows(
        at, shuffled_of(at, sent, after(shuffled, input_low)), from_z, from_part
    )
    (input_grad,) = call(
        widen_kernel, [((SEQ, NEAR), F32)],
        (steps % RING * 2 + from_part).astype(jnp.int32), input_rows,
        scalars=1,
    )

    attn_came, ffn_came, input_grad, block_out = lax.optimization_barrier(
        (attn_came, ffn_came, input_grad, block_out)
    )
    attn_rows = plane_sum(attn_grads[0], attn_came)
    attn_came = [plane_shift(attn_rows[i], i, True) for i in range(1, RING)]
    ffn0, ffn1 = share_cores(at, ffn_rows[0], [ffn_came[i] for i in (1, 2, 3)])
    gate_out, up_out = (
        jnp.concatenate([ffn0[:, i : i + 1024], ffn1[:, i : i + 1024]], axis=1)
        for i in range(0, 2048, 1024)
    )
    mine, theirs = (down_rows[64 * k : 64 * (k + 1)] for k in range(2))
    flip = at.c == 1
    mine, theirs = jnp.where(flip, theirs, mine), jnp.where(flip, mine, theirs)
    came = core_swap(theirs)
    down_out = jnp.concatenate(
        [jnp.where(flip, came, mine), jnp.where(flip, mine, came)], axis=1
    ).astype(F32)
    attn0, attn1 = share_cores(at, attn_rows[0], attn_came)
    query, key, value, mix_out = (
        jnp.concatenate([attn0[:64, i : i + 256], attn1[:64, i : i + 256]], axis=1)
        for i in range(0, 1024, 256)
    )
    width = attn0[64:66, :128] + attn1[64:66, :128]
    width = jnp.where(flip, width[:, 64:], width[:, :64])
    heads = jnp.where(at.s == 0, attn0[66:68, :32], attn1[66:68, :32])
    heads = jnp.where(flip, heads[:, 16:], heads[:, :16])

    return (
        block_out, input_grad, query, key, value, mix_out.T, gate_out, up_out, down_out.T,
        width[0], width[1], heads[0], heads[1],
    )


def solution(mesh):
    fine = Mesh(mesh.devices.reshape(4, 2, 2, 4, 2), ("y", "xh", "core", "z", "xl"))
    dp = ("y", "xh", "core")
    row, col = "z", "xl"
    return jax.shard_map(
        local,
        mesh=fine,
        in_specs=(
            P(dp, col), P(dp), P(col, row), P(col, row), P(col, row), P(row, col),
            P(col, row), P(col, row), P(row, col), P(col), P(col), P((row, col)),
            P((row, col)), P(dp, col),
        ),
        out_specs=(
            P(dp, col), P(dp, col),
            P((col,) + dp, row), P((col,) + dp, row), P((col,) + dp, row), P(row, (col,) + dp),
            P((col,) + dp, row), P((col,) + dp, row), P(row, (col,) + dp),
            P((col,) + dp), P((col,) + dp), P((row, col) + dp), P((row, col) + dp),
        ),
        check_vma=False,
    )
```

```python
import functools

import jax
import jax.numpy as jnp
from jax import lax
from jax.experimental import pallas as pl
from jax.experimental.pallas import tpu as pltpu
from jax.sharding import Mesh, PartitionSpec as P

D = 2048
HEAD = 128
SEQ = 768
NEAR = D // 2
OWN = SEQ // 2
RING = 4
BLOCK = SEQ // 8
EPSILON = 1e-06
ROPE_BASE = 500000.0
MASKED = -1e30
LOW = jnp.bfloat16
F32 = jnp.float32
FREE = pl.CostEstimate(flops=0, bytes_accessed=0, transcendentals=0)
PARAMS = pltpu.CompilerParams(vmem_limit_bytes=24 * 1024 * 1024)
EARLY = pltpu.CompilerParams(vmem_limit_bytes=60 * 1024 * 1024)


def dot(a, b, dims=((1,), (0,))):
    return lax.dot_general(a, b, (dims, ((), ())), preferred_element_type=F32)


NT = ((1,), (1,))
TN = ((0,), (0,))


def after(value, *earlier):
    return lax.optimization_barrier((value, earlier))[0]


def ring_shift(a, axes, step):
    return lax.ppermute(a, axes, [(i, (i + step) % RING) for i in range(RING)])


def z_shift(a, step):
    return ring_shift(a, "z", step)


def plane_shift(a, step, swapped):
    pairs = []
    for y in range(4):
        for x in range(4):
            for c in range(2):
                there = ((y + step) % 4, x) if (c == 0) != swapped else (y, (x + step) % 4)
                xh, xl = x // 2, x % 2
                source = ((y * 2 + xh) * 2 + c) * 2 + xl
                pairs.append((source, ((there[0] * 2 + there[1] // 2) * 2 + c) * 2 + there[1] % 2))
    return lax.ppermute(a, ("y", "xh", "core", "xl"), pairs)


def core_swap(a):
    return lax.ppermute(a, "core", [(0, 1), (1, 0)])


def pair_swap(a):
    return lax.ppermute(a, "xl", [(0, 1), (1, 0)])


def wrap_swap(a):
    return lax.ppermute(a, ("xh", "xl"), [(0, 3), (3, 0), (1, 2), (2, 1)])


def pick(blocks, index, axis=0):
    return lax.dynamic_index_in_dim(blocks, index, axis, keepdims=False)


class Place:
    def __init__(self):
        self.s = lax.axis_index("xl")
        self.xh = lax.axis_index("xh")
        self.x = self.xh * 2 + self.s
        self.y = lax.axis_index("y")
        self.c = lax.axis_index("core")
        self.z = lax.axis_index("z")
        self.home = self.c == self.s
        self.z_scalar = self.z.reshape(1).astype(jnp.int32)
        steps = jnp.arange(RING, dtype=jnp.int32)
        self.back = (self.z - steps) % RING
        self.rows = jnp.concatenate([self.c * 4 + self.back, (1 - self.c) * 4 + self.back])
        first, second = steps[:, None], steps[None, :]
        dx = jnp.where(self.c == 0, second, first)
        dy = jnp.where(self.c == 0, first, second)
        self.columns = (
            (dx % 2) * 8 + ((self.y + dy) % 4) * 2 + ((self.x + dx) % 4) // 2
        ).reshape(-1)
        y, x = first, second
        self.plain = (((x % 2) ^ self.s) * 8 + y * 2 + x // 2).reshape(-1)


def place_kernel(plan, sources, table, *refs):
    ins, outs, sems = refs[:sources], refs[sources:-1], refs[-1]
    copies = []
    for i, (source, there) in enumerate(plan(table, ins, outs)):
        copies.append(pltpu.make_async_copy(source, there, sems.at[i]))
        copies[-1].start()
    for copy in copies:
        copy.wait()


def place(plan, count, shapes, table, *sources, params=PARAMS):
    return pl.pallas_call(
        functools.partial(place_kernel, plan, len(sources)),
        in_specs=[pl.BlockSpec(memory_space=pltpu.SMEM)]
        + [pl.BlockSpec(memory_space=pltpu.HBM)] * len(sources),
        out_specs=tuple(pl.BlockSpec(memory_space=pltpu.VMEM) for _ in shapes),
        out_shape=tuple(jax.ShapeDtypeStruct(shape, LOW) for shape in shapes),
        scratch_shapes=[pltpu.SemaphoreType.DMA((count,))],
        compiler_params=params,
        cost_estimate=FREE,
    )(jnp.stack(table).astype(jnp.int32), *sources)


def at_block(index, size):
    return pl.ds(pl.multiple_of(index * size, size), size)


def first_hop(a):
    return lax.ppermute(a, ("core", "xl"), [(0, 2), (3, 1), (2, 3), (1, 0)])


def second_hop(first):
    return lax.ppermute(first, ("core", "xl"), [(0, 2), (3, 1)])


def sequence_kernel(count, table, a_ref, first_ref, second_ref, out_ref, sems):
    def move(near, far):
        copies = []
        for i in range(count):
            block = at_block(table[i], BLOCK)
            there = pl.ds(i * BLOCK, BLOCK)
            for source, lo in ((near.at[block], 0), (far.at[block], NEAR)):
                copies.append(
                    pltpu.make_async_copy(
                        source, out_ref.at[there, pl.ds(lo, NEAR)], sems.at[len(copies)]
                    )
                )
        for copy in copies:
            copy.start()
        for copy in copies:
            copy.wait()

    pl.when(table[count] == 1)(functools.partial(move, a_ref, first_ref))
    pl.when(table[count] == 0)(functools.partial(move, first_ref, second_ref))


def to_sequence(at, a, first, second, count=8):
    table = jnp.concatenate([at.rows[:count], at.home[None].astype(jnp.int32)])
    return pl.pallas_call(
        functools.partial(sequence_kernel, count),
        in_specs=[pl.BlockSpec(memory_space=pltpu.SMEM)]
        + [pl.BlockSpec(memory_space=pltpu.HBM)] * 3,
        out_specs=pl.BlockSpec(memory_space=pltpu.VMEM),
        out_shape=jax.ShapeDtypeStruct((count * BLOCK, D), LOW),
        scratch_shapes=[pltpu.SemaphoreType.DMA((2 * count,))],
        compiler_params=PARAMS,
        cost_estimate=FREE,
    )(table.astype(jnp.int32), a, first, second)


def order_rows(at, sources, index, which):
    joined = jnp.concatenate(sources) if len(sources) > 1 else sources[0]
    rows = sources[0].shape[0] // BLOCK

    def plan(table, ins, outs):
        return [
            (ins[0].at[at_block(table[i], BLOCK)], outs[0].at[pl.ds(i * BLOCK, BLOCK)])
            for i in range(8)
        ]

    table = index + rows * which if len(sources) > 1 else index * 2 + which
    return place(plan, 8, [(SEQ, joined.shape[1])], list(table), joined)[0]


def cut_columns(at, heights, *weights):
    width = weights[0].shape[1] // 2
    starts = [sum(heights[:i]) for i in range(len(heights))]

    def plan(table, ins, outs):
        return [
            (
                ref.at[pl.ds(start, height), at_block(table[0], width)],
                out.at[:, pl.ds(width * i, width)],
            )
            for i, ref in enumerate(ins)
            for start, height, out in zip(starts, heights, outs)
        ]

    shapes = [(height, width * len(weights)) for height in heights]
    return place(plan, len(heights) * len(weights), shapes, [at.c], *weights, params=EARLY)


PIECES = (
    (("gate", 0),), (("gate", 1),),
    (("gate", 2), ("up", 0)), (("gate", 3), ("up", 1)),
    (("up", 2), ("down", 0)), (("up", 3), ("down", 1)),
    (("down", 2),), (("down", 3),),
)
PART = 256


def cut_pieces(at, w_gate, w_up, w_down):
    def plan(table, ins, outs):
        named = dict(zip(("gate", "up", "down"), ins))
        copies = []
        for out, piece in zip(outs, PIECES):
            for i, (name, part) in enumerate(piece):
                if name == "down":
                    rows = pl.ds(pl.multiple_of(table[0] * NEAR + PART * part, PART), PART)
                    source = named[name].at[rows]
                else:
                    source = named[name].at[pl.ds(PART * part, PART), at_block(table[0], NEAR)]
                copies.append((source, out.at[pl.ds(PART * i, PART)]))
        return copies

    shapes = [(PART * len(piece), NEAR) for piece in PIECES]
    return place(plan, 12, shapes, [at.c], w_gate, w_up, w_down, params=EARLY)


def pieces_with(name):
    return [k for k, piece in enumerate(PIECES) if name in dict(piece)]


def views(name, refs):
    out = []
    for ref, k in zip(refs, pieces_with(name)):
        for i, (found, _) in enumerate(PIECES[k]):
            if found == name:
                out.append(ref.at[pl.ds(PART * i, PART)])
    return out


def join_columns(parts):
    starts = [sum(part.shape[1] for part in parts[:i]) for i in range(len(parts) + 1)]

    def plan(table, ins, outs):
        return [
            (ref, outs[0].at[:, pl.ds(starts[i], parts[i].shape[1])]) for i, ref in enumerate(ins)
        ]

    return place(plan, len(parts), [(D, starts[-1])], [0], *parts)[0]


def fetch(first, second):
    return pair_swap(first), wrap_swap(second)


def scatter_z(parts):
    total = parts[0]
    for i in range(1, RING):
        total = total + z_shift(parts[i], -i).astype(F32)
    return total


def gather_z(rows):
    return [rows] + [z_shift(rows, i) for i in range(1, RING)]


def all_stats(pair):
    theirs = core_swap(pair)
    pair = pair + jnp.concatenate([theirs[:, OWN:], theirs[:, :OWN]], axis=1)
    total = pair
    for i in range(1, RING):
        came, cut = z_shift(pair, i), OWN - i * BLOCK
        total = total + jnp.concatenate(
            [came[:, cut:OWN], came[:, :cut], came[:, OWN + cut :], came[:, OWN : OWN + cut]],
            axis=1,
        )
    return total


def plane_sum(own, came):
    total = own.astype(F32) + came[0].astype(F32) + came[1].astype(F32) + came[2].astype(F32)
    total = lax.optimization_barrier(total.astype(LOW))
    height = own.shape[0] // RING
    return [total[height * i : height * (i + 1)] for i in range(RING)]


def share_kernel(core, p0, p1, p2, p3, own_ref, sent_ref):
    total = p0[...].astype(F32) + p1[...].astype(F32) + p2[...].astype(F32) + p3[...].astype(F32)
    flip = core[0] == 1
    for i in range(total.shape[0] // 128):
        at = slice(64 * i, 64 * (i + 1))
        low, high = total[128 * i : 128 * i + 64, :], total[128 * i + 64 : 128 * (i + 1), :]
        own_ref[at, :] = jnp.where(flip, high, low)
        sent_ref[at, :] = jnp.where(flip, low, high).astype(LOW)
    rest = total.shape[0] % 128
    if rest:
        own_ref[-rest:, :] = total[-rest:, :]
        sent_ref[-rest:, :] = total[-rest:, :].astype(LOW)


def wide_kernel(plan, core, own_ref, came_ref, *outs):
    first = core[0] == 0
    own, came = own_ref[...], came_ref[...].astype(F32)
    sides = jnp.where(first, own, came), jnp.where(first, came, own)
    for i, (out, pieces) in enumerate(zip(outs, plan)):
        at = 0
        for side in sides:
            for rows, start, width in pieces:
                value = side[64 * rows : 64 * (rows + 1), start : start + width]
                if i == len(plan) - 1:
                    out[at : at + width, :] = value.T
                else:
                    out[:, at : at + width] = value
                at += width
    if len(outs) > len(plan):
        width_ref, heads_ref = outs[len(plan) :]
        zero, one = (side[-16:-8, :128] for side in sides)
        width_ref[...] = zero + one
        heads_ref[0:8, :] = zero
        heads_ref[8:16, :] = one


def share_cores(at, own, came, plan, extra=()):
    height, width = own.shape
    shape = (height // 128 * 64 + height % 128, width)
    core = at.c.reshape(1).astype(jnp.int32)
    own, sent = call(share_kernel, [(shape, F32), (shape, LOW)], core, own, *came, scalars=1)
    widths = [2 * sum(piece[2] for piece in pieces) for pieces in plan]
    shapes = [((64, width), F32) for width in widths[:-1]] + [((widths[-1], 64), F32)]
    shapes += [(shape, F32) for shape in extra]
    return call(functools.partial(wide_kernel, plan), shapes, core, own, core_swap(sent), scalars=1)


def call(kernel, shapes, *args, scratch=(), scalars=0):
    return pl.pallas_call(
        kernel,
        in_specs=[
            pl.BlockSpec(memory_space=pltpu.SMEM if i < scalars else pltpu.VMEM)
            for i in range(len(args))
        ],
        out_shape=tuple(jax.ShapeDtypeStruct(shape, dtype) for shape, dtype in shapes),
        scratch_shapes=list(scratch),
        compiler_params=PARAMS,
        cost_estimate=FREE,
    )(*args)


def row_dot(rows, refs, at):
    value = 0.0
    start = 0
    for ref in refs:
        height = ref.shape[0]
        value += dot(rows[:, start : start + height], ref[:, at])
        start += height
    return value


def strips(width, size):
    return [slice(i, i + size) for i in range(0, width, size)]


def as_rows(first, second):
    return jnp.concatenate([first, second, jnp.zeros((SEQ, 6), F32)], axis=1).T


def qkv_kernel(states_ref, *refs):
    *blocks, qkv_ref, sums_ref = refs
    sums = []
    for at in strips(SEQ, 256):
        value = row_dot(states_ref, blocks, at)
        qkv_ref[:, at] = value
        sums.append(jnp.sum(value * value, axis=1, keepdims=True))
    sums_ref[...] = as_rows(*sums[:2])


def product_kernel(body, *refs):
    *refs, out_ref = refs
    for at, value in body(refs):
        out_ref[:, at] = value.astype(out_ref.dtype)


def product(body, dtype, *args):
    return call(functools.partial(product_kernel, body), [((OWN, D), dtype)], *args)[0]


def half_rows(ref, half):
    return ref[OWN * half : OWN * (half + 1), :]


def mix(left, half, near, far, dtype):
    def body(refs):
        left, near, far = refs
        left = half_rows(left, half)
        for at in strips(NEAR, 512):
            yield at, dot(left, near[:, at])
            yield slice(NEAR + at.start, NEAR + at.stop), dot(left, far[:, at])

    return product(body, dtype, left, near, far)


def down(units, pieces, dtype):
    count = len(pieces) // 2

    def body(refs):
        units, *w = refs
        for i in range(2):
            blocks = views("down", w[count * i : count * (i + 1)])
            for at in strips(NEAR, 512):
                yield slice(NEAR * i + at.start, NEAR * i + at.stop), row_dot(units, blocks, at)

    return product(body, dtype, units, *pieces)


def pair_down(gate_back, up_back, gates, ups, dtype):
    def body(refs):
        gate_back, up_back, *w = refs
        for i in range(2):
            n, m = len(gates) // 2, len(ups) // 2
            gate = views("gate", w[n * i : n * (i + 1)])
            up = views("up", w[2 * n + m * i : 2 * n + m * (i + 1)])
            for k in range(4):
                value = dot(gate_back[...], gate[k][...], NT) + dot(up_back[...], up[k][...], NT)
                yield slice(NEAR * i + PART * k, NEAR * i + PART * (k + 1)), value

    return product(body, dtype, gate_back, up_back, *gates, *ups)


def qkv_down(back, half, blocks, dtype):
    def body(refs):
        back, *w = refs
        back = half_rows(back, half)
        start = 0
        for ref in w:
            for at in strips(ref.shape[0], 256):
                yield slice(start + at.start, start + at.stop), dot(back, ref[at, :], NT)
            start += ref.shape[0]

    return product(body, dtype, back, *blocks)


def settle_kernel(own_ref, came_ref, *outs):
    for i, ref in enumerate(outs):
        at = slice(i * BLOCK, (i + 1) * BLOCK)
        ref[...] = (own_ref[at, :] + came_ref[at, :].astype(F32)).astype(ref.dtype)


def settle(own, came):
    return call(
        settle_kernel, [((BLOCK, D), F32)] + [((BLOCK, D), LOW)] * 3, own, came
    )


def z_rows(z, i):
    return pl.ds(pl.multiple_of(lax.rem(z + RING - i, RING) * BLOCK, BLOCK), BLOCK)


def settle_ordered_kernel(z_ref, own_ref, came_ref, out_ref):
    for i in range(RING):
        at = slice(i * BLOCK, (i + 1) * BLOCK)
        value = own_ref[at, :] + came_ref[at, :].astype(F32)
        out_ref[z_rows(z_ref[0], i), :] = value.astype(LOW)


def settle_ordered(at, own, came):
    return call(settle_ordered_kernel, [((OWN, D), LOW)], at.z_scalar, own, came, scalars=1)[0]


def units_kernel(n, m, rows_ref, *refs):
    gate_ref, up_ref, units_ref = refs[-3:]
    gates = views("gate", refs[:n]) + views("gate", refs[n : 2 * n])
    ups = views("up", refs[2 * n : 2 * n + m]) + views("up", refs[2 * n + m : 2 * n + 2 * m])
    for at in strips(1024, 512):
        gate, up = row_dot(rows_ref, gates, at), row_dot(rows_ref, ups, at)
        gate_ref[:, at] = gate.astype(LOW)
        up_ref[:, at] = up.astype(LOW)
        units_ref[:, at] = (gate * jax.nn.sigmoid(gate) * up).astype(LOW)


def units_of(rows, gates, ups):
    kernel = functools.partial(units_kernel, len(gates) // 2, len(ups) // 2)
    return call(kernel, [((OWN, 1024), LOW)] * 3, rows, *gates, *ups)


def units_back_kernel(branch_ref, *refs):
    *w, gate_ref, up_ref, gate_back_ref, up_back_ref = refs
    count = len(w) // 2
    near, far = views("down", w[:count]), views("down", w[count:])
    for k in range(4):
        at = slice(PART * k, PART * (k + 1))
        grad = dot(branch_ref[:, :NEAR], near[k][...], NT)
        grad += dot(branch_ref[:, NEAR:], far[k][...], NT)
        gate, up = gate_ref[:, at].astype(F32), up_ref[:, at].astype(F32)
        sigmoid = jax.nn.sigmoid(gate)
        gate_back_ref[:, at] = (grad * up * sigmoid * (1.0 + gate * (1.0 - sigmoid))).astype(LOW)
        up_back_ref[:, at] = (grad * gate * sigmoid).astype(LOW)


def units_back(branch, pieces, gate, up):
    return call(units_back_kernel, [((OWN, 1024), LOW)] * 2, branch, *pieces, gate, up)


def grad_kernel(plan, count, extras, cut, *refs):
    table, ins = refs[0], refs[1 : 1 + count]
    extra, outs = refs[1 + count : 1 + count + extras], refs[1 + count + extras :]
    if cut:
        outs = [(outs[0],), outs[1:3], (outs[3],), outs[4:6]]
    for d in range(RING):
        blocks = [table[4 * d + e] for e in range(RING)]
        places = [at_block(block, 128) for block in blocks]
        start = 0
        for lo, width, terms in plan:
            value = 0.0
            for left, right, row in terms:
                left, right = ins[left], ins[right]
                chosen = jnp.concatenate([left[:, place] for place in places], axis=1)
                value += dot(chosen, right[row : row + left.shape[0], lo : lo + width], TN)
            value = value.astype(LOW)
            at = slice(start, start + width)
            if cut:
                put_columns(outs[d], start, value)
            elif not extras:
                outs[d][:, at] = value
            else:
                for e in range(RING):
                    outs[d][144 * e : 144 * e + 128, at] = value[128 * e : 128 * (e + 1)]
            start += width
        if extras:
            attn_ref, ffn_ref, heads_ref = extra
            for e in range(RING):
                block = lax.rem(blocks[e], 8)
                rows = [attn_ref[0:1, places[e]], ffn_ref[0:1, places[e]]]
                rows += [heads_ref[pl.ds(block + 8 * i, 1), :] for i in range(2)]
                rows = jnp.concatenate([*rows, jnp.zeros((12, 128), F32)])
                at = slice(144 * e + 128, 144 * (e + 1))
                outs[d][at, :128] = rows.astype(LOW)
                outs[d][at, 128:] = jnp.zeros((16, start - 128), LOW)


def put_columns(outs, start, value):
    at = 0
    for out in outs:
        lo, hi = max(start, at), min(start + value.shape[1], at + out.shape[1])
        if lo < hi:
            out[:, lo - at : hi - at] = value[:, lo - start : hi - start]
        at += out.shape[1]


def weight_grad(table, arrays, plan, extra=(), cut=False):
    width = sum(span[1] for span in plan)
    height = 576 if extra else 512
    kernel = functools.partial(grad_kernel, plan, len(arrays), len(extra), cut)
    widths = [width, width // 2, width // 2, width, width // 2, width // 2] if cut else [width] * RING
    outs = [((height, w), LOW) for w in widths]
    return call(kernel, outs, table.astype(jnp.int32), *arrays, *extra, scalars=1)


def turn(v, cosines, sines):
    return v * cosines + pltpu.roll(v, HEAD // 2, 1) * sines


def turn_back(v, cosines, sines):
    return v * cosines - pltpu.roll(v, HEAD // 2, 1) * sines


TILE = 256


def seen(table_ref, row_ref, lo):
    here = table_ref[lo : lo + TILE, 2 * HEAD : 3 * HEAD]
    there = row_ref[0:1, :]
    return (there <= here[:, 0:1]) & (there >= here[:, 1:2])


def attend_kernel(
    qkv_ref, sums_ref, gain_ref, table_ref, row_ref, mixed_ref, low_ref, scale_ref
):
    cosines, sines = table_ref[:, :HEAD], table_ref[:, HEAD : 2 * HEAD]
    scale_ref[...] = lax.rsqrt(sums_ref[...] * (1.0 / D) + EPSILON).T
    for h in range(2):
        at = slice(h * HEAD, (h + 1) * HEAD)
        k_at = slice(256 + h * HEAD, 256 + (h + 1) * HEAD)
        q = qkv_ref[:, at] * scale_ref[:, 0:1] * gain_ref[0:1, at]
        k = qkv_ref[:, k_at] * scale_ref[:, 1:2] * gain_ref[1:2, at]
        low_ref[:, at] = turn(q, cosines, sines).astype(LOW)
        k = turn(k, cosines, sines).astype(LOW)
        v = qkv_ref[:, 512 + h * HEAD : 512 + (h + 1) * HEAD].astype(LOW)
        low_ref[:, k_at] = k
        low_ref[:, 512 + h * HEAD : 512 + (h + 1) * HEAD] = v
        for lo in range(0, SEQ, TILE):
            q = low_ref[lo : lo + TILE, at]
            scores = dot(q, k, NT) * HEAD**-0.5
            scores = jnp.where(seen(table_ref, row_ref, lo), scores, MASKED)
            peak = jnp.max(scores, axis=1, keepdims=True)
            weights = jnp.exp(scores - peak)
            total = jnp.sum(weights, axis=1, keepdims=True)
            weights = (weights * (1.0 / total)).astype(LOW)
            mixed_ref[lo : lo + TILE, at] = dot(weights, v).astype(LOW)
            scale_ref[lo : lo + TILE, 2 + h : 3 + h] = peak + jnp.log(total)


def attend_back_kernel(
    qkv_ref, scale_ref, gain_ref, table_ref, row_ref, low_ref,
    own_ref, other_ref, near_ref, far_ref,
    hat_ref, value_ref, dots_ref, part_ref, dk_ref, dv_ref, grad_ref,
):
    cosines, sines = table_ref[:, :HEAD], table_ref[:, HEAD : 2 * HEAD]
    for i, ref in enumerate((own_ref, other_ref)):
        grad = dot(ref[:, :NEAR], near_ref[...], NT) + dot(ref[:, NEAR:], far_ref[...], NT)
        grad_ref[OWN * i : OWN * (i + 1), :] = grad.astype(LOW)
    for h in range(2):
        at = slice(h * HEAD, (h + 1) * HEAD)
        k_at = slice(256 + h * HEAD, 256 + (h + 1) * HEAD)
        k = low_ref[:, k_at]
        v = low_ref[:, 512 + h * HEAD : 512 + (h + 1) * HEAD]
        for lo in range(0, SEQ, TILE):
            q = low_ref[lo : lo + TILE, at]
            grad = grad_ref[lo : lo + TILE, at]
            scores = dot(q, k, NT) * HEAD**-0.5
            weights = jnp.exp(scores - scale_ref[lo : lo + TILE, 2 + h : 3 + h])
            weights = jnp.where(seen(table_ref, row_ref, lo), weights, 0.0)
            weight_grad = dot(grad, v, NT)
            centre = jnp.sum(weights * weight_grad, axis=1, keepdims=True)
            score_grad = (weights * (weight_grad - centre)).astype(LOW)
            hat_ref[lo : lo + TILE, at] = dot(score_grad, k) * HEAD**-0.5
            value_part = dot(weights.astype(LOW), grad, TN)
            key_part = dot(score_grad, q, TN)
            if lo == 0:
                dv_ref[...] = value_part
                dk_ref[...] = key_part
            else:
                dv_ref[...] += value_part
                dk_ref[...] += key_part
        value_ref[:, at] = dv_ref[...].astype(LOW)
        q_grad = turn_back(hat_ref[:, at], cosines, sines)
        k_grad = turn_back(dk_ref[...] * HEAD**-0.5, cosines, sines)
        q, k = qkv_ref[:, at], qkv_ref[:, k_at]
        part_ref[0:1, at] = jnp.sum(q_grad * q * scale_ref[:, 0:1], axis=0, keepdims=True)
        part_ref[1:2, at] = jnp.sum(k_grad * k * scale_ref[:, 1:2], axis=0, keepdims=True)
        hat_ref[:, at] = q_grad * gain_ref[0:1, at]
        hat_ref[:, k_at] = k_grad * gain_ref[1:2, at]
    dots_ref[...] = as_rows(
        jnp.sum(hat_ref[:, :256] * qkv_ref[:, :256], axis=1, keepdims=True),
        jnp.sum(hat_ref[:, 256:] * qkv_ref[:, 256:512], axis=1, keepdims=True),
    )


def qkv_back_kernel(hat_ref, qkv_ref, rms_ref, dots_ref, value_ref, out_ref):
    dots = dots_ref[...].T
    for i in range(2):
        at = slice(i * 256, (i + 1) * 256)
        rms = rms_ref[:, i : i + 1]
        coefficient = rms * rms * rms * dots[:, i : i + 1] * (1.0 / D)
        out_ref[:, at] = (rms * hat_ref[:, at] - qkv_ref[:, at] * coefficient).astype(LOW)
    out_ref[:, 512:] = value_ref[...]


def widen_kernel(table, rows_ref, out_ref):
    for i in range(8):
        block = pl.ds(pl.multiple_of(table[i] * BLOCK, BLOCK), BLOCK)
        out_ref[i * BLOCK : (i + 1) * BLOCK, :] = rows_ref[block, :].astype(F32)


def blocks_of(ref):
    return [slice(i * BLOCK, (i + 1) * BLOCK) for i in range(ref.shape[0] // BLOCK)]


def hidden_kernel(b0, b1, b2, b3, states_ref, gain_ref, low_ref, rms_ref):
    for at, ref in zip(blocks_of(low_ref), (b0, b1, b2, b3)):
        branch = ref[...].astype(F32)
        rms = lax.rsqrt(jnp.mean(branch * branch, axis=1, keepdims=True) + EPSILON)
        hidden = states_ref[at, :].astype(F32) + gain_ref[...] * branch * rms
        low_ref[at, :] = hidden.astype(LOW)
        rms_ref[at, :] = rms


def back_of(upstream, branch, rms, gain):
    part = jnp.sum(upstream * branch * rms, axis=0, keepdims=True)
    scaled = upstream * gain
    inner = jnp.sum(scaled * branch, axis=1, keepdims=True)
    return rms * scaled - branch * (rms * rms * rms * inner * (1.0 / D)), part


def ffn_back_kernel(b0, b1, b2, b3, upstream_ref, gain_ref, back_ref, rms_ref, part_ref):
    for i, (at, ref) in enumerate(zip(blocks_of(back_ref), (b0, b1, b2, b3))):
        branch = ref[...].astype(F32)
        rms = lax.rsqrt(jnp.mean(branch * branch, axis=1, keepdims=True) + EPSILON)
        back, part = back_of(upstream_ref[at, :].astype(F32), branch, rms, gain_ref[...])
        back_ref[at, :] = back.astype(LOW)
        rms_ref[at, :] = rms
        part_ref[...] = part if i == 0 else part_ref[...] + part


def attn_back_kernel(
    g0, g1, g2, g3, b0, b1, b2, b3, upstream_ref, rms_ref, gain_ref, back_ref, part_ref
):
    pairs = zip(blocks_of(back_ref), (g0, g1, g2, g3), (b0, b1, b2, b3))
    for i, (at, grad_ref, ref) in enumerate(pairs):
        grad = grad_ref[...].astype(F32) + upstream_ref[at, :].astype(F32)
        back, part = back_of(grad, ref[...].astype(F32), rms_ref[at, :], gain_ref[...])
        back_ref[at, :] = back.astype(LOW)
        part_ref[...] = part if i == 0 else part_ref[...] + part


def out_kernel(
    core_ref, a0, a1, a2, a3, b0, b1, b2, b3, states_ref, attn_rms_ref, ffn_rms_ref,
    attn_gain_ref, ffn_gain_ref, sent0_ref, sent1_ref,
):
    pairs = zip(blocks_of(states_ref), (a0, a1, a2, a3), (b0, b1, b2, b3))
    flip = core_ref[0] == 1
    for at, a_ref, b_ref in pairs:
        value = (
            states_ref[at, :].astype(F32)
            + attn_gain_ref[...] * a_ref[...].astype(F32) * attn_rms_ref[at, :]
            + ffn_gain_ref[...] * b_ref[...].astype(F32) * ffn_rms_ref[at, :]
        ).astype(LOW)
        near, far = value[:, :NEAR], value[:, NEAR:]
        sent0_ref[at, :] = jnp.where(flip, far, near)
        sent1_ref[at, :] = jnp.where(flip, near, far)


def shuffle(sent):
    out = []
    for k in range(2):
        perm = [(c * 2 + s, s * 2 + (s ^ c ^ k)) for s in range(2) for c in range(2)]
        out.append(lax.ppermute(sent[k], ("core", "xl"), [p for p in perm if p[0] != p[1]]))
    return out


def shuffled_of(at, sent, came):
    return [jnp.where((at.s == k) & (at.c == k), sent[k], came[k]) for k in range(2)]


def local(
    inputs, segments, w_query, w_key, w_value, w_mix, w_gate, w_up, w_down,
    attn_gain, ffn_gain, query_gain, key_gain, out_grad,
):
    at = Place()
    first = first_hop(inputs)
    near_qkv = cut_columns(at, (768, 256), w_query, w_key, w_value)
    far_qkv = [wrap_swap(near_qkv[0]), pair_swap(near_qkv[1])]
    near_mix = lax.dynamic_slice_in_dim(w_mix, at.c * 256, 256, 0)
    near = cut_pieces(at, after(w_gate, near_qkv), w_up, w_down)

    gains = jnp.concatenate([attn_gain, ffn_gain, query_gain, key_gain])
    their_gains = pair_swap(gains)
    attn_gains = jnp.concatenate([attn_gain, their_gains[:NEAR]])[None]
    ffn_gains = jnp.concatenate([ffn_gain, their_gains[NEAR:D]])[None]
    head_gains = jnp.where(at.home, gains[D:], their_gains[D:]).reshape(2, 256)

    segment_ids = jnp.where(at.home, segments, core_swap(segments))
    step_index = jnp.arange(SEQ, dtype=jnp.int32)
    earlier = jnp.concatenate([segment_ids[:1] - 1, segment_ids[:-1]])
    begins = lax.cummax(jnp.where(segment_ids != earlier, step_index, 0))
    chosen = at.rows[:, None, None] == jnp.arange(8, dtype=jnp.int32)[None, :, None]
    begins = jnp.sum(jnp.where(chosen, begins.reshape(1, 8, BLOCK), 0), axis=1).reshape(-1)
    index = (at.rows[:, None] * BLOCK + jnp.arange(BLOCK, dtype=jnp.int32)[None]).reshape(-1)
    frequency = ROPE_BASE ** (-2.0 * jnp.arange(HEAD // 2, dtype=F32) / HEAD)
    angles = (index - begins).astype(F32)[:, None] * frequency
    cosines, sines = jnp.cos(angles), jnp.sin(angles)
    place_columns = jnp.stack([index, begins], axis=1).astype(F32)
    table = jnp.concatenate(
        [cosines, cosines, -sines, sines, jnp.pad(place_columns, ((0, 0), (0, 126)))], axis=1
    )
    tables = (table, index[None].astype(F32))

    tables, head_gains, attn_gains, ffn_gains, at.columns, at.plain, at.rows, near, first = (
        lax.optimization_barrier(
            (tables, head_gains, attn_gains, ffn_gains, at.columns, at.plain, at.rows, near, first)
        )
    )
    states = to_sequence(at, inputs, first, second_hop(after(first, far_qkv)))
    states, far_qkv = lax.optimization_barrier((states, far_qkv))
    qkv_blocks = [*near_qkv, *far_qkv]
    qkv, squares = call(qkv_kernel, [((SEQ, SEQ), F32), ((8, SEQ), F32)], states, *qkv_blocks)
    far = fetch(*after(near[:2], far_qkv))
    both_mix = lax.all_gather(after(near_mix, far_qkv), "xl")
    squares = all_stats(squares)
    squares, far = lax.optimization_barrier((squares, far))
    far_mix = jnp.where(at.s == 0, both_mix[1], both_mix[0])
    mixed, low, scales = call(
        attend_kernel,
        [((SEQ, 256), LOW), ((SEQ, SEQ), LOW), ((SEQ, 8), F32)],
        qkv, squares, head_gains, *tables,
    )
    came = core_swap(mix(mixed, 1, near_mix, far_mix, LOW))
    mix_parts = settle(mix(mixed, 0, near_mix, far_mix, F32), came)
    mix_parts = lax.optimization_barrier(mix_parts)
    far = [*far, *fetch(*after(near[2:4], mix_parts))]
    attn_sum = scatter_z(mix_parts).astype(LOW)
    attn_sum, far = lax.optimization_barrier((attn_sum, far))
    far = [*far, *fetch(*after(near[4:6], attn_sum))]
    attn_blocks = gather_z(attn_sum)
    own_states = after(states, attn_sum)[:OWN]
    attn_blocks, far, own_states = lax.optimization_barrier((attn_blocks, far, own_states))
    far = [*far, *fetch(*after(near[6:], attn_blocks))]
    hidden_own, attn_rms = call(
        hidden_kernel,
        [((OWN, D), LOW), ((OWN, 1), F32)],
        *attn_blocks, own_states, attn_gains,
    )
    hidden_other = core_swap(hidden_own)

    gates, ups, downs = (
        [side[k] for side in (near, far) for k in pieces_with(name)]
        for name in ("gate", "up", "down")
    )
    gate_own, up_own, units_own = units_of(hidden_own, gates, ups)
    hidden_other = after(hidden_other, units_own)
    gate_other, up_other, units_other = units_of(hidden_other, gates, ups)
    came = core_swap(down(units_other, downs, LOW))
    ffn_parts = settle(down(after(units_own, units_other), downs, F32), came)
    ffn_parts = lax.optimization_barrier(ffn_parts)
    grad_first = first_hop(after(out_grad, ffn_parts))
    ffn_sum = scatter_z(ffn_parts).astype(LOW)
    ffn_sum, grad_first = lax.optimization_barrier((ffn_sum, grad_first))
    ffn_blocks = gather_z(ffn_sum)
    upstream = to_sequence(at, out_grad, grad_first, second_hop(grad_first), RING)
    ffn_blocks, upstream = lax.optimization_barrier((ffn_blocks, upstream))
    branch_own, ffn_rms, ffn_gain_part = call(
        ffn_back_kernel,
        [((OWN, D), LOW), ((OWN, 1), F32), ((1, D), F32)],
        *ffn_blocks, upstream, ffn_gains,
    )
    branch_other = core_swap(branch_own)
    gate_back_own, up_back_own = units_back(branch_own, downs, gate_own, up_own)
    sent = call(
        out_kernel,
        [((OWN, NEAR), LOW)] * 2,
        at.c.reshape(1).astype(jnp.int32), *attn_blocks, *ffn_blocks,
        own_states, attn_rms, after(ffn_rms, gate_back_own), attn_gains, ffn_gains,
        scalars=1,
    )
    branch_other = after(branch_other, gate_back_own, sent)
    gate_back_other, up_back_other = units_back(branch_other, downs, gate_other, up_other)
    came = core_swap(pair_down(gate_back_other, up_back_other, gates, ups, LOW))
    pair_parts = pair_down(after(gate_back_own, gate_back_other), up_back_own, gates, ups, F32)
    pair_parts = settle(pair_parts, came)

    hidden_sum = scatter_z(pair_parts)
    hidden_rows = hidden_sum + upstream[:BLOCK].astype(F32)
    branch_own, hidden_own, pair_parts = lax.optimization_barrier(
        (branch_own, hidden_own, pair_parts)
    )
    shuffled = shuffle(after(sent, pair_parts))
    gate_args = [hidden_own, hidden_other, gate_back_own, gate_back_other]
    up_args = [hidden_own, hidden_other, up_back_own, up_back_other]
    down_args = [branch_own, branch_other, units_own, units_other]
    terms = [(0, 2, 0), (1, 3, 0)]
    grads0 = weight_grad(
        at.columns,
        [*gate_args, *up_args[2:]],
        [(0, 1024, terms), (0, 512, [(0, 4, 0), (1, 5, 0)])],
    )
    hidden_sum, grads0, shuffled, up_args, down_args = lax.optimization_barrier(
        (hidden_sum.astype(LOW), grads0, shuffled, up_args, down_args)
    )

    hidden_blocks = gather_z(hidden_sum)
    came0 = {i: plane_shift(after(grads0[i], hidden_sum), i, False) for i in (1, 3)}
    grads1 = weight_grad(
        at.columns,
        [*up_args, *down_args],
        [(512, 512, terms), (0, 1024, [(4, 6, 0), (5, 7, 0)])],
        cut=True,
    )
    hidden_blocks, came0, grads1 = lax.optimization_barrier((hidden_blocks, came0, grads1))
    mix_own, attn_gain_part = call(
        attn_back_kernel,
        [((OWN, D), LOW), ((1, D), F32)],
        *hidden_blocks, *attn_blocks, upstream, attn_rms, attn_gains,
    )
    mix_other = core_swap(mix_own)

    keep1, up0, up1, far1, down0, down1 = after(grads1, hidden_blocks)
    came1a = [plane_shift(up0, 1, False), plane_shift(down0, 3, False)]
    hat, value_back, dots, head_parts = call(
        attend_back_kernel,
        [((SEQ, 512), F32), ((SEQ, 256), LOW), ((8, SEQ), F32), ((2, 256), F32)],
        qkv, scales, head_gains, *tables, low, mix_own, mix_other, near_mix, far_mix,
        scratch=[pltpu.VMEM((SEQ, HEAD), F32)] * 2 + [pltpu.VMEM((SEQ, 256), LOW)],
    )
    hat, dots, came1a, up1, down1 = lax.optimization_barrier((hat, dots, came1a, up1, down1))
    came1b = [plane_shift(up1, 1, False), plane_shift(down1, 3, False)]
    dots, came1b, far1 = lax.optimization_barrier((all_stats(dots), came1b, far1))
    came0[2] = plane_shift(after(grads0[2], dots), 2, False)
    came1 = plane_shift(far1, 2, False)
    (qkv_back,) = call(
        qkv_back_kernel, [((SEQ, SEQ), LOW)], hat, qkv, scales, dots, value_back
    )
    came = core_swap(qkv_down(qkv_back, 1, qkv_blocks, LOW))
    input_parts = settle_ordered(at, qkv_down(qkv_back, 0, qkv_blocks, F32), came)
    input_parts, qkv_back = lax.optimization_barrier((input_parts, qkv_back))

    input_sum = lax.psum_scatter(input_parts, "z", scatter_dimension=0, tiled=True)
    attn_grads = weight_grad(
        at.columns,
        [states, qkv_back, mix_own, mix_other, mixed],
        [(0, SEQ, [(0, 1, 0)]), (0, 256, [(2, 4, 0), (3, 4, OWN)])],
        [attn_gain_part, ffn_gain_part, jnp.pad(head_parts.reshape(16, 32), ((0, 0), (0, 96)))],
    )
    input_sum, attn_grads = lax.optimization_barrier((input_sum, attn_grads))
    input_low = (input_sum.astype(F32) + hidden_rows).astype(LOW)
    near, far = input_low[:, :NEAR], input_low[:, NEAR:]
    flip = at.c == 1
    input_sent = [jnp.where(flip, far, near), jnp.where(flip, near, far)]
    input_rows = shuffled_of(at, input_sent, shuffle(input_sent))
    input_rows, attn_grads, came0, came1 = lax.optimization_barrier(
        (jnp.concatenate(input_rows), attn_grads, came0, came1)
    )
    input_rows = lax.all_gather(input_rows, "z", axis=0, tiled=True)
    attn_came = [plane_shift(attn_grads[i], i, False) for i in range(1, RING)]
    steps = jnp.arange(8, dtype=jnp.int32)
    from_part = at.s ^ at.c ^ (steps // RING)
    from_z = (at.z - steps) % RING
    block_out = order_rows(
        at, shuffled_of(at, sent, after(shuffled, input_low)), from_z, from_part
    )
    (input_grad,) = call(
        widen_kernel, [((SEQ, NEAR), F32)],
        (steps % RING * 2 + from_part).astype(jnp.int32), input_rows,
        scalars=1,
    )

    block_out, came0, came1, came1a, came1b = lax.optimization_barrier(
        (block_out, came0, came1, came1a, came1b)
    )
    rows0 = plane_sum(grads0[0], [came0[i] for i in (1, 2, 3)])
    came1b = [jnp.concatenate(halves, axis=1) for halves in zip(came1a, came1b)]
    rows1 = plane_sum(keep1, [*came1b, came1])
    attn_came, rows0, rows1 = lax.optimization_barrier((attn_came, rows0, rows1))
    ffn_rows = [jnp.concatenate(rows) for rows in zip(rows0, rows1)]
    ffn_came = [plane_shift(ffn_rows[i], i, True) for i in range(1, RING)]
    attn_rows = plane_sum(attn_grads[0], attn_came)
    attn_came = [plane_shift(attn_rows[i], i, True) for i in range(1, RING)]
    attn_came, ffn_came, input_grad = lax.optimization_barrier((attn_came, ffn_came, input_grad))
    gate_out, up_out, down_out = share_cores(
        at,
        ffn_rows[0],
        ffn_came,
        [[(0, 0, 1024)], [(0, 1024, 512), (1, 0, 512)], [(1, 512, 1024)]],
    )
    query, key, value, mix_out, width, heads = share_cores(
        at, attn_rows[0], attn_came, [[(0, i, 256)] for i in range(0, 1024, 256)],
        [(8, 128), (16, 128)],
    )
    width = jnp.where(flip, width[:2, 64:], width[:2, :64])
    heads = jnp.where(at.s == 0, heads[2:4, :32], heads[10:12, :32])
    heads = jnp.where(flip, heads[:, 16:], heads[:, :16])

    return (
        block_out, input_grad, query, key, value, mix_out, gate_out, up_out, down_out,
        width[0], width[1], heads[0], heads[1],
    )


def solution(mesh):
    fine = Mesh(mesh.devices.reshape(4, 2, 2, 4, 2), ("y", "xh", "core", "z", "xl"))
    dp = ("y", "xh", "core")
    row, col = "z", "xl"
    return jax.shard_map(
        local,
        mesh=fine,
        in_specs=(
            P(dp, col), P(dp), P(col, row), P(col, row), P(col, row), P(row, col),
            P(col, row), P(col, row), P(row, col), P(col), P(col), P((row, col)),
            P((row, col)), P(dp, col),
        ),
        out_specs=(
            P(dp, col), P(dp, col),
            P((col,) + dp, row), P((col,) + dp, row), P((col,) + dp, row), P(row, (col,) + dp),
            P((col,) + dp, row), P((col,) + dp, row), P(row, (col,) + dp),
            P((col,) + dp), P((col,) + dp), P((row, col) + dp), P((row, col) + dp),
        ),
        check_vma=False,
    )
```

```python
import functools

import jax
import jax.numpy as jnp
from jax import lax
from jax.experimental import pallas as pl
from jax.experimental.pallas import tpu as pltpu
from jax.sharding import Mesh, PartitionSpec as P

D = 2048
HEAD = 128
SEQ = 768
NEAR = D // 2
OWN = SEQ // 2
RING = 4
BLOCK = SEQ // 8
EPSILON = 1e-06
ROPE_BASE = 500000.0
MASKED = -1e30
LOW = jnp.bfloat16
F32 = jnp.float32
FREE = pl.CostEstimate(flops=0, bytes_accessed=0, transcendentals=0)
PARAMS = pltpu.CompilerParams(vmem_limit_bytes=24 * 1024 * 1024)
EARLY = pltpu.CompilerParams(vmem_limit_bytes=60 * 1024 * 1024)


def dot(a, b, dims=((1,), (0,))):
    return lax.dot_general(a, b, (dims, ((), ())), preferred_element_type=F32)


NT = ((1,), (1,))
TN = ((0,), (0,))


def after(value, *earlier):
    return lax.optimization_barrier((value, earlier))[0]


def ring_shift(a, axes, step):
    return lax.ppermute(a, axes, [(i, (i + step) % RING) for i in range(RING)])


def z_shift(a, step):
    return ring_shift(a, "z", step)


def plane_shift(a, step, swapped):
    pairs = []
    for y in range(4):
        for x in range(4):
            for c in range(2):
                there = ((y + step) % 4, x) if (c == 0) != swapped else (y, (x + step) % 4)
                xh, xl = x // 2, x % 2
                source = ((y * 2 + xh) * 2 + c) * 2 + xl
                pairs.append((source, ((there[0] * 2 + there[1] // 2) * 2 + c) * 2 + there[1] % 2))
    return lax.ppermute(a, ("y", "xh", "core", "xl"), pairs)


def core_swap(a):
    return lax.ppermute(a, "core", [(0, 1), (1, 0)])


def pair_swap(a):
    return lax.ppermute(a, "xl", [(0, 1), (1, 0)])


def wrap_swap(a):
    return lax.ppermute(a, ("xh", "xl"), [(0, 3), (3, 0), (1, 2), (2, 1)])


def pick(blocks, index, axis=0):
    return lax.dynamic_index_in_dim(blocks, index, axis, keepdims=False)


class Place:
    def __init__(self):
        self.s = lax.axis_index("xl")
        self.xh = lax.axis_index("xh")
        self.x = self.xh * 2 + self.s
        self.y = lax.axis_index("y")
        self.c = lax.axis_index("core")
        self.z = lax.axis_index("z")
        self.home = self.c == self.s
        self.z_scalar = self.z.reshape(1).astype(jnp.int32)
        steps = jnp.arange(RING, dtype=jnp.int32)
        self.back = (self.z - steps) % RING
        self.rows = jnp.concatenate([self.c * 4 + self.back, (1 - self.c) * 4 + self.back])
        first, second = steps[:, None], steps[None, :]
        dx = jnp.where(self.c == 0, second, first)
        dy = jnp.where(self.c == 0, first, second)
        self.columns = (
            (dx % 2) * 8 + ((self.y + dy) % 4) * 2 + ((self.x + dx) % 4) // 2
        ).reshape(-1)
        y, x = first, second
        self.plain = (((x % 2) ^ self.s) * 8 + y * 2 + x // 2).reshape(-1)


def place_kernel(plan, sources, table, *refs):
    ins, outs, sems = refs[:sources], refs[sources:-1], refs[-1]
    copies = []
    for i, (source, there) in enumerate(plan(table, ins, outs)):
        copies.append(pltpu.make_async_copy(source, there, sems.at[i]))
        copies[-1].start()
    for copy in copies:
        copy.wait()


def place(plan, count, shapes, table, *sources, params=PARAMS):
    return pl.pallas_call(
        functools.partial(place_kernel, plan, len(sources)),
        in_specs=[pl.BlockSpec(memory_space=pltpu.SMEM)]
        + [pl.BlockSpec(memory_space=pltpu.HBM)] * len(sources),
        out_specs=tuple(pl.BlockSpec(memory_space=pltpu.VMEM) for _ in shapes),
        out_shape=tuple(jax.ShapeDtypeStruct(shape, LOW) for shape in shapes),
        scratch_shapes=[pltpu.SemaphoreType.DMA((count,))],
        compiler_params=params,
        cost_estimate=FREE,
    )(jnp.stack(table).astype(jnp.int32), *sources)


def at_block(index, size):
    return pl.ds(pl.multiple_of(index * size, size), size)


def first_hop(a):
    return lax.ppermute(a, ("core", "xl"), [(0, 2), (3, 1), (2, 3), (1, 0)])


def second_hop(first):
    return lax.ppermute(first, ("core", "xl"), [(0, 2), (3, 1)])


def sequence_kernel(count, table, a_ref, first_ref, second_ref, out_ref, sems):
    def move(near, far):
        copies = []
        for i in range(count):
            block = at_block(table[i], BLOCK)
            there = pl.ds(i * BLOCK, BLOCK)
            for source, lo in ((near.at[block], 0), (far.at[block], NEAR)):
                copies.append(
                    pltpu.make_async_copy(
                        source, out_ref.at[there, pl.ds(lo, NEAR)], sems.at[len(copies)]
                    )
                )
        for copy in copies:
            copy.start()
        for copy in copies:
            copy.wait()

    pl.when(table[count] == 1)(functools.partial(move, a_ref, first_ref))
    pl.when(table[count] == 0)(functools.partial(move, first_ref, second_ref))


def to_sequence(at, a, first, second, count=8):
    table = jnp.concatenate([at.rows[:count], at.home[None].astype(jnp.int32)])
    return pl.pallas_call(
        functools.partial(sequence_kernel, count),
        in_specs=[pl.BlockSpec(memory_space=pltpu.SMEM)]
        + [pl.BlockSpec(memory_space=pltpu.HBM)] * 3,
        out_specs=pl.BlockSpec(memory_space=pltpu.VMEM),
        out_shape=jax.ShapeDtypeStruct((count * BLOCK, D), LOW),
        scratch_shapes=[pltpu.SemaphoreType.DMA((2 * count,))],
        compiler_params=PARAMS,
        cost_estimate=FREE,
    )(table.astype(jnp.int32), a, first, second)


def order_rows(at, sources, index, which):
    joined = jnp.concatenate(sources) if len(sources) > 1 else sources[0]
    rows = sources[0].shape[0] // BLOCK

    def plan(table, ins, outs):
        return [
            (ins[0].at[at_block(table[i], BLOCK)], outs[0].at[pl.ds(i * BLOCK, BLOCK)])
            for i in range(8)
        ]

    table = index + rows * which if len(sources) > 1 else index * 2 + which
    return place(plan, 8, [(SEQ, joined.shape[1])], list(table), joined)[0]


def cut_columns(at, heights, *weights):
    width = weights[0].shape[1] // 2
    starts = [sum(heights[:i]) for i in range(len(heights))]

    def plan(table, ins, outs):
        return [
            (
                ref.at[pl.ds(start, height), at_block(table[0], width)],
                out.at[:, pl.ds(width * i, width)],
            )
            for i, ref in enumerate(ins)
            for start, height, out in zip(starts, heights, outs)
        ]

    shapes = [(height, width * len(weights)) for height in heights]
    return place(plan, len(heights) * len(weights), shapes, [at.c], *weights, params=EARLY)


PIECES = (
    (("gate", 0), ("mix", 0)), (("gate", 1), ("mix", 1)),
    (("gate", 2), ("up", 0)), (("gate", 3), ("up", 1)),
    (("up", 2), ("down", 0)), (("up", 3), ("down", 1)),
    (("down", 2),), (("down", 3),),
)
PART = 256


def part_height(name):
    return 128 if name == "mix" else PART


def part_starts(piece):
    heights = [part_height(name) for name, _ in piece]
    return [sum(heights[:i]) for i in range(len(heights) + 1)]


def cut_pieces(at, w_gate, w_up, w_down, w_mix):
    def plan(table, ins, outs):
        named = dict(zip(("gate", "up", "down", "mix"), ins))
        copies = []
        for out, piece in zip(outs, PIECES):
            for start, (name, part) in zip(part_starts(piece), piece):
                height = part_height(name)
                if name in ("down", "mix"):
                    half = named[name].shape[0] // 2
                    first = pl.multiple_of(table[0] * half + height * part, height)
                    source = named[name].at[pl.ds(first, height)]
                else:
                    rows = pl.ds(height * part, height)
                    source = named[name].at[rows, at_block(table[0], NEAR)]
                copies.append((source, out.at[pl.ds(start, height)]))
        return copies

    shapes = [(part_starts(piece)[-1], NEAR) for piece in PIECES]
    count = sum(len(piece) for piece in PIECES)
    return place(plan, count, shapes, [at.c], w_gate, w_up, w_down, w_mix, params=EARLY)


def pieces_with(name):
    return [k for k, piece in enumerate(PIECES) if name in dict(piece)]


def views(name, refs):
    out = []
    for ref, k in zip(refs, pieces_with(name)):
        for start, (found, _) in zip(part_starts(PIECES[k]), PIECES[k]):
            if found == name:
                out.append(ref.at[pl.ds(start, part_height(name))])
    return out


def join_columns(parts):
    starts = [sum(part.shape[1] for part in parts[:i]) for i in range(len(parts) + 1)]

    def plan(table, ins, outs):
        return [
            (ref, outs[0].at[:, pl.ds(starts[i], parts[i].shape[1])]) for i, ref in enumerate(ins)
        ]

    return place(plan, len(parts), [(D, starts[-1])], [0], *parts)[0]


def fetch(first, second):
    return pair_swap(first), wrap_swap(second)


def scatter_z(parts):
    total = parts[0]
    for i in range(1, RING):
        total = total + z_shift(parts[i], -i).astype(F32)
    return total


def gather_z(rows):
    return [rows] + [z_shift(rows, i) for i in range(1, RING)]


def all_stats(pair):
    theirs = core_swap(pair)
    pair = pair + jnp.concatenate([theirs[:, OWN:], theirs[:, :OWN]], axis=1)
    total = pair
    for i in range(1, RING):
        came, cut = z_shift(pair, i), OWN - i * BLOCK
        total = total + jnp.concatenate(
            [came[:, cut:OWN], came[:, :cut], came[:, OWN + cut :], came[:, OWN : OWN + cut]],
            axis=1,
        )
    return total


def plane_sum(own, came):
    total = own.astype(F32) + came[0].astype(F32) + came[1].astype(F32) + came[2].astype(F32)
    total = lax.optimization_barrier(total.astype(LOW))
    height = own.shape[0] // RING
    return [total[height * i : height * (i + 1)] for i in range(RING)]


def sum_kernel(p0, p1, p2, p3, *outs):
    for i, out in enumerate(outs):
        at = slice(128 * i, 128 * (i + 1))
        total = p0[at, :].astype(F32) + p1[at, :].astype(F32)
        out[...] = (total + p2[at, :].astype(F32) + p3[at, :].astype(F32)).astype(LOW)


def plane_parts(own, came):
    return call(sum_kernel, [((128, own.shape[1]), LOW)] * RING, own, *came)


def share_kernel(core, p0, p1, p2, p3, own_ref, sent_ref):
    total = p0[...].astype(F32) + p1[...].astype(F32) + p2[...].astype(F32) + p3[...].astype(F32)
    flip = core[0] == 1
    for i in range(total.shape[0] // 128):
        at = slice(64 * i, 64 * (i + 1))
        low, high = total[128 * i : 128 * i + 64, :], total[128 * i + 64 : 128 * (i + 1), :]
        own_ref[at, :] = jnp.where(flip, high, low)
        sent_ref[at, :] = jnp.where(flip, low, high).astype(LOW)
    rest = total.shape[0] % 128
    if rest:
        own_ref[-rest:, :] = total[-rest:, :]
        sent_ref[-rest:, :] = total[-rest:, :].astype(LOW)


def wide_kernel(plan, core, own_ref, came_ref, *outs):
    first = core[0] == 0
    own, came = own_ref[...], came_ref[...].astype(F32)
    sides = jnp.where(first, own, came), jnp.where(first, came, own)
    for out, pieces in zip(outs, plan):
        at = 0
        for side in sides:
            for rows, start, width in pieces:
                value = side[64 * rows : 64 * (rows + 1), start : start + width]
                out[:, at : at + width] = value
                at += width
    if len(outs) > len(plan):
        width_ref, heads_ref = outs[len(plan) :]
        zero, one = (side[-16:-8, :128] for side in sides)
        width_ref[...] = zero + one
        heads_ref[0:8, :] = zero
        heads_ref[8:16, :] = one


def share_cores(at, own, came, plan, extra=()):
    height, width = own.shape
    shape = (height // 128 * 64 + height % 128, width)
    core = at.c.reshape(1).astype(jnp.int32)
    own, sent = call(share_kernel, [(shape, F32), (shape, LOW)], core, own, *came, scalars=1)
    widths = [2 * sum(piece[2] for piece in pieces) for pieces in plan]
    shapes = [((64, width), F32) for width in widths]
    shapes += [(shape, F32) for shape in extra]
    return call(functools.partial(wide_kernel, plan), shapes, core, own, core_swap(sent), scalars=1)


def call(kernel, shapes, *args, scratch=(), scalars=0):
    return pl.pallas_call(
        kernel,
        in_specs=[
            pl.BlockSpec(memory_space=pltpu.SMEM if i < scalars else pltpu.VMEM)
            for i in range(len(args))
        ],
        out_shape=tuple(jax.ShapeDtypeStruct(shape, dtype) for shape, dtype in shapes),
        scratch_shapes=list(scratch),
        compiler_params=PARAMS,
        cost_estimate=FREE,
    )(*args)


def row_dot(rows, refs, at):
    value = 0.0
    start = 0
    for ref in refs:
        height = ref.shape[0]
        value += dot(rows[:, start : start + height], ref[:, at])
        start += height
    return value


def strips(width, size):
    return [slice(i, i + size) for i in range(0, width, size)]


def as_rows(first, second):
    return jnp.concatenate([first, second, jnp.zeros((SEQ, 6), F32)], axis=1).T


def qkv_kernel(states_ref, *refs):
    *blocks, qkv_ref, sums_ref = refs
    sums = []
    for at in strips(SEQ, 256):
        value = row_dot(states_ref, blocks, at)
        qkv_ref[:, at] = value
        sums.append(jnp.sum(value * value, axis=1, keepdims=True))
    sums_ref[...] = as_rows(*sums[:2])


def product_kernel(body, *refs):
    *refs, out_ref = refs
    for at, value in body(refs):
        out_ref[:, at] = value.astype(out_ref.dtype)


def product(body, dtype, *args):
    return call(functools.partial(product_kernel, body), [((OWN, D), dtype)], *args)[0]


def half_rows(ref, half):
    return ref[OWN * half : OWN * (half + 1), :]


def mix(left, half, pieces, dtype):
    count = len(pieces) // 2

    def body(refs):
        left, *w = refs
        left = half_rows(left, half)
        for i in range(2):
            blocks = views("mix", w[count * i : count * (i + 1)])
            for at in strips(NEAR, 512):
                yield slice(NEAR * i + at.start, NEAR * i + at.stop), row_dot(left, blocks, at)

    return product(body, dtype, left, *pieces)


def down(units, pieces, dtype):
    count = len(pieces) // 2

    def body(refs):
        units, *w = refs
        for i in range(2):
            blocks = views("down", w[count * i : count * (i + 1)])
            for at in strips(NEAR, 512):
                yield slice(NEAR * i + at.start, NEAR * i + at.stop), row_dot(units, blocks, at)

    return product(body, dtype, units, *pieces)


def pair_down(gate_back, up_back, gates, ups, dtype):
    def body(refs):
        gate_back, up_back, *w = refs
        for i in range(2):
            n, m = len(gates) // 2, len(ups) // 2
            gate = views("gate", w[n * i : n * (i + 1)])
            up = views("up", w[2 * n + m * i : 2 * n + m * (i + 1)])
            for k in range(4):
                value = dot(gate_back[...], gate[k][...], NT) + dot(up_back[...], up[k][...], NT)
                yield slice(NEAR * i + PART * k, NEAR * i + PART * (k + 1)), value

    return product(body, dtype, gate_back, up_back, *gates, *ups)


def qkv_down(back, half, blocks, dtype):
    def body(refs):
        back, *w = refs
        back = half_rows(back, half)
        start = 0
        for ref in w:
            for at in strips(ref.shape[0], 256):
                yield slice(start + at.start, start + at.stop), dot(back, ref[at, :], NT)
            start += ref.shape[0]

    return product(body, dtype, back, *blocks)


def settle_kernel(own_ref, came_ref, *outs):
    for i, ref in enumerate(outs):
        at = slice(i * BLOCK, (i + 1) * BLOCK)
        ref[...] = (own_ref[at, :] + came_ref[at, :].astype(F32)).astype(ref.dtype)


def settle(own, came):
    return call(
        settle_kernel, [((BLOCK, D), F32)] + [((BLOCK, D), LOW)] * 3, own, came
    )


def z_rows(z, i):
    return pl.ds(pl.multiple_of(lax.rem(z + RING - i, RING) * BLOCK, BLOCK), BLOCK)


def settle_ordered_kernel(z_ref, own_ref, came_ref, out_ref):
    for i in range(RING):
        at = slice(i * BLOCK, (i + 1) * BLOCK)
        value = own_ref[at, :] + came_ref[at, :].astype(F32)
        out_ref[z_rows(z_ref[0], i), :] = value.astype(LOW)


def settle_ordered(at, own, came):
    return call(settle_ordered_kernel, [((OWN, D), LOW)], at.z_scalar, own, came, scalars=1)[0]


def units_kernel(n, m, rows_ref, *refs):
    gate_ref, up_ref, units_ref = refs[-3:]
    gates = views("gate", refs[:n]) + views("gate", refs[n : 2 * n])
    ups = views("up", refs[2 * n : 2 * n + m]) + views("up", refs[2 * n + m : 2 * n + 2 * m])
    for at in strips(1024, 512):
        gate, up = row_dot(rows_ref, gates, at), row_dot(rows_ref, ups, at)
        gate_ref[:, at] = gate.astype(LOW)
        up_ref[:, at] = up.astype(LOW)
        units_ref[:, at] = (gate * jax.nn.sigmoid(gate) * up).astype(LOW)


def units_of(rows, gates, ups):
    kernel = functools.partial(units_kernel, len(gates) // 2, len(ups) // 2)
    return call(kernel, [((OWN, 1024), LOW)] * 3, rows, *gates, *ups)


def units_back_kernel(branch_ref, *refs):
    *w, gate_ref, up_ref, gate_back_ref, up_back_ref = refs
    count = len(w) // 2
    near, far = views("down", w[:count]), views("down", w[count:])
    for k in range(4):
        at = slice(PART * k, PART * (k + 1))
        grad = dot(branch_ref[:, :NEAR], near[k][...], NT)
        grad += dot(branch_ref[:, NEAR:], far[k][...], NT)
        gate, up = gate_ref[:, at].astype(F32), up_ref[:, at].astype(F32)
        sigmoid = jax.nn.sigmoid(gate)
        gate_back_ref[:, at] = (grad * up * sigmoid * (1.0 + gate * (1.0 - sigmoid))).astype(LOW)
        up_back_ref[:, at] = (grad * gate * sigmoid).astype(LOW)


def units_back(branch, pieces, gate, up):
    return call(units_back_kernel, [((OWN, 1024), LOW)] * 2, branch, *pieces, gate, up)


def grad_kernel(plan, count, extras, cut, *refs):
    table, ins = refs[0], refs[1 : 1 + count]
    extra, outs = refs[1 + count : 1 + count + extras], refs[1 + count + extras :]
    if cut:
        outs = [(outs[0],), outs[1:3], (outs[3],), outs[4:6]]
    for d in range(RING):
        blocks = [table[4 * d + e] for e in range(RING)]
        places = [at_block(block, 128) for block in blocks]
        start = 0
        for lo, width, terms in plan:
            value = 0.0
            for left, right, row in terms:
                left, right = ins[left], ins[right]
                chosen = jnp.concatenate([left[:, place] for place in places], axis=1)
                value += dot(chosen, right[row : row + left.shape[0], lo : lo + width], TN)
            value = value.astype(LOW)
            at = slice(start, start + width)
            if cut:
                put_columns(outs[d], start, value)
            elif not extras:
                outs[d][:, at] = value
            else:
                for e in range(RING):
                    outs[d][144 * e : 144 * e + 128, at] = value[128 * e : 128 * (e + 1)]
            start += width
        if extras:
            attn_ref, ffn_ref, heads_ref = extra
            for e in range(RING):
                block = lax.rem(blocks[e], 8)
                rows = [attn_ref[0:1, places[e]], ffn_ref[0:1, places[e]]]
                rows += [heads_ref[pl.ds(block + 8 * i, 1), :] for i in range(2)]
                rows = jnp.concatenate([*rows, jnp.zeros((12, 128), F32)])
                at = slice(144 * e + 128, 144 * (e + 1))
                outs[d][at, :128] = rows.astype(LOW)
                outs[d][at, 128:] = jnp.zeros((16, start - 128), LOW)


def put_columns(outs, start, value):
    at = 0
    for out in outs:
        lo, hi = max(start, at), min(start + value.shape[1], at + out.shape[1])
        if lo < hi:
            out[:, lo - at : hi - at] = value[:, lo - start : hi - start]
        at += out.shape[1]


def weight_grad(table, arrays, plan, extra=(), cut=False):
    width = sum(span[1] for span in plan)
    height = 576 if extra else 512
    kernel = functools.partial(grad_kernel, plan, len(arrays), len(extra), cut)
    widths = [width, width // 2, width // 2, width, width // 2, width // 2] if cut else [width] * RING
    outs = [((height, w), LOW) for w in widths]
    return call(kernel, outs, table.astype(jnp.int32), *arrays, *extra, scalars=1)


def turn(v, cosines, sines):
    return v * cosines + pltpu.roll(v, HEAD // 2, 1) * sines


def turn_back(v, cosines, sines):
    return v * cosines - pltpu.roll(v, HEAD // 2, 1) * sines


TILE = 384


def seen(table_ref, row_ref, lo):
    here = table_ref[lo : lo + TILE, 2 * HEAD : 3 * HEAD]
    there = row_ref[0:1, :]
    return (there <= here[:, 0:1]) & (there >= here[:, 1:2])


def attend_kernel(
    qkv_ref, sums_ref, gain_ref, table_ref, row_ref, mixed_ref, low_ref, scale_ref
):
    cosines, sines = table_ref[:, :HEAD], table_ref[:, HEAD : 2 * HEAD]
    scale_ref[...] = lax.rsqrt(sums_ref[...] * (1.0 / D) + EPSILON).T
    for h in range(2):
        at = slice(h * HEAD, (h + 1) * HEAD)
        k_at = slice(256 + h * HEAD, 256 + (h + 1) * HEAD)
        q = qkv_ref[:, at] * scale_ref[:, 0:1] * gain_ref[0:1, at]
        k = qkv_ref[:, k_at] * scale_ref[:, 1:2] * gain_ref[1:2, at]
        low_ref[:, at] = turn(q, cosines, sines).astype(LOW)
        k = turn(k, cosines, sines).astype(LOW)
        v = qkv_ref[:, 512 + h * HEAD : 512 + (h + 1) * HEAD].astype(LOW)
        low_ref[:, k_at] = k
        low_ref[:, 512 + h * HEAD : 512 + (h + 1) * HEAD] = v
        for lo in range(0, SEQ, TILE):
            q = low_ref[lo : lo + TILE, at]
            scores = dot(q, k, NT) * HEAD**-0.5
            scores = jnp.where(seen(table_ref, row_ref, lo), scores, MASKED)
            peak = jnp.max(scores, axis=1, keepdims=True)
            weights = jnp.exp(scores - peak)
            total = jnp.sum(weights, axis=1, keepdims=True)
            weights = (weights * (1.0 / total)).astype(LOW)
            mixed_ref[lo : lo + TILE, at] = dot(weights, v).astype(LOW)
            scale_ref[lo : lo + TILE, 2 + h : 3 + h] = peak + jnp.log(total)


def attend_back_kernel(
    qkv_ref, scale_ref, gain_ref, table_ref, row_ref, low_ref,
    own_ref, other_ref, near0, near1, far0, far1,
    hat_ref, value_ref, dots_ref, part_ref, dk_ref, dv_ref, grad_ref,
):
    cosines, sines = table_ref[:, :HEAD], table_ref[:, HEAD : 2 * HEAD]
    for i, ref in enumerate((own_ref, other_ref)):
        pairs = zip(views("mix", (near0, near1)), views("mix", (far0, far1)))
        for k, (near, far) in enumerate(pairs):
            grad = dot(ref[:, :NEAR], near[...], NT) + dot(ref[:, NEAR:], far[...], NT)
            grad_ref[OWN * i : OWN * (i + 1), 128 * k : 128 * (k + 1)] = grad.astype(LOW)
    for h in range(2):
        at = slice(h * HEAD, (h + 1) * HEAD)
        k_at = slice(256 + h * HEAD, 256 + (h + 1) * HEAD)
        k = low_ref[:, k_at]
        v = low_ref[:, 512 + h * HEAD : 512 + (h + 1) * HEAD]
        for lo in range(0, SEQ, TILE):
            q = low_ref[lo : lo + TILE, at]
            grad = grad_ref[lo : lo + TILE, at]
            scores = dot(q, k, NT) * HEAD**-0.5
            weights = jnp.exp(scores - scale_ref[lo : lo + TILE, 2 + h : 3 + h])
            weights = jnp.where(seen(table_ref, row_ref, lo), weights, 0.0)
            weight_grad = dot(grad, v, NT)
            centre = jnp.sum(weights * weight_grad, axis=1, keepdims=True)
            score_grad = (weights * (weight_grad - centre)).astype(LOW)
            hat_ref[lo : lo + TILE, at] = dot(score_grad, k) * HEAD**-0.5
            value_part = dot(weights.astype(LOW), grad, TN)
            key_part = dot(score_grad, q, TN)
            if lo == 0:
                dv_ref[...] = value_part
                dk_ref[...] = key_part
            else:
                dv_ref[...] += value_part
                dk_ref[...] += key_part
        value_ref[:, at] = dv_ref[...].astype(LOW)
        q_grad = turn_back(hat_ref[:, at], cosines, sines)
        k_grad = turn_back(dk_ref[...] * HEAD**-0.5, cosines, sines)
        q, k = qkv_ref[:, at], qkv_ref[:, k_at]
        part_ref[0:1, at] = jnp.sum(q_grad * q * scale_ref[:, 0:1], axis=0, keepdims=True)
        part_ref[1:2, at] = jnp.sum(k_grad * k * scale_ref[:, 1:2], axis=0, keepdims=True)
        hat_ref[:, at] = q_grad * gain_ref[0:1, at]
        hat_ref[:, k_at] = k_grad * gain_ref[1:2, at]
    dots_ref[...] = as_rows(
        jnp.sum(hat_ref[:, :256] * qkv_ref[:, :256], axis=1, keepdims=True),
        jnp.sum(hat_ref[:, 256:] * qkv_ref[:, 256:512], axis=1, keepdims=True),
    )


def qkv_back_kernel(hat_ref, qkv_ref, rms_ref, dots_ref, value_ref, out_ref):
    dots = dots_ref[...].T
    for i in range(2):
        at = slice(i * 256, (i + 1) * 256)
        rms = rms_ref[:, i : i + 1]
        coefficient = rms * rms * rms * dots[:, i : i + 1] * (1.0 / D)
        out_ref[:, at] = (rms * hat_ref[:, at] - qkv_ref[:, at] * coefficient).astype(LOW)
    out_ref[:, 512:] = value_ref[...]


def widen_kernel(table, rows_ref, out_ref):
    for i in range(8):
        block = pl.ds(pl.multiple_of(table[i] * BLOCK, BLOCK), BLOCK)
        out_ref[i * BLOCK : (i + 1) * BLOCK, :] = rows_ref[block, :].astype(F32)


def blocks_of(ref):
    return [slice(i * BLOCK, (i + 1) * BLOCK) for i in range(ref.shape[0] // BLOCK)]


def hidden_kernel(b0, b1, b2, b3, states_ref, gain_ref, low_ref, rms_ref):
    for at, ref in zip(blocks_of(low_ref), (b0, b1, b2, b3)):
        branch = ref[...].astype(F32)
        rms = lax.rsqrt(jnp.mean(branch * branch, axis=1, keepdims=True) + EPSILON)
        hidden = states_ref[at, :].astype(F32) + gain_ref[...] * branch * rms
        low_ref[at, :] = hidden.astype(LOW)
        rms_ref[at, :] = rms


def back_of(upstream, branch, rms, gain):
    part = jnp.sum(upstream * branch * rms, axis=0, keepdims=True)
    scaled = upstream * gain
    inner = jnp.sum(scaled * branch, axis=1, keepdims=True)
    return rms * scaled - branch * (rms * rms * rms * inner * (1.0 / D)), part


def ffn_back_kernel(b0, b1, b2, b3, upstream_ref, gain_ref, back_ref, rms_ref, part_ref):
    for i, (at, ref) in enumerate(zip(blocks_of(back_ref), (b0, b1, b2, b3))):
        branch = ref[...].astype(F32)
        rms = lax.rsqrt(jnp.mean(branch * branch, axis=1, keepdims=True) + EPSILON)
        back, part = back_of(upstream_ref[at, :].astype(F32), branch, rms, gain_ref[...])
        back_ref[at, :] = back.astype(LOW)
        rms_ref[at, :] = rms
        part_ref[...] = part if i == 0 else part_ref[...] + part


def attn_back_kernel(
    g0, g1, g2, g3, b0, b1, b2, b3, upstream_ref, rms_ref, gain_ref, back_ref, part_ref
):
    pairs = zip(blocks_of(back_ref), (g0, g1, g2, g3), (b0, b1, b2, b3))
    for i, (at, grad_ref, ref) in enumerate(pairs):
        grad = grad_ref[...].astype(F32) + upstream_ref[at, :].astype(F32)
        back, part = back_of(grad, ref[...].astype(F32), rms_ref[at, :], gain_ref[...])
        back_ref[at, :] = back.astype(LOW)
        part_ref[...] = part if i == 0 else part_ref[...] + part


def out_kernel(
    core_ref, a0, a1, a2, a3, b0, b1, b2, b3, states_ref, attn_rms_ref, ffn_rms_ref,
    attn_gain_ref, ffn_gain_ref, sent0_ref, sent1_ref,
):
    pairs = zip(blocks_of(states_ref), (a0, a1, a2, a3), (b0, b1, b2, b3))
    flip = core_ref[0] == 1
    for at, a_ref, b_ref in pairs:
        value = (
            states_ref[at, :].astype(F32)
            + attn_gain_ref[...] * a_ref[...].astype(F32) * attn_rms_ref[at, :]
            + ffn_gain_ref[...] * b_ref[...].astype(F32) * ffn_rms_ref[at, :]
        ).astype(LOW)
        near, far = value[:, :NEAR], value[:, NEAR:]
        sent0_ref[at, :] = jnp.where(flip, far, near)
        sent1_ref[at, :] = jnp.where(flip, near, far)


def shuffle(sent):
    out = []
    for k in range(2):
        perm = [(c * 2 + s, s * 2 + (s ^ c ^ k)) for s in range(2) for c in range(2)]
        out.append(lax.ppermute(sent[k], ("core", "xl"), [p for p in perm if p[0] != p[1]]))
    return out


def shuffled_of(at, sent, came):
    return [jnp.where((at.s == k) & (at.c == k), sent[k], came[k]) for k in range(2)]


def local(
    inputs, segments, w_query, w_key, w_value, w_mix, w_gate, w_up, w_down,
    attn_gain, ffn_gain, query_gain, key_gain, out_grad,
):
    at = Place()
    first = first_hop(inputs)
    near_qkv = cut_columns(at, (768, 256), w_query, w_key, w_value)
    far_qkv = [wrap_swap(near_qkv[0]), pair_swap(near_qkv[1])]
    near = cut_pieces(at, after(w_gate, near_qkv), w_up, w_down, w_mix)

    gains = jnp.concatenate([attn_gain, ffn_gain, query_gain, key_gain])
    their_gains = pair_swap(gains)
    attn_gains = jnp.concatenate([attn_gain, their_gains[:NEAR]])[None]
    ffn_gains = jnp.concatenate([ffn_gain, their_gains[NEAR:D]])[None]
    head_gains = jnp.where(at.home, gains[D:], their_gains[D:]).reshape(2, 256)

    segment_ids = jnp.where(at.home, segments, core_swap(segments))
    step_index = jnp.arange(SEQ, dtype=jnp.int32)
    earlier = jnp.concatenate([segment_ids[:1] - 1, segment_ids[:-1]])
    begins = lax.cummax(jnp.where(segment_ids != earlier, step_index, 0))
    chosen = at.rows[:, None, None] == jnp.arange(8, dtype=jnp.int32)[None, :, None]
    begins = jnp.sum(jnp.where(chosen, begins.reshape(1, 8, BLOCK), 0), axis=1).reshape(-1)
    index = (at.rows[:, None] * BLOCK + jnp.arange(BLOCK, dtype=jnp.int32)[None]).reshape(-1)
    frequency = ROPE_BASE ** (-2.0 * jnp.arange(HEAD // 2, dtype=F32) / HEAD)
    angles = (index - begins).astype(F32)[:, None] * frequency
    cosines, sines = jnp.cos(angles), jnp.sin(angles)
    place_columns = jnp.stack([index, begins], axis=1).astype(F32)
    table = jnp.concatenate(
        [cosines, cosines, -sines, sines, jnp.pad(place_columns, ((0, 0), (0, 126)))], axis=1
    )
    tables = (table, index[None].astype(F32))

    tables, head_gains, attn_gains, ffn_gains, at.columns, at.plain, at.rows, near, first = (
        lax.optimization_barrier(
            (tables, head_gains, attn_gains, ffn_gains, at.columns, at.plain, at.rows, near, first)
        )
    )
    states = to_sequence(at, inputs, first, second_hop(after(first, far_qkv)))
    states, far_qkv = lax.optimization_barrier((states, far_qkv))
    qkv_blocks = [*near_qkv, *far_qkv]
    qkv, squares = call(qkv_kernel, [((SEQ, SEQ), F32), ((8, SEQ), F32)], states, *qkv_blocks)
    far = fetch(*after(near[:2], far_qkv))
    squares = all_stats(squares)
    squares = lax.optimization_barrier(squares)
    mixed, low, scales = call(
        attend_kernel,
        [((SEQ, 256), LOW), ((SEQ, SEQ), LOW), ((SEQ, 8), F32)],
        qkv, squares, head_gains, *tables,
    )
    mixed, far = lax.optimization_barrier((mixed, far))
    mixes = [*near[:2], *far[:2]]
    came = core_swap(mix(mixed, 1, mixes, LOW))
    mix_parts = settle(mix(mixed, 0, mixes, F32), came)
    mix_parts = lax.optimization_barrier(mix_parts)
    far = [*far, *fetch(*after(near[2:4], mix_parts))]
    attn_sum = scatter_z(mix_parts).astype(LOW)
    attn_sum, far = lax.optimization_barrier((attn_sum, far))
    far = [*far, *fetch(*after(near[4:6], attn_sum))]
    attn_blocks = gather_z(attn_sum)
    own_states = after(states, attn_sum)[:OWN]
    attn_blocks, far, own_states = lax.optimization_barrier((attn_blocks, far, own_states))
    far = [*far, *fetch(*after(near[6:], attn_blocks))]
    hidden_own, attn_rms = call(
        hidden_kernel,
        [((OWN, D), LOW), ((OWN, 1), F32)],
        *attn_blocks, own_states, attn_gains,
    )
    hidden_other = core_swap(hidden_own)

    gates, ups, downs = (
        [side[k] for side in (near, far) for k in pieces_with(name)]
        for name in ("gate", "up", "down")
    )
    gate_own, up_own, units_own = units_of(hidden_own, gates, ups)
    hidden_other = after(hidden_other, units_own)
    gate_other, up_other, units_other = units_of(hidden_other, gates, ups)
    came = core_swap(down(units_other, downs, LOW))
    ffn_parts = settle(down(after(units_own, units_other), downs, F32), came)
    ffn_parts = lax.optimization_barrier(ffn_parts)
    grad_first = first_hop(after(out_grad, ffn_parts))
    ffn_sum = scatter_z(ffn_parts).astype(LOW)
    ffn_sum, grad_first = lax.optimization_barrier((ffn_sum, grad_first))
    ffn_blocks = gather_z(ffn_sum)
    upstream = to_sequence(at, out_grad, grad_first, second_hop(grad_first), RING)
    ffn_blocks, upstream = lax.optimization_barrier((ffn_blocks, upstream))
    branch_own, ffn_rms, ffn_gain_part = call(
        ffn_back_kernel,
        [((OWN, D), LOW), ((OWN, 1), F32), ((1, D), F32)],
        *ffn_blocks, upstream, ffn_gains,
    )
    branch_other = core_swap(branch_own)
    gate_back_own, up_back_own = units_back(branch_own, downs, gate_own, up_own)
    sent = call(
        out_kernel,
        [((OWN, NEAR), LOW)] * 2,
        at.c.reshape(1).astype(jnp.int32), *attn_blocks, *ffn_blocks,
        own_states, attn_rms, after(ffn_rms, gate_back_own), attn_gains, ffn_gains,
        scalars=1,
    )
    branch_other = after(branch_other, gate_back_own, sent)
    gate_back_other, up_back_other = units_back(branch_other, downs, gate_other, up_other)
    came = core_swap(pair_down(gate_back_other, up_back_other, gates, ups, LOW))
    pair_parts = pair_down(after(gate_back_own, gate_back_other), up_back_own, gates, ups, F32)
    pair_parts = settle(pair_parts, came)

    hidden_sum = scatter_z(pair_parts)
    hidden_rows = hidden_sum + upstream[:BLOCK].astype(F32)
    branch_own, hidden_own, pair_parts = lax.optimization_barrier(
        (branch_own, hidden_own, pair_parts)
    )
    shuffled = shuffle(after(sent, pair_parts))
    gate_args = [hidden_own, hidden_other, gate_back_own, gate_back_other]
    up_args = [hidden_own, hidden_other, up_back_own, up_back_other]
    down_args = [branch_own, branch_other, units_own, units_other]
    terms = [(0, 2, 0), (1, 3, 0)]
    grads0 = weight_grad(
        at.columns,
        [*gate_args, *up_args[2:]],
        [(0, 1024, terms), (0, 512, [(0, 4, 0), (1, 5, 0)])],
    )
    hidden_sum, grads0, shuffled, up_args, down_args = lax.optimization_barrier(
        (hidden_sum.astype(LOW), grads0, shuffled, up_args, down_args)
    )

    hidden_blocks = gather_z(hidden_sum)
    came0 = {i: plane_shift(after(grads0[i], hidden_sum), i, False) for i in (1, 3)}
    grads1 = weight_grad(
        at.columns,
        [*up_args, *down_args],
        [(512, 512, terms), (0, 1024, [(4, 6, 0), (5, 7, 0)])],
        cut=True,
    )
    hidden_blocks, came0, grads1 = lax.optimization_barrier((hidden_blocks, came0, grads1))
    mix_own, attn_gain_part = call(
        attn_back_kernel,
        [((OWN, D), LOW), ((1, D), F32)],
        *hidden_blocks, *attn_blocks, upstream, attn_rms, attn_gains,
    )
    mix_other = core_swap(mix_own)

    keep1, up0, up1, far1, down0, down1 = after(grads1, hidden_blocks)
    came1a = [plane_shift(up0, 1, False), plane_shift(down0, 3, False)]
    hat, value_back, dots, head_parts = call(
        attend_back_kernel,
        [((SEQ, 512), F32), ((SEQ, 256), LOW), ((8, SEQ), F32), ((2, 256), F32)],
        qkv, scales, head_gains, *tables, low, mix_own, mix_other, *mixes,
        scratch=[pltpu.VMEM((SEQ, HEAD), F32)] * 2 + [pltpu.VMEM((SEQ, 256), LOW)],
    )
    hat, dots, came1a, up1, down1 = lax.optimization_barrier((hat, dots, came1a, up1, down1))
    came1b = [plane_shift(up1, 1, False), plane_shift(down1, 3, False)]
    dots, came1b, far1 = lax.optimization_barrier((all_stats(dots), came1b, far1))
    came0[2] = plane_shift(after(grads0[2], dots), 2, False)
    came1 = plane_shift(far1, 2, False)
    (qkv_back,) = call(
        qkv_back_kernel, [((SEQ, SEQ), LOW)], hat, qkv, scales, dots, value_back
    )
    came = core_swap(qkv_down(qkv_back, 1, qkv_blocks, LOW))
    input_parts = settle_ordered(at, qkv_down(qkv_back, 0, qkv_blocks, F32), came)
    input_parts, qkv_back = lax.optimization_barrier((input_parts, qkv_back))

    input_sum = lax.psum_scatter(input_parts, "z", scatter_dimension=0, tiled=True)
    attn_grads = weight_grad(
        at.columns,
        [states, qkv_back, mix_own, mix_other, mixed],
        [(0, SEQ, [(0, 1, 0)]), (0, 256, [(2, 4, 0), (3, 4, OWN)])],
        [attn_gain_part, ffn_gain_part, jnp.pad(head_parts.reshape(16, 32), ((0, 0), (0, 96)))],
    )
    input_sum, attn_grads = lax.optimization_barrier((input_sum, attn_grads))
    input_low = (input_sum.astype(F32) + hidden_rows).astype(LOW)
    near, far = input_low[:, :NEAR], input_low[:, NEAR:]
    flip = at.c == 1
    input_sent = [jnp.where(flip, far, near), jnp.where(flip, near, far)]
    input_rows = shuffled_of(at, input_sent, shuffle(input_sent))
    input_rows, attn_grads, came0, came1 = lax.optimization_barrier(
        (jnp.concatenate(input_rows), attn_grads, came0, came1)
    )
    input_rows = lax.all_gather(input_rows, "z", axis=0, tiled=True)
    attn_came = [plane_shift(attn_grads[i], i, False) for i in range(1, RING)]
    steps = jnp.arange(8, dtype=jnp.int32)
    from_part = at.s ^ at.c ^ (steps // RING)
    from_z = (at.z - steps) % RING
    block_out = order_rows(
        at, shuffled_of(at, sent, after(shuffled, input_low)), from_z, from_part
    )
    (input_grad,) = call(
        widen_kernel, [((SEQ, NEAR), F32)],
        (steps % RING * 2 + from_part).astype(jnp.int32), input_rows,
        scalars=1,
    )

    block_out, came0, came1, came1a, came1b = lax.optimization_barrier(
        (block_out, came0, came1, came1a, came1b)
    )
    rows0 = plane_parts(grads0[0], [came0[i] for i in (1, 2, 3)])
    came1b = [jnp.concatenate(halves, axis=1) for halves in zip(came1a, came1b)]
    rows1 = plane_parts(keep1, [*came1b, came1])
    ffn_rows = [jnp.concatenate(rows) for rows in zip(rows0, rows1)]
    ffn_came = {i: plane_shift(ffn_rows[i], i, True) for i in (1, 3)}
    attn_came, ffn_came = lax.optimization_barrier((attn_came, ffn_came))
    ffn_came[2] = plane_shift(after(ffn_rows[2], ffn_came), 2, True)
    attn_rows = plane_sum(attn_grads[0], attn_came)
    attn_came = [plane_shift(attn_rows[i], i, True) for i in range(1, RING)]
    attn_came, input_grad = lax.optimization_barrier((attn_came, input_grad))
    gate_out, up_out, down_out = share_cores(
        at,
        ffn_rows[0],
        [ffn_came[i] for i in (1, 2, 3)],
        [[(0, 0, 1024)], [(0, 1024, 512), (1, 0, 512)], [(1, 512, 1024)]],
    )
    query, key, value, mix_out, width, heads = share_cores(
        at, attn_rows[0], attn_came, [[(0, i, 256)] for i in range(0, 1024, 256)],
        [(8, 128), (16, 128)],
    )
    width = jnp.where(flip, width[:2, 64:], width[:2, :64])
    heads = jnp.where(at.s == 0, heads[2:4, :32], heads[10:12, :32])
    heads = jnp.where(flip, heads[:, 16:], heads[:, :16])

    return (
        block_out, input_grad, query, key, value, mix_out.T, gate_out, up_out, down_out.T,
        width[0], width[1], heads[0], heads[1],
    )


def solution(mesh):
    fine = Mesh(mesh.devices.reshape(4, 2, 2, 4, 2), ("y", "xh", "core", "z", "xl"))
    dp = ("y", "xh", "core")
    row, col = "z", "xl"
    return jax.shard_map(
        local,
        mesh=fine,
        in_specs=(
            P(dp, col), P(dp), P(col, row), P(col, row), P(col, row), P(row, col),
            P(col, row), P(col, row), P(row, col), P(col), P(col), P((row, col)),
            P((row, col)), P(dp, col),
        ),
        out_specs=(
            P(dp, col), P(dp, col),
            P((col,) + dp, row), P((col,) + dp, row), P((col,) + dp, row), P(row, (col,) + dp),
            P((col,) + dp, row), P((col,) + dp, row), P(row, (col,) + dp),
            P((col,) + dp), P((col,) + dp), P((row, col) + dp), P((row, col) + dp),
        ),
        check_vma=False,
    )
```

```python
import functools

import jax
import jax.numpy as jnp
from jax import lax
from jax.experimental import pallas as pl
from jax.experimental.pallas import tpu as pltpu
from jax.sharding import Mesh, PartitionSpec as P

D = 2048
HEAD = 128
SEQ = 768
NEAR = D // 2
OWN = SEQ // 2
RING = 4
BLOCK = SEQ // 8
EPSILON = 1e-06
ROPE_BASE = 500000.0
MASKED = -1e30
LOW = jnp.bfloat16
F32 = jnp.float32
FREE = pl.CostEstimate(flops=0, bytes_accessed=0, transcendentals=0)
PARAMS = pltpu.CompilerParams(vmem_limit_bytes=24 * 1024 * 1024)
EARLY = pltpu.CompilerParams(vmem_limit_bytes=60 * 1024 * 1024)


def dot(a, b, dims=((1,), (0,))):
    return lax.dot_general(a, b, (dims, ((), ())), preferred_element_type=F32)


NT = ((1,), (1,))
TN = ((0,), (0,))


def after(value, *earlier):
    return lax.optimization_barrier((value, earlier))[0]


def ring_shift(a, axes, step):
    return lax.ppermute(a, axes, [(i, (i + step) % RING) for i in range(RING)])


def z_shift(a, step):
    return ring_shift(a, "z", step)


def plane_shift(a, step, swapped):
    pairs = []
    for y in range(4):
        for x in range(4):
            for c in range(2):
                there = ((y + step) % 4, x) if (c == 0) != swapped else (y, (x + step) % 4)
                xh, xl = x // 2, x % 2
                source = ((y * 2 + xh) * 2 + c) * 2 + xl
                pairs.append((source, ((there[0] * 2 + there[1] // 2) * 2 + c) * 2 + there[1] % 2))
    return lax.ppermute(a, ("y", "xh", "core", "xl"), pairs)


def core_swap(a):
    return lax.ppermute(a, "core", [(0, 1), (1, 0)])


def pair_swap(a):
    return lax.ppermute(a, "xl", [(0, 1), (1, 0)])


def wrap_swap(a):
    return lax.ppermute(a, ("xh", "xl"), [(0, 3), (3, 0), (1, 2), (2, 1)])


def pick(blocks, index, axis=0):
    return lax.dynamic_index_in_dim(blocks, index, axis, keepdims=False)


class Place:
    def __init__(self):
        self.s = lax.axis_index("xl")
        self.xh = lax.axis_index("xh")
        self.x = self.xh * 2 + self.s
        self.y = lax.axis_index("y")
        self.c = lax.axis_index("core")
        self.z = lax.axis_index("z")
        self.home = self.c == self.s
        self.z_scalar = self.z.reshape(1).astype(jnp.int32)
        steps = jnp.arange(RING, dtype=jnp.int32)
        self.back = (self.z - steps) % RING
        self.rows = jnp.concatenate([self.c * 4 + self.back, (1 - self.c) * 4 + self.back])
        first, second = steps[:, None], steps[None, :]
        dx = jnp.where(self.c == 0, second, first)
        dy = jnp.where(self.c == 0, first, second)
        self.columns = (
            (dx % 2) * 8 + ((self.y + dy) % 4) * 2 + ((self.x + dx) % 4) // 2
        ).reshape(-1)
        y, x = first, second
        self.plain = (((x % 2) ^ self.s) * 8 + y * 2 + x // 2).reshape(-1)


def place_kernel(plan, sources, table, *refs):
    ins, outs, sems = refs[:sources], refs[sources:-1], refs[-1]
    copies = []
    for i, (source, there) in enumerate(plan(table, ins, outs)):
        copies.append(pltpu.make_async_copy(source, there, sems.at[i]))
        copies[-1].start()
    for copy in copies:
        copy.wait()


def place(plan, count, shapes, table, *sources, params=PARAMS):
    return pl.pallas_call(
        functools.partial(place_kernel, plan, len(sources)),
        in_specs=[pl.BlockSpec(memory_space=pltpu.SMEM)]
        + [pl.BlockSpec(memory_space=pltpu.HBM)] * len(sources),
        out_specs=tuple(pl.BlockSpec(memory_space=pltpu.VMEM) for _ in shapes),
        out_shape=tuple(jax.ShapeDtypeStruct(shape, LOW) for shape in shapes),
        scratch_shapes=[pltpu.SemaphoreType.DMA((count,))],
        compiler_params=params,
        cost_estimate=FREE,
    )(jnp.stack(table).astype(jnp.int32), *sources)


def at_block(index, size):
    return pl.ds(pl.multiple_of(index * size, size), size)


def first_hop(a):
    return lax.ppermute(a, ("core", "xl"), [(0, 2), (3, 1), (2, 3), (1, 0)])


def second_hop(first):
    return lax.ppermute(first, ("core", "xl"), [(0, 2), (3, 1)])


def sequence_kernel(count, table, a_ref, first_ref, second_ref, out_ref, sems):
    def move(near, far):
        copies = []
        for i in range(count):
            block = at_block(table[i], BLOCK)
            there = pl.ds(i * BLOCK, BLOCK)
            for source, lo in ((near.at[block], 0), (far.at[block], NEAR)):
                copies.append(
                    pltpu.make_async_copy(
                        source, out_ref.at[there, pl.ds(lo, NEAR)], sems.at[len(copies)]
                    )
                )
        for copy in copies:
            copy.start()
        for copy in copies:
            copy.wait()

    pl.when(table[count] == 1)(functools.partial(move, a_ref, first_ref))
    pl.when(table[count] == 0)(functools.partial(move, first_ref, second_ref))


def to_sequence(at, a, first, second, count=8):
    table = jnp.concatenate([at.rows[:count], at.home[None].astype(jnp.int32)])
    return pl.pallas_call(
        functools.partial(sequence_kernel, count),
        in_specs=[pl.BlockSpec(memory_space=pltpu.SMEM)]
        + [pl.BlockSpec(memory_space=pltpu.HBM)] * 3,
        out_specs=pl.BlockSpec(memory_space=pltpu.VMEM),
        out_shape=jax.ShapeDtypeStruct((count * BLOCK, D), LOW),
        scratch_shapes=[pltpu.SemaphoreType.DMA((2 * count,))],
        compiler_params=PARAMS,
        cost_estimate=FREE,
    )(table.astype(jnp.int32), a, first, second)


def order_rows(at, sources, index, which):
    joined = jnp.concatenate(sources) if len(sources) > 1 else sources[0]
    rows = sources[0].shape[0] // BLOCK

    def plan(table, ins, outs):
        return [
            (ins[0].at[at_block(table[i], BLOCK)], outs[0].at[pl.ds(i * BLOCK, BLOCK)])
            for i in range(8)
        ]

    table = index + rows * which if len(sources) > 1 else index * 2 + which
    return place(plan, 8, [(SEQ, joined.shape[1])], list(table), joined)[0]


def cut_columns(at, heights, *weights):
    width = weights[0].shape[1] // 2
    starts = [sum(heights[:i]) for i in range(len(heights))]

    def plan(table, ins, outs):
        return [
            (
                ref.at[pl.ds(start, height), at_block(table[0], width)],
                out.at[:, pl.ds(width * i, width)],
            )
            for i, ref in enumerate(ins)
            for start, height, out in zip(starts, heights, outs)
        ]

    shapes = [(height, width * len(weights)) for height in heights]
    return place(plan, len(heights) * len(weights), shapes, [at.c], *weights, params=EARLY)


PIECES = (
    (("gate", 0), ("mix", 0)), (("gate", 1), ("mix", 1)),
    (("gate", 2), ("up", 0)), (("gate", 3), ("up", 1)),
    (("up", 2), ("down", 0)), (("up", 3), ("down", 1)),
    (("down", 2),), (("down", 3),),
)
PART = 256


def part_height(name):
    return 128 if name == "mix" else PART


def part_starts(piece):
    heights = [part_height(name) for name, _ in piece]
    return [sum(heights[:i]) for i in range(len(heights) + 1)]


def cut_pieces(at, w_gate, w_up, w_down, w_mix):
    def plan(table, ins, outs):
        named = dict(zip(("gate", "up", "down", "mix"), ins))
        copies = []
        for out, piece in zip(outs, PIECES):
            for start, (name, part) in zip(part_starts(piece), piece):
                height = part_height(name)
                if name in ("down", "mix"):
                    half = named[name].shape[0] // 2
                    first = pl.multiple_of(table[0] * half + height * part, height)
                    source = named[name].at[pl.ds(first, height)]
                else:
                    rows = pl.ds(height * part, height)
                    source = named[name].at[rows, at_block(table[0], NEAR)]
                copies.append((source, out.at[pl.ds(start, height)]))
        return copies

    shapes = [(part_starts(piece)[-1], NEAR) for piece in PIECES]
    count = sum(len(piece) for piece in PIECES)
    return place(plan, count, shapes, [at.c], w_gate, w_up, w_down, w_mix, params=EARLY)


def pieces_with(name):
    return [k for k, piece in enumerate(PIECES) if name in dict(piece)]


def views(name, refs):
    out = []
    for ref, k in zip(refs, pieces_with(name)):
        for start, (found, _) in zip(part_starts(PIECES[k]), PIECES[k]):
            if found == name:
                out.append(ref.at[pl.ds(start, part_height(name))])
    return out


def join_columns(parts):
    starts = [sum(part.shape[1] for part in parts[:i]) for i in range(len(parts) + 1)]

    def plan(table, ins, outs):
        return [
            (ref, outs[0].at[:, pl.ds(starts[i], parts[i].shape[1])]) for i, ref in enumerate(ins)
        ]

    return place(plan, len(parts), [(D, starts[-1])], [0], *parts)[0]


def fetch(first, second):
    return pair_swap(first), wrap_swap(second)


def scatter_z(parts):
    total = parts[0]
    for i in range(1, RING):
        total = total + z_shift(parts[i], -i).astype(F32)
    return total


def gather_z(rows):
    return [rows] + [z_shift(rows, i) for i in range(1, RING)]


def all_stats(pair):
    theirs = core_swap(pair)
    pair = pair + jnp.concatenate([theirs[:, OWN:], theirs[:, :OWN]], axis=1)
    total = pair
    for i in range(1, RING):
        came, cut = z_shift(pair, i), OWN - i * BLOCK
        total = total + jnp.concatenate(
            [came[:, cut:OWN], came[:, :cut], came[:, OWN + cut :], came[:, OWN : OWN + cut]],
            axis=1,
        )
    return total


def plane_sum(own, came):
    total = own.astype(F32) + came[0].astype(F32) + came[1].astype(F32) + came[2].astype(F32)
    total = lax.optimization_barrier(total.astype(LOW))
    height = own.shape[0] // RING
    return [total[height * i : height * (i + 1)] for i in range(RING)]


def sum_kernel(p0, p1, p2, p3, *outs):
    for i, out in enumerate(outs):
        at = slice(128 * i, 128 * (i + 1))
        total = p0[at, :].astype(F32) + p1[at, :].astype(F32)
        out[...] = (total + p2[at, :].astype(F32) + p3[at, :].astype(F32)).astype(LOW)


def plane_parts(own, came):
    return call(sum_kernel, [((128, own.shape[1]), LOW)] * RING, own, *came)


def share_kernel(core, p0, p1, p2, p3, own_ref, sent_ref):
    total = p0[...].astype(F32) + p1[...].astype(F32) + p2[...].astype(F32) + p3[...].astype(F32)
    flip = core[0] == 1
    for i in range(total.shape[0] // 128):
        at = slice(64 * i, 64 * (i + 1))
        low, high = total[128 * i : 128 * i + 64, :], total[128 * i + 64 : 128 * (i + 1), :]
        own_ref[at, :] = jnp.where(flip, high, low)
        sent_ref[at, :] = jnp.where(flip, low, high).astype(LOW)
    rest = total.shape[0] % 128
    if rest:
        own_ref[-rest:, :] = total[-rest:, :]
        sent_ref[-rest:, :] = total[-rest:, :].astype(LOW)


def wide_kernel(plan, core, own_ref, came_ref, *outs):
    first = core[0] == 0
    own, came = own_ref[...], came_ref[...].astype(F32)
    sides = jnp.where(first, own, came), jnp.where(first, came, own)
    for out, pieces in zip(outs, plan):
        at = 0
        for side in sides:
            for rows, start, width in pieces:
                value = side[64 * rows : 64 * (rows + 1), start : start + width]
                out[:, at : at + width] = value
                at += width
    if len(outs) > len(plan):
        width_ref, heads_ref = outs[len(plan) :]
        zero, one = (side[-16:-8, :128] for side in sides)
        width_ref[...] = zero + one
        heads_ref[0:8, :] = zero
        heads_ref[8:16, :] = one


def share_cores(at, own, came, plan, extra=()):
    height, width = own.shape
    shape = (height // 128 * 64 + height % 128, width)
    core = at.c.reshape(1).astype(jnp.int32)
    own, sent = call(share_kernel, [(shape, F32), (shape, LOW)], core, own, *came, scalars=1)
    widths = [2 * sum(piece[2] for piece in pieces) for pieces in plan]
    shapes = [((64, width), F32) for width in widths]
    shapes += [(shape, F32) for shape in extra]
    return call(functools.partial(wide_kernel, plan), shapes, core, own, core_swap(sent), scalars=1)


def call(kernel, shapes, *args, scratch=(), scalars=0):
    return pl.pallas_call(
        kernel,
        in_specs=[
            pl.BlockSpec(memory_space=pltpu.SMEM if i < scalars else pltpu.VMEM)
            for i in range(len(args))
        ],
        out_shape=tuple(jax.ShapeDtypeStruct(shape, dtype) for shape, dtype in shapes),
        scratch_shapes=list(scratch),
        compiler_params=PARAMS,
        cost_estimate=FREE,
    )(*args)


def row_dot(rows, refs, at):
    value = 0.0
    start = 0
    for ref in refs:
        height = ref.shape[0]
        value += dot(rows[:, start : start + height], ref[:, at])
        start += height
    return value


def strips(width, size):
    return [slice(i, i + size) for i in range(0, width, size)]


def as_rows(first, second):
    return jnp.concatenate([first, second, jnp.zeros((SEQ, 6), F32)], axis=1).T


def qkv_kernel(states_ref, *refs):
    *blocks, qkv_ref, sums_ref = refs
    sums = []
    for at in strips(SEQ, 256):
        value = row_dot(states_ref, blocks, at)
        qkv_ref[:, at] = value
        sums.append(jnp.sum(value * value, axis=1, keepdims=True))
    sums_ref[...] = as_rows(*sums[:2])


def product_kernel(body, *refs):
    *refs, out_ref = refs
    for at, value in body(refs):
        out_ref[:, at] = value.astype(out_ref.dtype)


def product(body, dtype, *args):
    return call(functools.partial(product_kernel, body), [((OWN, D), dtype)], *args)[0]


def half_rows(ref, half):
    return ref[OWN * half : OWN * (half + 1), :]


def mix(left, half, pieces, dtype):
    count = len(pieces) // 2

    def body(refs):
        left, *w = refs
        left = half_rows(left, half)
        for i in range(2):
            blocks = views("mix", w[count * i : count * (i + 1)])
            for at in strips(NEAR, 512):
                yield slice(NEAR * i + at.start, NEAR * i + at.stop), row_dot(left, blocks, at)

    return product(body, dtype, left, *pieces)


def down(units, pieces, dtype):
    count = len(pieces) // 2

    def body(refs):
        units, *w = refs
        for i in range(2):
            blocks = views("down", w[count * i : count * (i + 1)])
            for at in strips(NEAR, 512):
                yield slice(NEAR * i + at.start, NEAR * i + at.stop), row_dot(units, blocks, at)

    return product(body, dtype, units, *pieces)


def pair_down(gate_back, up_back, gates, ups, dtype):
    def body(refs):
        gate_back, up_back, *w = refs
        for i in range(2):
            n, m = len(gates) // 2, len(ups) // 2
            gate = views("gate", w[n * i : n * (i + 1)])
            up = views("up", w[2 * n + m * i : 2 * n + m * (i + 1)])
            for k in range(4):
                value = dot(gate_back[...], gate[k][...], NT) + dot(up_back[...], up[k][...], NT)
                yield slice(NEAR * i + PART * k, NEAR * i + PART * (k + 1)), value

    return product(body, dtype, gate_back, up_back, *gates, *ups)


def qkv_down(back, half, blocks, dtype):
    def body(refs):
        back, *w = refs
        back = half_rows(back, half)
        start = 0
        for ref in w:
            for at in strips(ref.shape[0], 256):
                yield slice(start + at.start, start + at.stop), dot(back, ref[at, :], NT)
            start += ref.shape[0]

    return product(body, dtype, back, *blocks)


def settle_kernel(own_ref, came_ref, *outs):
    for i, ref in enumerate(outs):
        at = slice(i * BLOCK, (i + 1) * BLOCK)
        ref[...] = (own_ref[at, :] + came_ref[at, :].astype(F32)).astype(ref.dtype)


def settle(own, came):
    return call(
        settle_kernel, [((BLOCK, D), F32)] + [((BLOCK, D), LOW)] * 3, own, came
    )


def z_rows(z, i):
    return pl.ds(pl.multiple_of(lax.rem(z + RING - i, RING) * BLOCK, BLOCK), BLOCK)


def settle_ordered_kernel(z_ref, own_ref, came_ref, out_ref):
    for i in range(RING):
        at = slice(i * BLOCK, (i + 1) * BLOCK)
        value = own_ref[at, :] + came_ref[at, :].astype(F32)
        out_ref[z_rows(z_ref[0], i), :] = value.astype(LOW)


def settle_ordered(at, own, came):
    return call(settle_ordered_kernel, [((OWN, D), LOW)], at.z_scalar, own, came, scalars=1)[0]


def units_kernel(n, m, rows_ref, *refs):
    gate_ref, up_ref, units_ref = refs[-3:]
    gates = views("gate", refs[:n]) + views("gate", refs[n : 2 * n])
    ups = views("up", refs[2 * n : 2 * n + m]) + views("up", refs[2 * n + m : 2 * n + 2 * m])
    for at in strips(1024, 512):
        gate, up = row_dot(rows_ref, gates, at), row_dot(rows_ref, ups, at)
        gate_ref[:, at] = gate.astype(LOW)
        up_ref[:, at] = up.astype(LOW)
        units_ref[:, at] = (gate * jax.nn.sigmoid(gate) * up).astype(LOW)


def units_of(rows, gates, ups):
    kernel = functools.partial(units_kernel, len(gates) // 2, len(ups) // 2)
    return call(kernel, [((OWN, 1024), LOW)] * 3, rows, *gates, *ups)


def units_back_kernel(branch_ref, *refs):
    *w, gate_ref, up_ref, gate_back_ref, up_back_ref = refs
    count = len(w) // 2
    near, far = views("down", w[:count]), views("down", w[count:])
    for k in range(4):
        at = slice(PART * k, PART * (k + 1))
        grad = dot(branch_ref[:, :NEAR], near[k][...], NT)
        grad += dot(branch_ref[:, NEAR:], far[k][...], NT)
        gate, up = gate_ref[:, at].astype(F32), up_ref[:, at].astype(F32)
        sigmoid = jax.nn.sigmoid(gate)
        gate_back_ref[:, at] = (grad * up * sigmoid * (1.0 + gate * (1.0 - sigmoid))).astype(LOW)
        up_back_ref[:, at] = (grad * gate * sigmoid).astype(LOW)


def units_back(branch, pieces, gate, up):
    return call(units_back_kernel, [((OWN, 1024), LOW)] * 2, branch, *pieces, gate, up)


def grad_kernel(plan, count, extras, cut, *refs):
    table, ins = refs[0], refs[1 : 1 + count]
    extra, outs = refs[1 + count : 1 + count + extras], refs[1 + count + extras :]
    if cut:
        outs = [(outs[0],), outs[1:3], (outs[3],), outs[4:6]]
    for d in range(RING):
        blocks = [table[4 * d + e] for e in range(RING)]
        places = [at_block(block, 128) for block in blocks]
        start = 0
        for lo, width, terms in plan:
            value = 0.0
            for left, right, row in terms:
                left, right = ins[left], ins[right]
                chosen = jnp.concatenate([left[:, place] for place in places], axis=1)
                value += dot(chosen, right[row : row + left.shape[0], lo : lo + width], TN)
            value = value.astype(LOW)
            at = slice(start, start + width)
            if cut:
                put_columns(outs[d], start, value)
            elif not extras:
                outs[d][:, at] = value
            else:
                for e in range(RING):
                    outs[d][144 * e : 144 * e + 128, at] = value[128 * e : 128 * (e + 1)]
            start += width
        if extras:
            attn_ref, ffn_ref, heads_ref = extra
            for e in range(RING):
                block = lax.rem(blocks[e], 8)
                rows = [attn_ref[0:1, places[e]], ffn_ref[0:1, places[e]]]
                rows += [heads_ref[pl.ds(block + 8 * i, 1), :] for i in range(2)]
                rows = jnp.concatenate([*rows, jnp.zeros((12, 128), F32)])
                at = slice(144 * e + 128, 144 * (e + 1))
                outs[d][at, :128] = rows.astype(LOW)
                outs[d][at, 128:] = jnp.zeros((16, start - 128), LOW)


def put_columns(outs, start, value):
    at = 0
    for out in outs:
        lo, hi = max(start, at), min(start + value.shape[1], at + out.shape[1])
        if lo < hi:
            out[:, lo - at : hi - at] = value[:, lo - start : hi - start]
        at += out.shape[1]


def weight_grad(table, arrays, plan, extra=(), cut=False):
    width = sum(span[1] for span in plan)
    height = 576 if extra else 512
    kernel = functools.partial(grad_kernel, plan, len(arrays), len(extra), cut)
    widths = [width, width // 2, width // 2, width, width // 2, width // 2] if cut else [width] * RING
    outs = [((height, w), LOW) for w in widths]
    return call(kernel, outs, table.astype(jnp.int32), *arrays, *extra, scalars=1)


def turn(v, cosines, sines):
    return v * cosines + pltpu.roll(v, HEAD // 2, 1) * sines


def turn_back(v, cosines, sines):
    return v * cosines - pltpu.roll(v, HEAD // 2, 1) * sines


TILE = 384


def seen(table_ref, row_ref, lo):
    here = table_ref[lo : lo + TILE, 2 * HEAD : 3 * HEAD]
    there = row_ref[0:1, :]
    return (there <= here[:, 0:1]) & (there >= here[:, 1:2])


def attend_kernel(
    qkv_ref, sums_ref, gain_ref, table_ref, row_ref, mixed_ref, low_ref, scale_ref
):
    cosines, sines = table_ref[:, :HEAD], table_ref[:, HEAD : 2 * HEAD]
    scale_ref[...] = lax.rsqrt(sums_ref[...] * (1.0 / D) + EPSILON).T
    for h in range(2):
        at = slice(h * HEAD, (h + 1) * HEAD)
        k_at = slice(256 + h * HEAD, 256 + (h + 1) * HEAD)
        q = qkv_ref[:, at] * scale_ref[:, 0:1] * gain_ref[0:1, at]
        k = qkv_ref[:, k_at] * scale_ref[:, 1:2] * gain_ref[1:2, at]
        low_ref[:, at] = turn(q, cosines, sines).astype(LOW)
        k = turn(k, cosines, sines).astype(LOW)
        v = qkv_ref[:, 512 + h * HEAD : 512 + (h + 1) * HEAD].astype(LOW)
        low_ref[:, k_at] = k
        low_ref[:, 512 + h * HEAD : 512 + (h + 1) * HEAD] = v
        for lo in range(0, SEQ, TILE):
            q = low_ref[lo : lo + TILE, at]
            scores = dot(q, k, NT) * HEAD**-0.5
            scores = jnp.where(seen(table_ref, row_ref, lo), scores, MASKED)
            peak = jnp.max(scores, axis=1, keepdims=True)
            weights = jnp.exp(scores - peak)
            total = jnp.sum(weights, axis=1, keepdims=True)
            weights = (weights * (1.0 / total)).astype(LOW)
            mixed_ref[lo : lo + TILE, at] = dot(weights, v).astype(LOW)
            scale_ref[lo : lo + TILE, 2 + h : 3 + h] = peak + jnp.log(total)


def attend_back_kernel(
    qkv_ref, scale_ref, gain_ref, table_ref, row_ref, low_ref,
    own_ref, other_ref, near0, near1, far0, far1,
    hat_ref, value_ref, dots_ref, part_ref, dk_ref, dv_ref, grad_ref,
):
    cosines, sines = table_ref[:, :HEAD], table_ref[:, HEAD : 2 * HEAD]
    for i, ref in enumerate((own_ref, other_ref)):
        pairs = zip(views("mix", (near0, near1)), views("mix", (far0, far1)))
        for k, (near, far) in enumerate(pairs):
            grad = dot(ref[:, :NEAR], near[...], NT) + dot(ref[:, NEAR:], far[...], NT)
            grad_ref[OWN * i : OWN * (i + 1), 128 * k : 128 * (k + 1)] = grad.astype(LOW)
    for h in range(2):
        at = slice(h * HEAD, (h + 1) * HEAD)
        k_at = slice(256 + h * HEAD, 256 + (h + 1) * HEAD)
        k = low_ref[:, k_at]
        v = low_ref[:, 512 + h * HEAD : 512 + (h + 1) * HEAD]
        for lo in range(0, SEQ, TILE):
            q = low_ref[lo : lo + TILE, at]
            grad = grad_ref[lo : lo + TILE, at]
            scores = dot(q, k, NT) * HEAD**-0.5
            weights = jnp.exp(scores - scale_ref[lo : lo + TILE, 2 + h : 3 + h])
            weights = jnp.where(seen(table_ref, row_ref, lo), weights, 0.0)
            weight_grad = dot(grad, v, NT)
            centre = jnp.sum(weights * weight_grad, axis=1, keepdims=True)
            score_grad = (weights * (weight_grad - centre)).astype(LOW)
            hat_ref[lo : lo + TILE, at] = dot(score_grad, k) * HEAD**-0.5
            value_part = dot(weights.astype(LOW), grad, TN)
            key_part = dot(score_grad, q, TN)
            if lo == 0:
                dv_ref[...] = value_part
                dk_ref[...] = key_part
            else:
                dv_ref[...] += value_part
                dk_ref[...] += key_part
        value_ref[:, at] = dv_ref[...].astype(LOW)
        q_grad = turn_back(hat_ref[:, at], cosines, sines)
        k_grad = turn_back(dk_ref[...] * HEAD**-0.5, cosines, sines)
        q, k = qkv_ref[:, at], qkv_ref[:, k_at]
        part_ref[0:1, at] = jnp.sum(q_grad * q * scale_ref[:, 0:1], axis=0, keepdims=True)
        part_ref[1:2, at] = jnp.sum(k_grad * k * scale_ref[:, 1:2], axis=0, keepdims=True)
        hat_ref[:, at] = q_grad * gain_ref[0:1, at]
        hat_ref[:, k_at] = k_grad * gain_ref[1:2, at]
    dots_ref[...] = as_rows(
        jnp.sum(hat_ref[:, :256] * qkv_ref[:, :256], axis=1, keepdims=True),
        jnp.sum(hat_ref[:, 256:] * qkv_ref[:, 256:512], axis=1, keepdims=True),
    )


def qkv_back_kernel(hat_ref, qkv_ref, rms_ref, dots_ref, value_ref, out_ref):
    dots = dots_ref[...].T
    for i in range(2):
        at = slice(i * 256, (i + 1) * 256)
        rms = rms_ref[:, i : i + 1]
        coefficient = rms * rms * rms * dots[:, i : i + 1] * (1.0 / D)
        out_ref[:, at] = (rms * hat_ref[:, at] - qkv_ref[:, at] * coefficient).astype(LOW)
    out_ref[:, 512:] = value_ref[...]


def widen_kernel(table, rows_ref, out_ref):
    for i in range(8):
        block = pl.ds(pl.multiple_of(table[i] * BLOCK, BLOCK), BLOCK)
        out_ref[i * BLOCK : (i + 1) * BLOCK, :] = rows_ref[block, :].astype(F32)


def blocks_of(ref):
    return [slice(i * BLOCK, (i + 1) * BLOCK) for i in range(ref.shape[0] // BLOCK)]


def hidden_kernel(b0, b1, b2, b3, states_ref, gain_ref, low_ref, rms_ref):
    for at, ref in zip(blocks_of(low_ref), (b0, b1, b2, b3)):
        branch = ref[...].astype(F32)
        rms = lax.rsqrt(jnp.mean(branch * branch, axis=1, keepdims=True) + EPSILON)
        hidden = states_ref[at, :].astype(F32) + gain_ref[...] * branch * rms
        low_ref[at, :] = hidden.astype(LOW)
        rms_ref[at, :] = rms


def back_of(upstream, branch, rms, gain):
    part = jnp.sum(upstream * branch * rms, axis=0, keepdims=True)
    scaled = upstream * gain
    inner = jnp.sum(scaled * branch, axis=1, keepdims=True)
    return rms * scaled - branch * (rms * rms * rms * inner * (1.0 / D)), part


def ffn_back_kernel(b0, b1, b2, b3, upstream_ref, gain_ref, back_ref, rms_ref, part_ref):
    for i, (at, ref) in enumerate(zip(blocks_of(back_ref), (b0, b1, b2, b3))):
        branch = ref[...].astype(F32)
        rms = lax.rsqrt(jnp.mean(branch * branch, axis=1, keepdims=True) + EPSILON)
        back, part = back_of(upstream_ref[at, :].astype(F32), branch, rms, gain_ref[...])
        back_ref[at, :] = back.astype(LOW)
        rms_ref[at, :] = rms
        part_ref[...] = part if i == 0 else part_ref[...] + part


def attn_back_kernel(
    g0, g1, g2, g3, b0, b1, b2, b3, upstream_ref, rms_ref, gain_ref, back_ref, part_ref
):
    pairs = zip(blocks_of(back_ref), (g0, g1, g2, g3), (b0, b1, b2, b3))
    for i, (at, grad_ref, ref) in enumerate(pairs):
        grad = grad_ref[...].astype(F32) + upstream_ref[at, :].astype(F32)
        back, part = back_of(grad, ref[...].astype(F32), rms_ref[at, :], gain_ref[...])
        back_ref[at, :] = back.astype(LOW)
        part_ref[...] = part if i == 0 else part_ref[...] + part


def out_kernel(
    core_ref, a0, a1, a2, a3, b0, b1, b2, b3, states_ref, attn_rms_ref, ffn_rms_ref,
    attn_gain_ref, ffn_gain_ref, sent0_ref, sent1_ref,
):
    pairs = zip(blocks_of(states_ref), (a0, a1, a2, a3), (b0, b1, b2, b3))
    flip = core_ref[0] == 1
    for at, a_ref, b_ref in pairs:
        value = (
            states_ref[at, :].astype(F32)
            + attn_gain_ref[...] * a_ref[...].astype(F32) * attn_rms_ref[at, :]
            + ffn_gain_ref[...] * b_ref[...].astype(F32) * ffn_rms_ref[at, :]
        ).astype(LOW)
        near, far = value[:, :NEAR], value[:, NEAR:]
        sent0_ref[at, :] = jnp.where(flip, far, near)
        sent1_ref[at, :] = jnp.where(flip, near, far)


def shuffle(sent):
    out = []
    for k in range(2):
        perm = [(c * 2 + s, s * 2 + (s ^ c ^ k)) for s in range(2) for c in range(2)]
        out.append(lax.ppermute(sent[k], ("core", "xl"), [p for p in perm if p[0] != p[1]]))
    return out


def shuffled_of(at, sent, came):
    return [jnp.where((at.s == k) & (at.c == k), sent[k], came[k]) for k in range(2)]


def local(
    inputs, segments, w_query, w_key, w_value, w_mix, w_gate, w_up, w_down,
    attn_gain, ffn_gain, query_gain, key_gain, out_grad,
):
    at = Place()
    first = first_hop(inputs)
    near_qkv = cut_columns(at, (768, 256), w_query, w_key, w_value)
    far_qkv = [wrap_swap(near_qkv[0]), pair_swap(near_qkv[1])]
    near = cut_pieces(at, after(w_gate, near_qkv), w_up, w_down, w_mix)

    gains = jnp.concatenate([attn_gain, ffn_gain, query_gain, key_gain])
    their_gains = pair_swap(gains)
    attn_gains = jnp.concatenate([attn_gain, their_gains[:NEAR]])[None]
    ffn_gains = jnp.concatenate([ffn_gain, their_gains[NEAR:D]])[None]
    head_gains = jnp.where(at.home, gains[D:], their_gains[D:]).reshape(2, 256)

    segment_ids = jnp.where(at.home, segments, core_swap(segments))
    step_index = jnp.arange(SEQ, dtype=jnp.int32)
    earlier = jnp.concatenate([segment_ids[:1] - 1, segment_ids[:-1]])
    begins = lax.cummax(jnp.where(segment_ids != earlier, step_index, 0))
    chosen = at.rows[:, None, None] == jnp.arange(8, dtype=jnp.int32)[None, :, None]
    begins = jnp.sum(jnp.where(chosen, begins.reshape(1, 8, BLOCK), 0), axis=1).reshape(-1)
    index = (at.rows[:, None] * BLOCK + jnp.arange(BLOCK, dtype=jnp.int32)[None]).reshape(-1)
    frequency = ROPE_BASE ** (-2.0 * jnp.arange(HEAD // 2, dtype=F32) / HEAD)
    angles = (index - begins).astype(F32)[:, None] * frequency
    cosines, sines = jnp.cos(angles), jnp.sin(angles)
    place_columns = jnp.stack([index, begins], axis=1).astype(F32)
    table = jnp.concatenate(
        [cosines, cosines, -sines, sines, jnp.pad(place_columns, ((0, 0), (0, 126)))], axis=1
    )
    tables = (table, index[None].astype(F32))

    tables, head_gains, attn_gains, ffn_gains, at.columns, at.plain, at.rows, near, first = (
        lax.optimization_barrier(
            (tables, head_gains, attn_gains, ffn_gains, at.columns, at.plain, at.rows, near, first)
        )
    )
    states = to_sequence(at, inputs, first, second_hop(after(first, far_qkv)))
    states, far_qkv = lax.optimization_barrier((states, far_qkv))
    qkv_blocks = [*near_qkv, *far_qkv]
    qkv, squares = call(qkv_kernel, [((SEQ, SEQ), F32), ((8, SEQ), F32)], states, *qkv_blocks)
    far = fetch(*after(near[:2], far_qkv))
    squares = all_stats(squares)
    squares = lax.optimization_barrier(squares)
    mixed, low, scales = call(
        attend_kernel,
        [((SEQ, 256), LOW), ((SEQ, SEQ), LOW), ((SEQ, 8), F32)],
        qkv, squares, head_gains, *tables,
    )
    mixed, far = lax.optimization_barrier((mixed, far))
    mixes = [*near[:2], *far[:2]]
    came = core_swap(mix(mixed, 1, mixes, LOW))
    mix_parts = settle(mix(mixed, 0, mixes, F32), came)
    mix_parts = lax.optimization_barrier(mix_parts)
    far = [*far, *fetch(*after(near[2:4], mixed))]
    attn_sum = scatter_z(mix_parts).astype(LOW)
    attn_sum, far = lax.optimization_barrier((attn_sum, far))
    far = [*far, *fetch(*after(near[4:6], attn_sum))]
    attn_blocks = gather_z(attn_sum)
    own_states = after(states, attn_sum)[:OWN]
    attn_blocks, far, own_states = lax.optimization_barrier((attn_blocks, far, own_states))
    far = [*far, *fetch(*after(near[6:], attn_blocks))]
    hidden_own, attn_rms = call(
        hidden_kernel,
        [((OWN, D), LOW), ((OWN, 1), F32)],
        *attn_blocks, own_states, attn_gains,
    )
    hidden_other = core_swap(hidden_own)

    gates, ups, downs = (
        [side[k] for side in (near, far) for k in pieces_with(name)]
        for name in ("gate", "up", "down")
    )
    gate_own, up_own, units_own = units_of(hidden_own, gates, ups)
    hidden_other = after(hidden_other, units_own)
    gate_other, up_other, units_other = units_of(hidden_other, gates, ups)
    came = core_swap(down(units_other, downs, LOW))
    ffn_parts = settle(down(after(units_own, units_other), downs, F32), came)
    ffn_parts = lax.optimization_barrier(ffn_parts)
    grad_first = first_hop(after(out_grad, ffn_parts))
    ffn_sum = scatter_z(ffn_parts).astype(LOW)
    ffn_sum, grad_first = lax.optimization_barrier((ffn_sum, grad_first))
    ffn_blocks = gather_z(ffn_sum)
    upstream = to_sequence(at, out_grad, grad_first, second_hop(grad_first), RING)
    ffn_blocks, upstream = lax.optimization_barrier((ffn_blocks, upstream))
    branch_own, ffn_rms, ffn_gain_part = call(
        ffn_back_kernel,
        [((OWN, D), LOW), ((OWN, 1), F32), ((1, D), F32)],
        *ffn_blocks, upstream, ffn_gains,
    )
    branch_other = core_swap(branch_own)
    gate_back_own, up_back_own = units_back(branch_own, downs, gate_own, up_own)
    sent = call(
        out_kernel,
        [((OWN, NEAR), LOW)] * 2,
        at.c.reshape(1).astype(jnp.int32), *attn_blocks, *ffn_blocks,
        own_states, attn_rms, after(ffn_rms, gate_back_own), attn_gains, ffn_gains,
        scalars=1,
    )
    branch_other = after(branch_other, gate_back_own, sent)
    gate_back_other, up_back_other = units_back(branch_other, downs, gate_other, up_other)
    came = core_swap(pair_down(gate_back_other, up_back_other, gates, ups, LOW))
    pair_parts = pair_down(after(gate_back_own, gate_back_other), up_back_own, gates, ups, F32)
    pair_parts = settle(pair_parts, came)

    hidden_sum = scatter_z(pair_parts)
    hidden_rows = hidden_sum + upstream[:BLOCK].astype(F32)
    branch_own, hidden_own, pair_parts = lax.optimization_barrier(
        (branch_own, hidden_own, pair_parts)
    )
    shuffled = shuffle(after(sent, pair_parts))
    gate_args = [hidden_own, hidden_other, gate_back_own, gate_back_other]
    up_args = [hidden_own, hidden_other, up_back_own, up_back_other]
    down_args = [branch_own, branch_other, units_own, units_other]
    terms = [(0, 2, 0), (1, 3, 0)]
    grads0 = weight_grad(
        at.columns,
        [*gate_args, *up_args[2:]],
        [(0, 1024, terms), (0, 512, [(0, 4, 0), (1, 5, 0)])],
    )
    hidden_sum, grads0, shuffled, up_args, down_args = lax.optimization_barrier(
        (hidden_sum.astype(LOW), grads0, shuffled, up_args, down_args)
    )

    hidden_blocks = gather_z(hidden_sum)
    came0 = {i: plane_shift(after(grads0[i], hidden_sum), i, False) for i in (1, 3)}
    grads1 = weight_grad(
        at.columns,
        [*up_args, *down_args],
        [(512, 512, terms), (0, 1024, [(4, 6, 0), (5, 7, 0)])],
        cut=True,
    )
    hidden_blocks, came0, grads1 = lax.optimization_barrier((hidden_blocks, came0, grads1))
    mix_own, attn_gain_part = call(
        attn_back_kernel,
        [((OWN, D), LOW), ((1, D), F32)],
        *hidden_blocks, *attn_blocks, upstream, attn_rms, attn_gains,
    )
    mix_other = core_swap(mix_own)

    keep1, up0, up1, far1, down0, down1 = after(grads1, hidden_blocks)
    came1a = [plane_shift(up0, 1, False), plane_shift(down0, 3, False)]
    hat, value_back, dots, head_parts = call(
        attend_back_kernel,
        [((SEQ, 512), F32), ((SEQ, 256), LOW), ((8, SEQ), F32), ((2, 256), F32)],
        qkv, scales, head_gains, *tables, low, mix_own, mix_other, *mixes,
        scratch=[pltpu.VMEM((SEQ, HEAD), F32)] * 2 + [pltpu.VMEM((SEQ, 256), LOW)],
    )
    hat, dots, came1a, up1, down1 = lax.optimization_barrier((hat, dots, came1a, up1, down1))
    came1b = [plane_shift(up1, 1, False), plane_shift(down1, 3, False)]
    dots, came1b, far1 = lax.optimization_barrier((all_stats(dots), came1b, far1))
    came0[2] = plane_shift(after(grads0[2], dots), 2, False)
    came1 = plane_shift(far1, 2, False)
    (qkv_back,) = call(
        qkv_back_kernel, [((SEQ, SEQ), LOW)], hat, qkv, scales, dots, value_back
    )
    came = core_swap(qkv_down(qkv_back, 1, qkv_blocks, LOW))
    input_parts = settle_ordered(at, qkv_down(qkv_back, 0, qkv_blocks, F32), came)
    input_parts, qkv_back = lax.optimization_barrier((input_parts, qkv_back))

    input_sum = lax.psum_scatter(input_parts, "z", scatter_dimension=0, tiled=True)
    attn_grads = weight_grad(
        at.columns,
        [states, qkv_back, mix_own, mix_other, mixed],
        [(0, SEQ, [(0, 1, 0)]), (0, 256, [(2, 4, 0), (3, 4, OWN)])],
        [attn_gain_part, ffn_gain_part, jnp.pad(head_parts.reshape(16, 32), ((0, 0), (0, 96)))],
    )
    input_sum, attn_grads = lax.optimization_barrier((input_sum, attn_grads))
    input_low = (input_sum.astype(F32) + hidden_rows).astype(LOW)
    near, far = input_low[:, :NEAR], input_low[:, NEAR:]
    flip = at.c == 1
    input_sent = [jnp.where(flip, far, near), jnp.where(flip, near, far)]
    input_rows = shuffled_of(at, input_sent, shuffle(input_sent))
    input_rows, attn_grads, came0, came1 = lax.optimization_barrier(
        (jnp.concatenate(input_rows), attn_grads, came0, came1)
    )
    input_rows = lax.all_gather(input_rows, "z", axis=0, tiled=True)
    attn_came = [plane_shift(attn_grads[i], i, False) for i in range(1, RING)]
    steps = jnp.arange(8, dtype=jnp.int32)
    from_part = at.s ^ at.c ^ (steps // RING)
    from_z = (at.z - steps) % RING
    block_out = order_rows(
        at, shuffled_of(at, sent, after(shuffled, input_low)), from_z, from_part
    )
    (input_grad,) = call(
        widen_kernel, [((SEQ, NEAR), F32)],
        (steps % RING * 2 + from_part).astype(jnp.int32), input_rows,
        scalars=1,
    )

    block_out, came0, came1, came1a, came1b = lax.optimization_barrier(
        (block_out, came0, came1, came1a, came1b)
    )
    rows0 = plane_parts(grads0[0], [came0[i] for i in (1, 2, 3)])
    came1b = [jnp.concatenate(halves, axis=1) for halves in zip(came1a, came1b)]
    rows1 = plane_parts(keep1, [*came1b, came1])
    ffn_rows = [jnp.concatenate(rows) for rows in zip(rows0, rows1)]
    ffn_came = {i: plane_shift(ffn_rows[i], i, True) for i in (1, 3)}
    attn_came, ffn_came = lax.optimization_barrier((attn_came, ffn_came))
    ffn_came[2] = plane_shift(after(ffn_rows[2], ffn_came), 2, True)
    attn_rows = plane_sum(attn_grads[0], attn_came)
    attn_came = [plane_shift(attn_rows[i], i, True) for i in range(1, RING)]
    attn_came, input_grad = lax.optimization_barrier((attn_came, input_grad))
    gate_out, up_out, down_out = share_cores(
        at,
        ffn_rows[0],
        [ffn_came[i] for i in (1, 2, 3)],
        [[(0, 0, 1024)], [(0, 1024, 512), (1, 0, 512)], [(1, 512, 1024)]],
    )
    query, key, value, mix_out, width, heads = share_cores(
        at, attn_rows[0], attn_came, [[(0, i, 256)] for i in range(0, 1024, 256)],
        [(8, 128), (16, 128)],
    )
    width = jnp.where(flip, width[:2, 64:], width[:2, :64])
    heads = jnp.where(at.s == 0, heads[2:4, :32], heads[10:12, :32])
    heads = jnp.where(flip, heads[:, 16:], heads[:, :16])

    return (
        block_out, input_grad, query, key, value, mix_out.T, gate_out, up_out, down_out.T,
        width[0], width[1], heads[0], heads[1],
    )


def solution(mesh):
    fine = Mesh(mesh.devices.reshape(4, 2, 2, 4, 2), ("y", "xh", "core", "z", "xl"))
    dp = ("y", "xh", "core")
    row, col = "z", "xl"
    return jax.shard_map(
        local,
        mesh=fine,
        in_specs=(
            P(dp, col), P(dp), P(col, row), P(col, row), P(col, row), P(row, col),
            P(col, row), P(col, row), P(row, col), P(col), P(col), P((row, col)),
            P((row, col)), P(dp, col),
        ),
        out_specs=(
            P(dp, col), P(dp, col),
            P((col,) + dp, row), P((col,) + dp, row), P((col,) + dp, row), P(row, (col,) + dp),
            P((col,) + dp, row), P((col,) + dp, row), P(row, (col,) + dp),
            P((col,) + dp), P((col,) + dp), P((row, col) + dp), P((row, col) + dp),
        ),
        check_vma=False,
    )
```

```python
import functools

import jax
import jax.numpy as jnp
from jax import lax
from jax.experimental import pallas as pl
from jax.experimental.pallas import tpu as pltpu
from jax.sharding import Mesh, PartitionSpec as P

D = 2048
HEAD = 128
SEQ = 768
NEAR = D // 2
OWN = SEQ // 2
RING = 4
BLOCK = SEQ // 8
EPSILON = 1e-06
ROPE_BASE = 500000.0
MASKED = -1e30
LOW = jnp.bfloat16
F32 = jnp.float32
FREE = pl.CostEstimate(flops=0, bytes_accessed=0, transcendentals=0)
PARAMS = pltpu.CompilerParams(vmem_limit_bytes=24 * 1024 * 1024)
EARLY = pltpu.CompilerParams(vmem_limit_bytes=60 * 1024 * 1024)


def dot(a, b, dims=((1,), (0,))):
    return lax.dot_general(a, b, (dims, ((), ())), preferred_element_type=F32)


NT = ((1,), (1,))
TN = ((0,), (0,))


def after(value, *earlier):
    return lax.optimization_barrier((value, earlier))[0]


def ring_shift(a, axes, step):
    return lax.ppermute(a, axes, [(i, (i + step) % RING) for i in range(RING)])


def z_shift(a, step):
    return ring_shift(a, "z", step)


def plane_shift(a, step, swapped):
    pairs = []
    for y in range(4):
        for x in range(4):
            for c in range(2):
                there = ((y + step) % 4, x) if (c == 0) != swapped else (y, (x + step) % 4)
                xh, xl = x // 2, x % 2
                source = ((y * 2 + xh) * 2 + c) * 2 + xl
                pairs.append((source, ((there[0] * 2 + there[1] // 2) * 2 + c) * 2 + there[1] % 2))
    return lax.ppermute(a, ("y", "xh", "core", "xl"), pairs)


def core_swap(a):
    return lax.ppermute(a, "core", [(0, 1), (1, 0)])


def pair_swap(a):
    return lax.ppermute(a, "xl", [(0, 1), (1, 0)])


def wrap_swap(a):
    return lax.ppermute(a, ("xh", "xl"), [(0, 3), (3, 0), (1, 2), (2, 1)])


def pick(blocks, index, axis=0):
    return lax.dynamic_index_in_dim(blocks, index, axis, keepdims=False)


class Place:
    def __init__(self):
        self.s = lax.axis_index("xl")
        self.xh = lax.axis_index("xh")
        self.x = self.xh * 2 + self.s
        self.y = lax.axis_index("y")
        self.c = lax.axis_index("core")
        self.z = lax.axis_index("z")
        self.home = self.c == self.s
        self.z_scalar = self.z.reshape(1).astype(jnp.int32)
        steps = jnp.arange(RING, dtype=jnp.int32)
        self.back = (self.z - steps) % RING
        self.rows = jnp.concatenate([self.c * 4 + self.back, (1 - self.c) * 4 + self.back])
        first, second = steps[:, None], steps[None, :]
        dx = jnp.where(self.c == 0, second, first)
        dy = jnp.where(self.c == 0, first, second)
        self.columns = (
            (dx % 2) * 8 + ((self.y + dy) % 4) * 2 + ((self.x + dx) % 4) // 2
        ).reshape(-1)
        y, x = first, second
        self.plain = (((x % 2) ^ self.s) * 8 + y * 2 + x // 2).reshape(-1)


def place_kernel(plan, sources, table, *refs):
    ins, outs, sems = refs[:sources], refs[sources:-1], refs[-1]
    copies = []
    for i, (source, there) in enumerate(plan(table, ins, outs)):
        copies.append(pltpu.make_async_copy(source, there, sems.at[i]))
        copies[-1].start()
    for copy in copies:
        copy.wait()


def place(plan, count, shapes, table, *sources, params=PARAMS):
    return pl.pallas_call(
        functools.partial(place_kernel, plan, len(sources)),
        in_specs=[pl.BlockSpec(memory_space=pltpu.SMEM)]
        + [pl.BlockSpec(memory_space=pltpu.HBM)] * len(sources),
        out_specs=tuple(pl.BlockSpec(memory_space=pltpu.VMEM) for _ in shapes),
        out_shape=tuple(jax.ShapeDtypeStruct(shape, LOW) for shape in shapes),
        scratch_shapes=[pltpu.SemaphoreType.DMA((count,))],
        compiler_params=params,
        cost_estimate=FREE,
    )(jnp.stack(table).astype(jnp.int32), *sources)


def at_block(index, size):
    return pl.ds(pl.multiple_of(index * size, size), size)


def first_hop(a):
    return lax.ppermute(a, ("core", "xl"), [(0, 2), (3, 1), (2, 3), (1, 0)])


def second_hop(first):
    return lax.ppermute(first, ("core", "xl"), [(0, 2), (3, 1)])


def sequence_kernel(count, table, a_ref, first_ref, second_ref, out_ref, sems):
    def move(near, far):
        copies = []
        for i in range(count):
            block = at_block(table[i], BLOCK)
            there = pl.ds(i * BLOCK, BLOCK)
            for source, lo in ((near.at[block], 0), (far.at[block], NEAR)):
                copies.append(
                    pltpu.make_async_copy(
                        source, out_ref.at[there, pl.ds(lo, NEAR)], sems.at[len(copies)]
                    )
                )
        for copy in copies:
            copy.start()
        for copy in copies:
            copy.wait()

    pl.when(table[count] == 1)(functools.partial(move, a_ref, first_ref))
    pl.when(table[count] == 0)(functools.partial(move, first_ref, second_ref))


def to_sequence(at, a, first, second, count=8):
    table = jnp.concatenate([at.rows[:count], at.home[None].astype(jnp.int32)])
    return pl.pallas_call(
        functools.partial(sequence_kernel, count),
        in_specs=[pl.BlockSpec(memory_space=pltpu.SMEM)]
        + [pl.BlockSpec(memory_space=pltpu.HBM)] * 3,
        out_specs=pl.BlockSpec(memory_space=pltpu.VMEM),
        out_shape=jax.ShapeDtypeStruct((count * BLOCK, D), LOW),
        scratch_shapes=[pltpu.SemaphoreType.DMA((2 * count,))],
        compiler_params=PARAMS,
        cost_estimate=FREE,
    )(table.astype(jnp.int32), a, first, second)


def order_rows(at, sources, index, which):
    joined = jnp.concatenate(sources) if len(sources) > 1 else sources[0]
    rows = sources[0].shape[0] // BLOCK

    def plan(table, ins, outs):
        return [
            (ins[0].at[at_block(table[i], BLOCK)], outs[0].at[pl.ds(i * BLOCK, BLOCK)])
            for i in range(8)
        ]

    table = index + rows * which if len(sources) > 1 else index * 2 + which
    return place(plan, 8, [(SEQ, joined.shape[1])], list(table), joined)[0]


def cut_columns(at, heights, *weights):
    width = weights[0].shape[1] // 2
    starts = [sum(heights[:i]) for i in range(len(heights))]

    def plan(table, ins, outs):
        return [
            (
                ref.at[pl.ds(start, height), at_block(table[0], width)],
                out.at[:, pl.ds(width * i, width)],
            )
            for i, ref in enumerate(ins)
            for start, height, out in zip(starts, heights, outs)
        ]

    shapes = [(height, width * len(weights)) for height in heights]
    return place(plan, len(heights) * len(weights), shapes, [at.c], *weights, params=EARLY)


PIECES = (
    (("gate", 0), ("mix", 0)), (("gate", 1), ("mix", 1)),
    (("gate", 2), ("up", 0)), (("gate", 3), ("up", 1)),
    (("up", 2), ("down", 0)), (("up", 3), ("down", 1)),
    (("down", 2),), (("down", 3),),
)
PART = 256


def part_height(name):
    return 128 if name == "mix" else PART


def part_starts(piece):
    heights = [part_height(name) for name, _ in piece]
    return [sum(heights[:i]) for i in range(len(heights) + 1)]


def cut_pieces(at, w_gate, w_up, w_down, w_mix):
    def plan(table, ins, outs):
        named = dict(zip(("gate", "up", "down", "mix"), ins))
        copies = []
        for out, piece in zip(outs, PIECES):
            for start, (name, part) in zip(part_starts(piece), piece):
                height = part_height(name)
                if name in ("down", "mix"):
                    half = named[name].shape[0] // 2
                    first = pl.multiple_of(table[0] * half + height * part, height)
                    source = named[name].at[pl.ds(first, height)]
                else:
                    rows = pl.ds(height * part, height)
                    source = named[name].at[rows, at_block(table[0], NEAR)]
                copies.append((source, out.at[pl.ds(start, height)]))
        return copies

    shapes = [(part_starts(piece)[-1], NEAR) for piece in PIECES]
    count = sum(len(piece) for piece in PIECES)
    return place(plan, count, shapes, [at.c], w_gate, w_up, w_down, w_mix, params=EARLY)


def pieces_with(name):
    return [k for k, piece in enumerate(PIECES) if name in dict(piece)]


def views(name, refs):
    out = []
    for ref, k in zip(refs, pieces_with(name)):
        for start, (found, _) in zip(part_starts(PIECES[k]), PIECES[k]):
            if found == name:
                out.append(ref.at[pl.ds(start, part_height(name))])
    return out


def join_columns(parts):
    starts = [sum(part.shape[1] for part in parts[:i]) for i in range(len(parts) + 1)]

    def plan(table, ins, outs):
        return [
            (ref, outs[0].at[:, pl.ds(starts[i], parts[i].shape[1])]) for i, ref in enumerate(ins)
        ]

    return place(plan, len(parts), [(D, starts[-1])], [0], *parts)[0]


def fetch(first, second):
    return pair_swap(first), wrap_swap(second)


def scatter_z(parts):
    total = parts[0]
    for i in range(1, RING):
        total = total + z_shift(parts[i], -i).astype(F32)
    return total


def gather_z(rows):
    return [rows] + [z_shift(rows, i) for i in range(1, RING)]


def all_stats(pair):
    theirs = core_swap(pair)
    pair = pair + jnp.concatenate([theirs[:, OWN:], theirs[:, :OWN]], axis=1)
    total = pair
    for i in range(1, RING):
        came, cut = z_shift(pair, i), OWN - i * BLOCK
        total = total + jnp.concatenate(
            [came[:, cut:OWN], came[:, :cut], came[:, OWN + cut :], came[:, OWN : OWN + cut]],
            axis=1,
        )
    return total


def plane_sum(own, came):
    total = own.astype(F32) + came[0].astype(F32) + came[1].astype(F32) + came[2].astype(F32)
    total = lax.optimization_barrier(total.astype(LOW))
    height = own.shape[0] // RING
    return [total[height * i : height * (i + 1)] for i in range(RING)]


def sum_kernel(p0, p1, p2, p3, *outs):
    for i, out in enumerate(outs):
        at = slice(128 * i, 128 * (i + 1))
        total = p0[at, :].astype(F32) + p1[at, :].astype(F32)
        out[...] = (total + p2[at, :].astype(F32) + p3[at, :].astype(F32)).astype(LOW)


def plane_parts(own, came):
    return call(sum_kernel, [((128, own.shape[1]), LOW)] * RING, own, *came)


def share_kernel(core, p0, p1, p2, p3, own_ref, sent_ref):
    total = p0[...].astype(F32) + p1[...].astype(F32) + p2[...].astype(F32) + p3[...].astype(F32)
    flip = core[0] == 1
    for i in range(total.shape[0] // 128):
        at = slice(64 * i, 64 * (i + 1))
        low, high = total[128 * i : 128 * i + 64, :], total[128 * i + 64 : 128 * (i + 1), :]
        own_ref[at, :] = jnp.where(flip, high, low)
        sent_ref[at, :] = jnp.where(flip, low, high).astype(LOW)
    rest = total.shape[0] % 128
    if rest:
        own_ref[-rest:, :] = total[-rest:, :]
        sent_ref[-rest:, :] = total[-rest:, :].astype(LOW)


def wide_kernel(plan, core, own_ref, came_ref, *outs):
    first = core[0] == 0
    own, came = own_ref[...], came_ref[...].astype(F32)
    sides = jnp.where(first, own, came), jnp.where(first, came, own)
    for out, pieces in zip(outs, plan):
        at = 0
        for side in sides:
            for rows, start, width in pieces:
                value = side[64 * rows : 64 * (rows + 1), start : start + width]
                out[:, at : at + width] = value
                at += width
    if len(outs) > len(plan):
        width_ref, heads_ref = outs[len(plan) :]
        zero, one = (side[-16:-8, :128] for side in sides)
        width_ref[...] = zero + one
        heads_ref[0:8, :] = zero
        heads_ref[8:16, :] = one


def share_cores(at, own, came, plan, extra=()):
    height, width = own.shape
    shape = (height // 128 * 64 + height % 128, width)
    core = at.c.reshape(1).astype(jnp.int32)
    own, sent = call(share_kernel, [(shape, F32), (shape, LOW)], core, own, *came, scalars=1)
    widths = [2 * sum(piece[2] for piece in pieces) for pieces in plan]
    shapes = [((64, width), F32) for width in widths]
    shapes += [(shape, F32) for shape in extra]
    return call(functools.partial(wide_kernel, plan), shapes, core, own, core_swap(sent), scalars=1)


def call(kernel, shapes, *args, scratch=(), scalars=0):
    return pl.pallas_call(
        kernel,
        in_specs=[
            pl.BlockSpec(memory_space=pltpu.SMEM if i < scalars else pltpu.VMEM)
            for i in range(len(args))
        ],
        out_shape=tuple(jax.ShapeDtypeStruct(shape, dtype) for shape, dtype in shapes),
        scratch_shapes=list(scratch),
        compiler_params=PARAMS,
        cost_estimate=FREE,
    )(*args)


def row_dot(rows, refs, at):
    value = 0.0
    start = 0
    for ref in refs:
        height = ref.shape[0]
        value += dot(rows[:, start : start + height], ref[:, at])
        start += height
    return value


def strips(width, size):
    return [slice(i, i + size) for i in range(0, width, size)]


def as_rows(first, second):
    return jnp.concatenate([first, second, jnp.zeros((SEQ, 6), F32)], axis=1).T


def qkv_kernel(states_ref, *refs):
    *blocks, qkv_ref, sums_ref = refs
    sums = []
    for at in strips(SEQ, 256):
        value = row_dot(states_ref, blocks, at)
        qkv_ref[:, at] = value
        sums.append(jnp.sum(value * value, axis=1, keepdims=True))
    sums_ref[...] = as_rows(*sums[:2])


def product_kernel(body, *refs):
    *refs, out_ref = refs
    for at, value in body(refs):
        out_ref[:, at] = value.astype(out_ref.dtype)


def product(body, dtype, *args):
    return call(functools.partial(product_kernel, body), [((OWN, D), dtype)], *args)[0]


def half_rows(ref, half):
    return ref[OWN * half : OWN * (half + 1), :]


def mix(left, half, pieces, dtype):
    count = len(pieces) // 2

    def body(refs):
        left, *w = refs
        left = half_rows(left, half)
        for i in range(2):
            blocks = views("mix", w[count * i : count * (i + 1)])
            for at in strips(NEAR, 512):
                yield slice(NEAR * i + at.start, NEAR * i + at.stop), row_dot(left, blocks, at)

    return product(body, dtype, left, *pieces)


def down(units, pieces, dtype):
    count = len(pieces) // 2

    def body(refs):
        units, *w = refs
        for i in range(2):
            blocks = views("down", w[count * i : count * (i + 1)])
            for at in strips(NEAR, 512):
                yield slice(NEAR * i + at.start, NEAR * i + at.stop), row_dot(units, blocks, at)

    return product(body, dtype, units, *pieces)


def pair_down(gate_back, up_back, gates, ups, dtype):
    def body(refs):
        gate_back, up_back, *w = refs
        for i in range(2):
            n, m = len(gates) // 2, len(ups) // 2
            gate = views("gate", w[n * i : n * (i + 1)])
            up = views("up", w[2 * n + m * i : 2 * n + m * (i + 1)])
            for k in range(4):
                value = dot(gate_back[...], gate[k][...], NT) + dot(up_back[...], up[k][...], NT)
                yield slice(NEAR * i + PART * k, NEAR * i + PART * (k + 1)), value

    return product(body, dtype, gate_back, up_back, *gates, *ups)


def qkv_down(back, half, blocks, dtype):
    def body(refs):
        back, *w = refs
        back = half_rows(back, half)
        start = 0
        for ref in w:
            for at in strips(ref.shape[0], 256):
                yield slice(start + at.start, start + at.stop), dot(back, ref[at, :], NT)
            start += ref.shape[0]

    return product(body, dtype, back, *blocks)


def settle_kernel(own_ref, came_ref, *outs):
    for i, ref in enumerate(outs):
        at = slice(i * BLOCK, (i + 1) * BLOCK)
        ref[...] = (own_ref[at, :] + came_ref[at, :].astype(F32)).astype(ref.dtype)


def settle(own, came):
    return call(
        settle_kernel, [((BLOCK, D), F32)] + [((BLOCK, D), LOW)] * 3, own, came
    )


def z_rows(z, i):
    return pl.ds(pl.multiple_of(lax.rem(z + RING - i, RING) * BLOCK, BLOCK), BLOCK)


def settle_ordered_kernel(z_ref, own_ref, came_ref, out_ref):
    for i in range(RING):
        at = slice(i * BLOCK, (i + 1) * BLOCK)
        value = own_ref[at, :] + came_ref[at, :].astype(F32)
        out_ref[z_rows(z_ref[0], i), :] = value.astype(LOW)


def settle_ordered(at, own, came):
    return call(settle_ordered_kernel, [((OWN, D), LOW)], at.z_scalar, own, came, scalars=1)[0]


def units_kernel(n, m, rows_ref, *refs):
    gate_ref, up_ref, units_ref = refs[-3:]
    gates = views("gate", refs[:n]) + views("gate", refs[n : 2 * n])
    ups = views("up", refs[2 * n : 2 * n + m]) + views("up", refs[2 * n + m : 2 * n + 2 * m])
    for at in strips(1024, 512):
        gate, up = row_dot(rows_ref, gates, at), row_dot(rows_ref, ups, at)
        gate_ref[:, at] = gate.astype(LOW)
        up_ref[:, at] = up.astype(LOW)
        units_ref[:, at] = (gate * jax.nn.sigmoid(gate) * up).astype(LOW)


def units_of(rows, gates, ups):
    kernel = functools.partial(units_kernel, len(gates) // 2, len(ups) // 2)
    return call(kernel, [((OWN, 1024), LOW)] * 3, rows, *gates, *ups)


def units_back_kernel(branch_ref, *refs):
    *w, gate_ref, up_ref, gate_back_ref, up_back_ref = refs
    count = len(w) // 2
    near, far = views("down", w[:count]), views("down", w[count:])
    for k in range(4):
        at = slice(PART * k, PART * (k + 1))
        grad = dot(branch_ref[:, :NEAR], near[k][...], NT)
        grad += dot(branch_ref[:, NEAR:], far[k][...], NT)
        gate, up = gate_ref[:, at].astype(F32), up_ref[:, at].astype(F32)
        sigmoid = jax.nn.sigmoid(gate)
        gate_back_ref[:, at] = (grad * up * sigmoid * (1.0 + gate * (1.0 - sigmoid))).astype(LOW)
        up_back_ref[:, at] = (grad * gate * sigmoid).astype(LOW)


def units_back(branch, pieces, gate, up):
    return call(units_back_kernel, [((OWN, 1024), LOW)] * 2, branch, *pieces, gate, up)


def grad_kernel(plan, count, extras, cut, *refs):
    table, ins = refs[0], refs[1 : 1 + count]
    extra, outs = refs[1 + count : 1 + count + extras], refs[1 + count + extras :]
    if cut:
        outs = [(outs[0],), outs[1:3], (outs[3],), outs[4:6]]
    for d in range(RING):
        blocks = [table[4 * d + e] for e in range(RING)]
        places = [at_block(block, 128) for block in blocks]
        start = 0
        for lo, width, terms in plan:
            value = 0.0
            for left, right, row in terms:
                left, right = ins[left], ins[right]
                chosen = jnp.concatenate([left[:, place] for place in places], axis=1)
                value += dot(chosen, right[row : row + left.shape[0], lo : lo + width], TN)
            value = value.astype(LOW)
            at = slice(start, start + width)
            if cut:
                put_columns(outs[d], start, value)
            elif not extras:
                outs[d][:, at] = value
            else:
                for e in range(RING):
                    outs[d][144 * e : 144 * e + 128, at] = value[128 * e : 128 * (e + 1)]
            start += width
        if extras:
            attn_ref, ffn_ref, heads_ref = extra
            for e in range(RING):
                block = lax.rem(blocks[e], 8)
                rows = [attn_ref[0:1, places[e]], ffn_ref[0:1, places[e]]]
                rows += [heads_ref[pl.ds(block + 8 * i, 1), :] for i in range(2)]
                rows = jnp.concatenate([*rows, jnp.zeros((12, 128), F32)])
                at = slice(144 * e + 128, 144 * (e + 1))
                outs[d][at, :128] = rows.astype(LOW)
                outs[d][at, 128:] = jnp.zeros((16, start - 128), LOW)


def put_columns(outs, start, value):
    at = 0
    for out in outs:
        lo, hi = max(start, at), min(start + value.shape[1], at + out.shape[1])
        if lo < hi:
            out[:, lo - at : hi - at] = value[:, lo - start : hi - start]
        at += out.shape[1]


def weight_grad(table, arrays, plan, extra=(), cut=False):
    width = sum(span[1] for span in plan)
    height = 576 if extra else 512
    kernel = functools.partial(grad_kernel, plan, len(arrays), len(extra), cut)
    widths = [width, width // 2, width // 2, width, width // 2, width // 2] if cut else [width] * RING
    outs = [((height, w), LOW) for w in widths]
    return call(kernel, outs, table.astype(jnp.int32), *arrays, *extra, scalars=1)


def turn(v, cosines, sines):
    return v * cosines + pltpu.roll(v, HEAD // 2, 1) * sines


def turn_back(v, cosines, sines):
    return v * cosines - pltpu.roll(v, HEAD // 2, 1) * sines


TILE = 384


def seen(table_ref, row_ref, lo):
    here = table_ref[lo : lo + TILE, 2 * HEAD : 3 * HEAD]
    there = row_ref[0:1, :]
    return (there <= here[:, 0:1]) & (there >= here[:, 1:2])


def attend_kernel(
    qkv_ref, sums_ref, gain_ref, table_ref, row_ref, mixed_ref, low_ref, scale_ref
):
    cosines, sines = table_ref[:, :HEAD], table_ref[:, HEAD : 2 * HEAD]
    scale_ref[...] = lax.rsqrt(sums_ref[...] * (1.0 / D) + EPSILON).T
    for h in range(2):
        at = slice(h * HEAD, (h + 1) * HEAD)
        k_at = slice(256 + h * HEAD, 256 + (h + 1) * HEAD)
        q = qkv_ref[:, at] * scale_ref[:, 0:1] * gain_ref[0:1, at]
        k = qkv_ref[:, k_at] * scale_ref[:, 1:2] * gain_ref[1:2, at]
        low_ref[:, at] = turn(q, cosines, sines).astype(LOW)
        k = turn(k, cosines, sines).astype(LOW)
        v = qkv_ref[:, 512 + h * HEAD : 512 + (h + 1) * HEAD].astype(LOW)
        low_ref[:, k_at] = k
        low_ref[:, 512 + h * HEAD : 512 + (h + 1) * HEAD] = v
        for lo in range(0, SEQ, TILE):
            q = low_ref[lo : lo + TILE, at]
            scores = dot(q, k, NT) * HEAD**-0.5
            scores = jnp.where(seen(table_ref, row_ref, lo), scores, MASKED)
            peak = jnp.max(scores, axis=1, keepdims=True)
            weights = jnp.exp(scores - peak)
            total = jnp.sum(weights, axis=1, keepdims=True)
            weights = (weights * (1.0 / total)).astype(LOW)
            mixed_ref[lo : lo + TILE, at] = dot(weights, v).astype(LOW)
            scale_ref[lo : lo + TILE, 2 + h : 3 + h] = peak + jnp.log(total)


def attend_back_kernel(
    qkv_ref, scale_ref, gain_ref, table_ref, row_ref, low_ref,
    own_ref, other_ref, near0, near1, far0, far1,
    hat_ref, value_ref, dots_ref, part_ref, dk_ref, dv_ref, grad_ref,
):
    cosines, sines = table_ref[:, :HEAD], table_ref[:, HEAD : 2 * HEAD]
    for i, ref in enumerate((own_ref, other_ref)):
        pairs = zip(views("mix", (near0, near1)), views("mix", (far0, far1)))
        for k, (near, far) in enumerate(pairs):
            grad = dot(ref[:, :NEAR], near[...], NT) + dot(ref[:, NEAR:], far[...], NT)
            grad_ref[OWN * i : OWN * (i + 1), 128 * k : 128 * (k + 1)] = grad.astype(LOW)
    for h in range(2):
        at = slice(h * HEAD, (h + 1) * HEAD)
        k_at = slice(256 + h * HEAD, 256 + (h + 1) * HEAD)
        k = low_ref[:, k_at]
        v = low_ref[:, 512 + h * HEAD : 512 + (h + 1) * HEAD]
        for lo in range(0, SEQ, TILE):
            q = low_ref[lo : lo + TILE, at]
            grad = grad_ref[lo : lo + TILE, at]
            scores = dot(q, k, NT) * HEAD**-0.5
            weights = jnp.exp(scores - scale_ref[lo : lo + TILE, 2 + h : 3 + h])
            weights = jnp.where(seen(table_ref, row_ref, lo), weights, 0.0)
            weight_grad = dot(grad, v, NT)
            centre = jnp.sum(weights * weight_grad, axis=1, keepdims=True)
            score_grad = (weights * (weight_grad - centre)).astype(LOW)
            hat_ref[lo : lo + TILE, at] = dot(score_grad, k) * HEAD**-0.5
            value_part = dot(weights.astype(LOW), grad, TN)
            key_part = dot(score_grad, q, TN)
            if lo == 0:
                dv_ref[...] = value_part
                dk_ref[...] = key_part
            else:
                dv_ref[...] += value_part
                dk_ref[...] += key_part
        value_ref[:, at] = dv_ref[...].astype(LOW)
        q_grad = turn_back(hat_ref[:, at], cosines, sines)
        k_grad = turn_back(dk_ref[...] * HEAD**-0.5, cosines, sines)
        q, k = qkv_ref[:, at], qkv_ref[:, k_at]
        part_ref[0:1, at] = jnp.sum(q_grad * q * scale_ref[:, 0:1], axis=0, keepdims=True)
        part_ref[1:2, at] = jnp.sum(k_grad * k * scale_ref[:, 1:2], axis=0, keepdims=True)
        hat_ref[:, at] = q_grad * gain_ref[0:1, at]
        hat_ref[:, k_at] = k_grad * gain_ref[1:2, at]
    dots_ref[...] = as_rows(
        jnp.sum(hat_ref[:, :256] * qkv_ref[:, :256], axis=1, keepdims=True),
        jnp.sum(hat_ref[:, 256:] * qkv_ref[:, 256:512], axis=1, keepdims=True),
    )


def qkv_back_kernel(hat_ref, qkv_ref, rms_ref, dots_ref, value_ref, out_ref):
    dots = dots_ref[...].T
    for i in range(2):
        at = slice(i * 256, (i + 1) * 256)
        rms = rms_ref[:, i : i + 1]
        coefficient = rms * rms * rms * dots[:, i : i + 1] * (1.0 / D)
        out_ref[:, at] = (rms * hat_ref[:, at] - qkv_ref[:, at] * coefficient).astype(LOW)
    out_ref[:, 512:] = value_ref[...]


def widen_kernel(table, rows_ref, out_ref):
    for i in range(8):
        block = pl.ds(pl.multiple_of(table[i] * BLOCK, BLOCK), BLOCK)
        out_ref[i * BLOCK : (i + 1) * BLOCK, :] = rows_ref[block, :].astype(F32)


def blocks_of(ref):
    return [slice(i * BLOCK, (i + 1) * BLOCK) for i in range(ref.shape[0] // BLOCK)]


def hidden_kernel(b0, b1, b2, b3, states_ref, gain_ref, low_ref, rms_ref):
    for at, ref in zip(blocks_of(low_ref), (b0, b1, b2, b3)):
        branch = ref[...].astype(F32)
        rms = lax.rsqrt(jnp.mean(branch * branch, axis=1, keepdims=True) + EPSILON)
        hidden = states_ref[at, :].astype(F32) + gain_ref[...] * branch * rms
        low_ref[at, :] = hidden.astype(LOW)
        rms_ref[at, :] = rms


def back_of(upstream, branch, rms, gain):
    part = jnp.sum(upstream * branch * rms, axis=0, keepdims=True)
    scaled = upstream * gain
    inner = jnp.sum(scaled * branch, axis=1, keepdims=True)
    return rms * scaled - branch * (rms * rms * rms * inner * (1.0 / D)), part


def ffn_back_kernel(b0, b1, b2, b3, upstream_ref, gain_ref, back_ref, rms_ref, part_ref):
    for i, (at, ref) in enumerate(zip(blocks_of(back_ref), (b0, b1, b2, b3))):
        branch = ref[...].astype(F32)
        rms = lax.rsqrt(jnp.mean(branch * branch, axis=1, keepdims=True) + EPSILON)
        back, part = back_of(upstream_ref[at, :].astype(F32), branch, rms, gain_ref[...])
        back_ref[at, :] = back.astype(LOW)
        rms_ref[at, :] = rms
        part_ref[...] = part if i == 0 else part_ref[...] + part


def attn_back_kernel(
    g0, g1, g2, g3, b0, b1, b2, b3, upstream_ref, rms_ref, gain_ref, back_ref, part_ref
):
    pairs = zip(blocks_of(back_ref), (g0, g1, g2, g3), (b0, b1, b2, b3))
    for i, (at, grad_ref, ref) in enumerate(pairs):
        grad = grad_ref[...].astype(F32) + upstream_ref[at, :].astype(F32)
        back, part = back_of(grad, ref[...].astype(F32), rms_ref[at, :], gain_ref[...])
        back_ref[at, :] = back.astype(LOW)
        part_ref[...] = part if i == 0 else part_ref[...] + part


def out_kernel(
    core_ref, a0, a1, a2, a3, b0, b1, b2, b3, states_ref, attn_rms_ref, ffn_rms_ref,
    attn_gain_ref, ffn_gain_ref, sent0_ref, sent1_ref,
):
    pairs = zip(blocks_of(states_ref), (a0, a1, a2, a3), (b0, b1, b2, b3))
    flip = core_ref[0] == 1
    for at, a_ref, b_ref in pairs:
        value = (
            states_ref[at, :].astype(F32)
            + attn_gain_ref[...] * a_ref[...].astype(F32) * attn_rms_ref[at, :]
            + ffn_gain_ref[...] * b_ref[...].astype(F32) * ffn_rms_ref[at, :]
        ).astype(LOW)
        near, far = value[:, :NEAR], value[:, NEAR:]
        sent0_ref[at, :] = jnp.where(flip, far, near)
        sent1_ref[at, :] = jnp.where(flip, near, far)


def shuffle(sent):
    out = []
    for k in range(2):
        perm = [(c * 2 + s, s * 2 + (s ^ c ^ k)) for s in range(2) for c in range(2)]
        out.append(lax.ppermute(sent[k], ("core", "xl"), [p for p in perm if p[0] != p[1]]))
    return out


def shuffled_of(at, sent, came):
    return [jnp.where((at.s == k) & (at.c == k), sent[k], came[k]) for k in range(2)]


def local(
    inputs, segments, w_query, w_key, w_value, w_mix, w_gate, w_up, w_down,
    attn_gain, ffn_gain, query_gain, key_gain, out_grad,
):
    at = Place()
    first = first_hop(inputs)
    near_qkv = cut_columns(at, (768, 256), w_query, w_key, w_value)
    far_qkv = [wrap_swap(near_qkv[0]), pair_swap(near_qkv[1])]
    near = cut_pieces(at, after(w_gate, near_qkv), w_up, w_down, w_mix)

    gains = jnp.concatenate([attn_gain, ffn_gain, query_gain, key_gain])
    their_gains = pair_swap(gains)
    attn_gains = jnp.concatenate([attn_gain, their_gains[:NEAR]])[None]
    ffn_gains = jnp.concatenate([ffn_gain, their_gains[NEAR:D]])[None]
    head_gains = jnp.where(at.home, gains[D:], their_gains[D:]).reshape(2, 256)

    segment_ids = jnp.where(at.home, segments, core_swap(segments))
    step_index = jnp.arange(SEQ, dtype=jnp.int32)
    earlier = jnp.concatenate([segment_ids[:1] - 1, segment_ids[:-1]])
    begins = lax.cummax(jnp.where(segment_ids != earlier, step_index, 0))
    chosen = at.rows[:, None, None] == jnp.arange(8, dtype=jnp.int32)[None, :, None]
    begins = jnp.sum(jnp.where(chosen, begins.reshape(1, 8, BLOCK), 0), axis=1).reshape(-1)
    index = (at.rows[:, None] * BLOCK + jnp.arange(BLOCK, dtype=jnp.int32)[None]).reshape(-1)
    frequency = ROPE_BASE ** (-2.0 * jnp.arange(HEAD // 2, dtype=F32) / HEAD)
    angles = (index - begins).astype(F32)[:, None] * frequency
    cosines, sines = jnp.cos(angles), jnp.sin(angles)
    place_columns = jnp.stack([index, begins], axis=1).astype(F32)
    table = jnp.concatenate(
        [cosines, cosines, -sines, sines, jnp.pad(place_columns, ((0, 0), (0, 126)))], axis=1
    )
    tables = (table, index[None].astype(F32))

    tables, head_gains, attn_gains, ffn_gains, at.columns, at.plain, at.rows, near, first = (
        lax.optimization_barrier(
            (tables, head_gains, attn_gains, ffn_gains, at.columns, at.plain, at.rows, near, first)
        )
    )
    states = to_sequence(at, inputs, first, second_hop(after(first, far_qkv)))
    states, far_qkv = lax.optimization_barrier((states, far_qkv))
    qkv_blocks = [*near_qkv, *far_qkv]
    qkv, squares = call(qkv_kernel, [((SEQ, SEQ), F32), ((8, SEQ), F32)], states, *qkv_blocks)
    far = fetch(*after(near[:2], far_qkv))
    squares = all_stats(squares)
    squares = lax.optimization_barrier(squares)
    mixed, low, scales = call(
        attend_kernel,
        [((SEQ, 256), LOW), ((SEQ, SEQ), LOW), ((SEQ, 8), F32)],
        qkv, squares, head_gains, *tables,
    )
    mixed, far = lax.optimization_barrier((mixed, far))
    mixes = [*near[:2], *far[:2]]
    came = core_swap(mix(mixed, 1, mixes, LOW))
    mix_parts = settle(mix(mixed, 0, mixes, F32), came)
    mix_parts = lax.optimization_barrier(mix_parts)
    far = [*far, *fetch(*after(near[2:4], mixed))]
    attn_sum = scatter_z(mix_parts).astype(LOW)
    next_pieces = after(near[4:6], far)
    attn_sum, far = lax.optimization_barrier((attn_sum, far))
    far = [*far, *fetch(*next_pieces)]
    attn_blocks = gather_z(attn_sum)
    own_states = after(states, attn_sum)[:OWN]
    attn_blocks, far, own_states = lax.optimization_barrier((attn_blocks, far, own_states))
    far = [*far, *fetch(*after(near[6:], attn_blocks))]
    hidden_own, attn_rms = call(
        hidden_kernel,
        [((OWN, D), LOW), ((OWN, 1), F32)],
        *attn_blocks, own_states, attn_gains,
    )
    hidden_other = core_swap(hidden_own)

    gates, ups, downs = (
        [side[k] for side in (near, far) for k in pieces_with(name)]
        for name in ("gate", "up", "down")
    )
    gate_own, up_own, units_own = units_of(hidden_own, gates, ups)
    hidden_other = after(hidden_other, units_own)
    gate_other, up_other, units_other = units_of(hidden_other, gates, ups)
    came = core_swap(down(units_other, downs, LOW))
    ffn_parts = settle(down(after(units_own, units_other), downs, F32), came)
    ffn_parts = lax.optimization_barrier(ffn_parts)
    grad_first = first_hop(after(out_grad, ffn_parts))
    ffn_sum = scatter_z(ffn_parts).astype(LOW)
    ffn_sum, grad_first = lax.optimization_barrier((ffn_sum, grad_first))
    ffn_blocks = gather_z(ffn_sum)
    upstream = to_sequence(at, out_grad, grad_first, second_hop(grad_first), RING)
    ffn_blocks, upstream = lax.optimization_barrier((ffn_blocks, upstream))
    branch_own, ffn_rms, ffn_gain_part = call(
        ffn_back_kernel,
        [((OWN, D), LOW), ((OWN, 1), F32), ((1, D), F32)],
        *ffn_blocks, upstream, ffn_gains,
    )
    branch_other = core_swap(branch_own)
    gate_back_own, up_back_own = units_back(branch_own, downs, gate_own, up_own)
    sent = call(
        out_kernel,
        [((OWN, NEAR), LOW)] * 2,
        at.c.reshape(1).astype(jnp.int32), *attn_blocks, *ffn_blocks,
        own_states, attn_rms, after(ffn_rms, gate_back_own), attn_gains, ffn_gains,
        scalars=1,
    )
    branch_other = after(branch_other, gate_back_own, sent)
    gate_back_other, up_back_other = units_back(branch_other, downs, gate_other, up_other)
    came = core_swap(pair_down(gate_back_other, up_back_other, gates, ups, LOW))
    pair_parts = pair_down(after(gate_back_own, gate_back_other), up_back_own, gates, ups, F32)
    pair_parts = settle(pair_parts, came)

    hidden_sum = scatter_z(pair_parts)
    hidden_rows = hidden_sum + upstream[:BLOCK].astype(F32)
    branch_own, hidden_own, pair_parts = lax.optimization_barrier(
        (branch_own, hidden_own, pair_parts)
    )
    shuffled = shuffle(after(sent, pair_parts))
    gate_args = [hidden_own, hidden_other, gate_back_own, gate_back_other]
    up_args = [hidden_own, hidden_other, up_back_own, up_back_other]
    down_args = [branch_own, branch_other, units_own, units_other]
    terms = [(0, 2, 0), (1, 3, 0)]
    grads0 = weight_grad(
        at.columns,
        [*gate_args, *up_args[2:]],
        [(0, 1024, terms), (0, 512, [(0, 4, 0), (1, 5, 0)])],
    )
    hidden_sum, grads0, shuffled, up_args, down_args = lax.optimization_barrier(
        (hidden_sum.astype(LOW), grads0, shuffled, up_args, down_args)
    )

    hidden_blocks = gather_z(hidden_sum)
    came0 = {i: plane_shift(after(grads0[i], hidden_sum), i, False) for i in (1, 3)}
    grads1 = weight_grad(
        at.columns,
        [*up_args, *down_args],
        [(512, 512, terms), (0, 1024, [(4, 6, 0), (5, 7, 0)])],
        cut=True,
    )
    hidden_blocks, came0, grads1 = lax.optimization_barrier((hidden_blocks, came0, grads1))
    mix_own, attn_gain_part = call(
        attn_back_kernel,
        [((OWN, D), LOW), ((1, D), F32)],
        *hidden_blocks, *attn_blocks, upstream, attn_rms, attn_gains,
    )
    mix_other = core_swap(mix_own)

    keep1, up0, up1, far1, down0, down1 = after(grads1, hidden_blocks)
    came1a = [plane_shift(up0, 1, False), plane_shift(down0, 3, False)]
    hat, value_back, dots, head_parts = call(
        attend_back_kernel,
        [((SEQ, 512), F32), ((SEQ, 256), LOW), ((8, SEQ), F32), ((2, 256), F32)],
        qkv, scales, head_gains, *tables, low, mix_own, mix_other, *mixes,
        scratch=[pltpu.VMEM((SEQ, HEAD), F32)] * 2 + [pltpu.VMEM((SEQ, 256), LOW)],
    )
    hat, dots, came1a, up1, down1 = lax.optimization_barrier((hat, dots, came1a, up1, down1))
    came1b = [plane_shift(up1, 1, False), plane_shift(down1, 3, False)]
    dots, came1b, far1 = lax.optimization_barrier((all_stats(dots), came1b, far1))
    came0[2] = plane_shift(after(grads0[2], dots), 2, False)
    came1 = plane_shift(far1, 2, False)
    (qkv_back,) = call(
        qkv_back_kernel, [((SEQ, SEQ), LOW)], hat, qkv, scales, dots, value_back
    )
    came = core_swap(qkv_down(qkv_back, 1, qkv_blocks, LOW))
    input_parts = settle_ordered(at, qkv_down(qkv_back, 0, qkv_blocks, F32), came)
    input_parts, qkv_back = lax.optimization_barrier((input_parts, qkv_back))

    input_sum = lax.psum_scatter(input_parts, "z", scatter_dimension=0, tiled=True)
    attn_grads = weight_grad(
        at.columns,
        [states, qkv_back, mix_own, mix_other, mixed],
        [(0, SEQ, [(0, 1, 0)]), (0, 256, [(2, 4, 0), (3, 4, OWN)])],
        [attn_gain_part, ffn_gain_part, jnp.pad(head_parts.reshape(16, 32), ((0, 0), (0, 96)))],
    )
    input_sum, attn_grads = lax.optimization_barrier((input_sum, attn_grads))
    input_low = (input_sum.astype(F32) + hidden_rows).astype(LOW)
    near, far = input_low[:, :NEAR], input_low[:, NEAR:]
    flip = at.c == 1
    input_sent = [jnp.where(flip, far, near), jnp.where(flip, near, far)]
    input_rows = shuffled_of(at, input_sent, shuffle(input_sent))
    input_rows, attn_grads, came0, came1 = lax.optimization_barrier(
        (jnp.concatenate(input_rows), attn_grads, came0, came1)
    )
    input_rows = lax.all_gather(input_rows, "z", axis=0, tiled=True)
    attn_came = [plane_shift(attn_grads[i], i, False) for i in range(1, RING)]
    steps = jnp.arange(8, dtype=jnp.int32)
    from_part = at.s ^ at.c ^ (steps // RING)
    from_z = (at.z - steps) % RING
    block_out = order_rows(
        at, shuffled_of(at, sent, after(shuffled, input_low)), from_z, from_part
    )
    (input_grad,) = call(
        widen_kernel, [((SEQ, NEAR), F32)],
        (steps % RING * 2 + from_part).astype(jnp.int32), input_rows,
        scalars=1,
    )

    block_out, came0, came1, came1a, came1b = lax.optimization_barrier(
        (block_out, came0, came1, came1a, came1b)
    )
    rows0 = plane_parts(grads0[0], [came0[i] for i in (1, 2, 3)])
    came1b = [jnp.concatenate(halves, axis=1) for halves in zip(came1a, came1b)]
    rows1 = plane_parts(keep1, [*came1b, came1])
    ffn_rows = [jnp.concatenate(rows) for rows in zip(rows0, rows1)]
    ffn_came = {i: plane_shift(ffn_rows[i], i, True) for i in (1, 3)}
    attn_came, ffn_came = lax.optimization_barrier((attn_came, ffn_came))
    ffn_came[2] = plane_shift(after(ffn_rows[2], ffn_came), 2, True)
    attn_rows = plane_sum(attn_grads[0], attn_came)
    attn_came = [plane_shift(attn_rows[i], i, True) for i in range(1, RING)]
    attn_came, input_grad = lax.optimization_barrier((attn_came, input_grad))
    gate_out, up_out, down_out = share_cores(
        at,
        ffn_rows[0],
        [ffn_came[i] for i in (1, 2, 3)],
        [[(0, 0, 1024)], [(0, 1024, 512), (1, 0, 512)], [(1, 512, 1024)]],
    )
    query, key, value, mix_out, width, heads = share_cores(
        at, attn_rows[0], attn_came, [[(0, i, 256)] for i in range(0, 1024, 256)],
        [(8, 128), (16, 128)],
    )
    width = jnp.where(flip, width[:2, 64:], width[:2, :64])
    heads = jnp.where(at.s == 0, heads[2:4, :32], heads[10:12, :32])
    heads = jnp.where(flip, heads[:, 16:], heads[:, :16])

    return (
        block_out, input_grad, query, key, value, mix_out.T, gate_out, up_out, down_out.T,
        width[0], width[1], heads[0], heads[1],
    )


def solution(mesh):
    fine = Mesh(mesh.devices.reshape(4, 2, 2, 4, 2), ("y", "xh", "core", "z", "xl"))
    dp = ("y", "xh", "core")
    row, col = "z", "xl"
    return jax.shard_map(
        local,
        mesh=fine,
        in_specs=(
            P(dp, col), P(dp), P(col, row), P(col, row), P(col, row), P(row, col),
            P(col, row), P(col, row), P(row, col), P(col), P(col), P((row, col)),
            P((row, col)), P(dp, col),
        ),
        out_specs=(
            P(dp, col), P(dp, col),
            P((col,) + dp, row), P((col,) + dp, row), P((col,) + dp, row), P(row, (col,) + dp),
            P((col,) + dp, row), P((col,) + dp, row), P(row, (col,) + dp),
            P((col,) + dp), P((col,) + dp), P((row, col) + dp), P((row, col) + dp),
        ),
        check_vma=False,
    )
```
